32 devices in a mesh: seq: 8 (over z, x), shard: 4 (over y, core).
Axes of the slice: x: 2, y: 2, z: 4, core: 2. Of those that a mesh axis runs over, the one named last changes fastest.
Arguments:
- tokens: bfloat16 [4, 2048, 2048], P('shard', 'seq'), may hold values from -6 to 6
- in_weight: bfloat16 [2048, 8512], P('shard'), may hold values from -0.125 to 0.125
- out_weight: bfloat16 [2048, 4096], P('shard'), may hold values from -0.09375 to 0.09375
- pre_gain: float32 [2048], replicated, may hold values from 0.1 to 1.9
- conv_kernel: float32 [4, 4352], replicated, may hold values from -3 to 3
- conv_bias: float32 [4352], replicated, may hold values from -3 to 3
- step_bias: float32 [64], replicated, may hold values from -11 to -4
- decay_log: float32 [64], replicated, may hold values from 0 to 2
- skip_gain: float32 [64], replicated, may hold values from 0.5 to 1.5
- gate_gain: float32 [4096], replicated, may hold values from 0.1 to 1.9
- segments: int32 [4, 2048], P('shard'), may hold values from 0 to 3, never falling along the last dimension, each value on 1 to 1024 neighbouring positions
- cotangent: bfloat16 [4, 2048, 2048], P('shard', 'seq'), may hold values from -6 to 6
Outputs:
- block_output: bfloat16 [4, 2048, 2048], P('shard', 'seq')
- token_gradient: float32 [4, 2048, 2048], P('shard', 'seq')
- in_weight_gradient: float32 [2048, 8512], P('shard')
- out_weight_gradient: float32 [2048, 4096], P('shard')
- pre_gain_gradient: float32 [2048], replicated
- conv_kernel_gradient: float32 [4, 4352], replicated
- conv_bias_gradient: float32 [4352], replicated
- step_bias_gradient: float32 [64], replicated
- decay_log_gradient: float32 [64], replicated
- skip_gain_gradient: float32 [64], replicated
- gate_gain_gradient: float32 [4096], replicated
The draws below stay inside these ranges and needn't reach their ends.
Inputs may be any that keep to these rules, and one draw needn't show every extreme that they name: `segments`: along each sequence the numbers never fall; a document is a run of equal numbers, 1 to 1024 tokens long, and one document in each sequence has exactly 1024 tokens.
All inputs are finite; a program needn't handle non-finite values.
Results may differ from the reference program's by a relative error of at most 0.015.
Values may be sent and summed in bfloat16 or wider, within the bound.
No kernel may reach another device: no remote copies, remote signals or barrier semaphores. Data moves between devices by JAX's collectives and lax.ppermute only.
A program may use at most 448 MiB of HBM per device.

```python
import math
from functools import partial
import jax
import jax.numpy as jnp
import numpy as np
from jax import lax

D = 2048
H = 64
P_SIZE = 64
N = 128
CONVK = 4
BLOCK = 256
DI = 4096
CH = 4352
E = 8512
LEN = 2048
SEQS = 4
DOC_MOST = 1024
DOC_COUNT = 4


def with_spikes(array, key, source, target, blocks, factor):
    def block_of(dim):
        return (jnp.arange(array.shape[dim]) // (array.shape[dim] // blocks)).reshape((-1,) + (1,) * (array.ndim - 1 - dim))

    first = jax.random.permutation(key, blocks)[block_of(target)]
    second = (block_of(target) + blocks // 2) % blocks
    return jnp.where((block_of(source) == first) | (block_of(source) == second), factor * array, array)


def levels(key, extent, pieces, smallest, largest):
    def one(dim, shards_of):
        steps = jax.random.uniform(jax.random.fold_in(jax.random.fold_in(key, 6), dim), (shards_of,), jnp.float32, smallest / len(pieces), largest / len(pieces))
        return jnp.repeat(jnp.exp(steps), extent[dim] // shards_of).reshape((-1,) + (1,) * (len(extent) - dim - 1))

    gain = one(*pieces[0])
    for cut in pieces[1:]:
        gain = gain * one(*cut)
    return gain


def length_profile(count, total, reach, lean):
    loads = [(1 << 20) // math.isqrt(grade ** lean) + 1 for grade in range(2, count + 1)]
    rest, counts = total - reach - (count - 1), [1] * (count - 1)
    while rest > 0:
        movable = [i for i in range(count - 1) if counts[i] < reach]
        whole, budget = sum([loads[i] for i in movable]), rest
        for i in movable:
            extra = min(reach - counts[i], max(1, budget * loads[i] // whole), rest)
            counts[i] = counts[i] + extra
            rest = rest - extra
    return np.array([reach] + counts)


def ragged(stream_key, count, total, bound, skew):
    if count == 2:
        one = jax.random.randint(stream_key, (), max(1, total - bound), min(bound, total - 1) + 1)
        return jnp.stack([one, total - one])
    tallies = jnp.asarray(length_profile(count, total, bound, skew), jnp.int32)
    couples = (count - 1) // 2
    donor, receiver = tallies[1:1 + 2 * couples:2], tallies[2:2 + 2 * couples:2]
    margin = jnp.minimum(donor - 1, bound - receiver)
    moved = jax.random.randint(jax.random.fold_in(stream_key, 1), (couples,), 0, 1 << 20) % (margin + 1)
    tallies = tallies.at[1:1 + 2 * couples:2].set(donor - moved).at[2:2 + 2 * couples:2].set(receiver + moved)
    return tallies[jax.random.permutation(jax.random.fold_in(stream_key, 2), count)]


def normal_values(own_key, extent, scale, reach, split=(), kind=jnp.bfloat16):
    entries = jax.random.normal(own_key, extent, jnp.float32) * scale
    if len(split) > 0:
        entries = levels(own_key, extent, split, -0.22, 0.18) * entries
    return jnp.clip(entries, min=-reach, max=reach).astype(kind)


def noise_with(rng, extent, scale, reach, pieces, heavy, kind=jnp.bfloat16):
    entries = scale * jax.random.normal(rng, extent, jnp.float32)
    if pieces:
        entries = entries * levels(rng, extent, pieces, -0.22, 0.18)
    return jnp.clip(with_spikes(entries, jax.random.fold_in(rng, 3), *heavy), -reach, reach).astype(kind)


def setup_inputs(seed: int = 0) -> dict:
    key_list = jax.random.split(jax.random.key(seed), 13)
    return {
        "tokens": normal_values(key_list[0], (SEQS, LEN, D), 1.0, 6.0, ((0, 4), (1, 8))),
        "in_weight": normal_values(key_list[1], (D, E), D ** -0.5, 0.125, ((0, 4),)),
        "out_weight": normal_values(key_list[2], (D, DI), DI ** -0.5, 0.09375, ((0, 4),)),
        "pre_gain": jnp.clip(1.0 + 0.18 * jax.random.normal(key_list[3], (D,), jnp.float32), 0.1, 1.9),
        "conv_kernel": normal_values(key_list[4], (CONVK, CH), CONVK ** -0.5, 3.0, (), jnp.float32),
        "conv_bias": normal_values(key_list[5], (CH,), 0.5, 3.0, (), jnp.float32),
        "step_bias": jnp.clip(jax.random.uniform(key_list[6], (H,), jnp.float32, -11.0, -4.0), -11.0, -4.0),
        "decay_log": jnp.clip(jax.random.uniform(key_list[7], (H,), jnp.float32, 0.0, 2.0), 0.0, 2.0),
        "skip_gain": jnp.clip(jax.random.uniform(key_list[8], (H,), jnp.float32, 0.5, 1.5), 0.5, 1.5),
        "gate_gain": jnp.clip(1.0 + 0.18 * jax.random.normal(key_list[9], (DI,), jnp.float32), 0.1, 1.9),
        "segments": jax.vmap(lambda own: jnp.searchsorted(jnp.cumsum(ragged(own, DOC_COUNT, LEN, DOC_MOST, 3)), jnp.arange(LEN), side="right"))(jax.random.split(key_list[10], SEQS)).reshape((SEQS, LEN)).astype(jnp.int32),
        "cotangent": noise_with(key_list[11], (SEQS, LEN, D), 1.0, 6.0, ((0, 4), (1, 8)), (1, 2, 8, 2.0)),
    }


epsilon = 1e-05
highest = lax.Precision.HIGHEST

@jax.custom_vjp
def low(v):
    return lax.optimization_barrier(v.astype(jnp.bfloat16)).astype(jnp.float32)

@jax.custom_vjp
def low_back(v):
    return v

def low_keep(v):
    return (low(v), None)

def low_pass(kept, grad):
    return (grad,)

def back_keep(v):
    return (v, None)

def back_low(kept, grad):
    return (low(grad),)
low.defvjp(low_keep, low_pass)
low_back.defvjp(back_keep, back_low)

def rms_scale(values):
    return lax.rsqrt(lax.optimization_barrier(jnp.mean(values * values, axis=-1, keepdims=True)) + epsilon)

def causal_conv(inputs, kernel, offset, segment):
    length = inputs.shape[0]
    result = offset[None, :] + kernel[0][None, :] * inputs
    for delay_steps in range(1, kernel.shape[0]):
        shifted = jnp.concatenate([jnp.zeros((delay_steps, inputs.shape[1]), inputs.dtype), inputs[:length - delay_steps]], axis=0)
        earlier = jnp.concatenate([jnp.full((delay_steps,), -1, jnp.int32), segment[:length - delay_steps]], axis=0)
        same_doc = (earlier == segment).astype(inputs.dtype)
        result = result + kernel[delay_steps][None, :] * shifted * same_doc[:, None]
    return result

def block_terms(block, decay_rates):
    inputs_x, step_sizes, keys_b, queries_c, segment = block
    block_rows = inputs_x.shape[0]
    cumulative = jnp.cumsum(step_sizes * decay_rates[None, :], axis=0)
    position = lax.iota(jnp.int32, block_rows)
    allowed = ((position[:, None] >= position[None, :]) & (segment[:, None] == segment[None, :]))[:, :, None]
    log_gaps = jnp.where(allowed, cumulative[:, None, :] - cumulative[None, :, :], 0.0)
    affinity = jnp.einsum('tn,sn->ts', queries_c, keys_b, precision=highest)
    weights = jnp.where(allowed, jnp.exp(log_gaps), 0.0) * affinity[:, :, None]
    scaled = inputs_x * step_sizes[:, :, None]
    local_out = jnp.einsum('tsk,skp->tkp', weights, scaled, precision=highest)
    tail_weight = jnp.where((segment == segment[block_rows - 1])[:, None], jnp.exp(cumulative[block_rows - 1][None, :] - cumulative), 0.0)
    state_add = jnp.einsum('sn,skp->knp', keys_b, scaled * tail_weight[:, :, None], precision=highest)
    return (local_out, state_add, cumulative)

def mix_sequence(inputs_x, step_sizes, keys_b, queries_c, decay_rates, segment, mapper):
    length, head_count, head_dim = inputs_x.shape
    block_count = length // BLOCK
    blocks = (inputs_x.reshape(block_count, BLOCK, head_count, head_dim), step_sizes.reshape(block_count, BLOCK, head_count), keys_b.reshape(block_count, BLOCK, -1), queries_c.reshape(block_count, BLOCK, -1), segment.reshape(block_count, BLOCK))
    local_out, state_add, cumulative = mapper(partial(block_terms, decay_rates=decay_rates), blocks)
    running = jnp.cumsum(cumulative[:, BLOCK - 1, :], axis=0)
    before = jnp.concatenate([jnp.zeros((1, head_count), running.dtype), running[:-1]], axis=0)
    block_ends = blocks[4][:, BLOCK - 1]
    prior_end = jnp.concatenate([jnp.full((1,), -1, jnp.int32), block_ends[:-1]], axis=0)
    block_index = lax.iota(jnp.int32, block_count)
    linked = ((block_index[:, None] > block_index[None, :]) & (prior_end[:, None] == block_ends[None, :]))[:, :, None]
    carried = jnp.where(linked, jnp.exp(jnp.where(linked, before[:, None, :] - running[None, :, :], 0.0)), 0.0)
    entering = jnp.einsum('cdk,dknp->cknp', carried, state_add, precision=highest)
    reach_weight = jnp.where((blocks[4] == prior_end[:, None])[:, :, None], jnp.exp(cumulative), 0.0)
    state_out = jnp.einsum('ctn,cknp->ctkp', blocks[3], entering, precision=highest) * reach_weight[:, :, :, None]
    return (local_out + state_out).reshape(length, head_count, head_dim)

def sequence_map(function, blocks):
    return lax.map(jax.checkpoint(function), blocks)

def layer_one(series, segment, params):
    in_weight, out_weight, pre_gain, conv_kernel, conv_bias, step_bias, decay_log, skip_gain, gate_gain = params
    normed = low(series * rms_scale(series) * pre_gain[None, :])
    projected = jnp.dot(normed, in_weight, precision=highest)
    gate_values = low_back(projected[:, :DI])
    packed = low(low_back(projected[:, DI:]))
    conv_out = jax.nn.silu(causal_conv(packed[:, :CH], conv_kernel, conv_bias, segment))
    inputs_x = conv_out[:, :DI].reshape(-1, H, P_SIZE)
    step_sizes = jax.nn.softplus(packed[:, CH:] + step_bias[None, :])
    mixed = mix_sequence(inputs_x, step_sizes, conv_out[:, DI:DI + N], conv_out[:, DI + N:], -jnp.exp(decay_log), segment, sequence_map)
    mixed = mixed + skip_gain[None, :, None] * inputs_x
    mixed = low(low_back(mixed.reshape(-1, DI)))
    gated = mixed * jax.nn.silu(gate_values)
    normed_out = low(gated * rms_scale(gated) * gate_gain[None, :])
    return series + jnp.dot(normed_out, out_weight.T, precision=highest)

def reference(tokens, in_weight, out_weight, pre_gain, conv_kernel, conv_bias, step_bias, decay_log, skip_gain, gate_gain, segments, cotangent):
    params = (in_weight.astype(jnp.float32), out_weight.astype(jnp.float32), pre_gain.astype(jnp.float32), conv_kernel.astype(jnp.float32), conv_bias.astype(jnp.float32), step_bias.astype(jnp.float32), decay_log.astype(jnp.float32), skip_gain.astype(jnp.float32), gate_gain.astype(jnp.float32))

    def forward(series_all, weights_all):

        def one_sequence(seq_pair):
            return layer_one(seq_pair[0], seq_pair[1], weights_all)
        return lax.map(jax.checkpoint(one_sequence), (series_all, segments))
    output, pullback = jax.vjp(forward, tokens.astype(jnp.float32), params)
    token_gradient, grads_all = pullback(cotangent.astype(jnp.float32))
    return (output.astype(jnp.bfloat16), token_gradient, grads_all[0], grads_all[1], grads_all[2], grads_all[3], grads_all[4], grads_all[5], grads_all[6], grads_all[7], grads_all[8])
```

```python
from functools import partial

import jax
import jax.numpy as jnp
from jax import lax
from jax.sharding import PartitionSpec as P

BLOCK = 256
HALO = 16
epsilon = 1e-05
highest = lax.Precision.HIGHEST
f32 = jnp.float32
bf16 = jnp.bfloat16
AXES = ("seq", "shard")


class Slice:
    def __init__(self, mesh):
        self.seq = mesh.shape["seq"]
        self.shard = mesh.shape["shard"]
        self.Y = self.shard // 2
        self.X = self.Y
        self.Z = self.seq // self.X
        self.TP = 2 * self.X

    def place(self):
        s, k = lax.axis_index("seq"), lax.axis_index("shard")
        self.z, self.x = s // self.X, s % self.X
        self.y, self.c = k // 2, k % 2
        self.j = self.x * 2 + self.c

    def move(self, a, target):
        pairs = []
        for z in range(self.Z):
            for x in range(self.X):
                for y in range(self.Y):
                    for c in range(2):
                        to = target(z, x, y, c)
                        if to is None:
                            continue
                        tz, tx, ty, tc = to
                        if not 0 <= tz < self.Z:
                            continue
                        src = (z * self.X + x) * self.shard + y * 2 + c
                        dst = (tz * self.X + tx % self.X) * self.shard + (ty % self.Y) * 2 + tc
                        pairs.append((src, dst))
        return lax.ppermute(a, AXES, pairs)

    def swap_core(self, a):
        return self.move(a, lambda z, x, y, c: (z, x, y, 1 - c))

    def shift_x(self, a, d):
        return self.move(a, lambda z, x, y, c: (z, x + d, y, c))

    def shift_y(self, a, d):
        return self.move(a, lambda z, x, y, c: (z, x, y + d, c))

    def shift_z(self, a, d):
        return self.move(a, lambda z, x, y, c: (z + d, x, y, c))

    def swap_z(self, a):
        return self.move(a, lambda z, x, y, c: (z ^ 1, x, y, c))

    def by_core(self, own, other):
        first = self.c == 0
        return jnp.where(first, own, other), jnp.where(first, other, own)

    def gather_tp(self, a):
        parts = [a] + [self.shift_x(a, d) for d in range(1, self.X)]
        buf = jnp.stack(parts)
        buf = self.true_x(parts)
        lo, hi = self.by_core(buf, self.swap_core(buf))
        return jnp.stack([lo, hi])

    def true_x(self, parts):
        rows = []
        for tx in range(self.X):
            pick = parts[0]
            for d in range(1, self.X):
                pick = jnp.where((self.x - d) % self.X == tx, parts[d], pick)
            rows.append(pick)
        return jnp.stack(rows)

    def scatter_tp(self, a):
        keep, send = self.by_core(a[0], a[1])
        total = (keep.astype(f32) + self.swap_core(send).astype(f32)).astype(bf16)
        acc = lax.dynamic_index_in_dim(total, self.x, 0, False).astype(f32)
        for d in range(1, self.X):
            part = lax.dynamic_index_in_dim(total, (self.x + d) % self.X, 0, False)
            acc = acc + self.shift_x(part, d).astype(f32)
        return acc

    def sum_tp(self, a):
        total = a
        for dx in range(self.X):
            for dc in range(2):
                if dx or dc:
                    total = total + self.move(a, lambda z, x, y, c: (z, x + dx, y, c ^ dc))
        return total

    def own_first(self, a):
        width = a.shape[-1] // self.Y
        parts = [
            lax.dynamic_slice_in_dim(a, ((self.y - i) % self.Y) * width, width, a.ndim - 1)
            for i in range(self.Y)
        ]
        return jnp.concatenate(parts, axis=-1)

    def fetch_rows(self, half):
        n = half.shape[0]
        shared = (n // 3 + 15) // 16 * 16
        direct = n - 2 * shared
        even = self.z % 2 == 0
        full = [half]
        for d in range(1, self.Y):
            b0, b1 = half[direct : direct + shared], half[direct + shared :]
            r = self.shift_y(jnp.where(even, b0, b1), d)
            straight = self.shift_y(half[:direct], d)
            o = self.swap_z(r)
            full += [straight, jnp.where(even, r, o), jnp.where(even, o, r)]
        return jnp.concatenate(full, axis=0)

    def columns(self, local, pick):
        own = pick(local, self.j)
        other = self.swap_core(pick(local, self.x * 2 + 1 - self.c))
        lo, hi = self.by_core(own, other)
        return self.fetch_rows(jnp.concatenate([lo, hi], axis=0))

    def reduce_gradient(self, part):
        rows = part.shape[0] // self.shard
        p = part.reshape(self.Y, 2, rows, part.shape[1])
        acc = p[0].astype(f32)
        for i in range(1, self.Y):
            acc = acc + self.shift_y(p[i], -i).astype(f32)
        acc = acc.astype(bf16)
        keep, send = self.by_core(acc[0], acc[1])
        lo, hi = self.by_core(keep, self.swap_core(send))
        q = jnp.stack([lo, hi])
        half = self.Z // 2
        for step in range(half - 1):
            r = self.move(
                q,
                lambda z, x, y, c: (z + 1, x, y, c)
                if z == step
                else ((z - 1, x, y, c) if z == self.Z - 1 - step else None),
            )
            q = (q.astype(f32) + r.astype(f32)).astype(bf16)
        r = self.move(
            q,
            lambda z, x, y, c: (z + 1, x, y, c)
            if z == half - 1
            else ((z - 1, x, y, c) if z == half else None),
        )
        q = (q.astype(f32) + r.astype(f32)).astype(bf16)
        for step in range(half - 1):
            a, b = half - 1 - step, half + step
            r = self.move(
                q,
                lambda z, x, y, c: (z - 1, x, y, c)
                if z == a
                else ((z + 1, x, y, c) if z == b else None),
            )
            q = jnp.where((self.z == a - 1) | (self.z == b + 1), r, q)
        return [q] + [self.shift_x(q, d) for d in range(1, self.X)]

    def sum_small(self, v, over_tp):
        def ordered(a, n, own, shift):
            buf = jnp.zeros((n,) + a.shape, a.dtype)
            buf = lax.dynamic_update_index_in_dim(buf, a, own, 0)
            for d in range(1, n):
                buf = lax.dynamic_update_index_in_dim(buf, shift(a, d), (own - d) % n, 0)
            return buf

        def turn_z(a, d):
            return self.move(a, lambda z, x, y, c: ((z + d) % self.Z, x, y, c))

        v = jnp.sum(ordered(v, self.Z, self.z, turn_z), axis=0)
        v = jnp.sum(ordered(v, self.Y, self.y, self.shift_y), axis=0)
        v = ordered(v, self.X, self.x, self.shift_x)
        v = ordered(v, 2, self.c, lambda a, d: self.swap_core(a))
        return jnp.sum(v, axis=(0, 1)) if over_tp else v


def silu_slope(v):
    g = jax.nn.sigmoid(v)
    return g * (1.0 + v * (1.0 - g))


def low_dot(a, b, dims):
    return lax.dot_general(a.astype(bf16), b.astype(bf16), dims, preferred_element_type=f32)


def mm(a, b):
    return low_dot(a, b, (((a.ndim - 1,), (0,)), ((), ())))


def intra_forward(keys, queries, cum, seg, xs):
    pos = lax.iota(jnp.int32, BLOCK)
    allowed = (pos[:, None] >= pos[None, :])[None] & (seg[:, :, None] == seg[:, None, :])
    gram = jnp.einsum("btn,bsn->bts", queries.astype(bf16), keys.astype(bf16), preferred_element_type=f32)
    ct = cum.transpose(0, 2, 1)
    gaps = jnp.where(allowed[:, None], ct[:, :, :, None] - ct[:, :, None, :], -1e30)
    weights = (jnp.exp(gaps) * gram[:, None]).astype(bf16)
    return jnp.einsum("bhts,bshp->bthp", weights, xs.astype(bf16), preferred_element_type=f32)


def intra_backward(keys, queries, cum, step, seg, x, d_out):
    pos = lax.iota(jnp.int32, BLOCK)
    allowed = (pos[:, None] >= pos[None, :])[None] & (seg[:, :, None] == seg[:, None, :])
    gram = jnp.einsum("btn,bsn->bts", queries.astype(bf16), keys.astype(bf16), preferred_element_type=f32)
    ct = cum.transpose(0, 2, 1)
    gaps = jnp.where(allowed[:, None], ct[:, :, :, None] - ct[:, :, None, :], -1e30)
    decay = jnp.exp(gaps)
    e = jnp.einsum("bthp,bshp->bhts", d_out.astype(bf16), x.astype(bf16), preferred_element_type=f32)
    st = step.transpose(0, 2, 1)
    le = decay * e * st[:, :, None, :]
    zsum = jnp.sum(le, axis=1)
    m = le * gram[:, None]
    across = (jnp.sum(m, axis=3) - jnp.sum(m, axis=2)).transpose(0, 2, 1)
    dxs = jnp.einsum(
        "bhts,bthp->bshp", (decay * gram[:, None]).astype(bf16), d_out.astype(bf16), preferred_element_type=f32
    )
    zl = zsum.astype(bf16)
    d_queries = jnp.einsum("bts,bsn->btn", zl, keys.astype(bf16), preferred_element_type=f32)
    d_keys = jnp.einsum("bts,btn->bsn", zl, queries.astype(bf16), preferred_element_type=f32)
    return dxs, across, d_keys, d_queries


def body(
    g,
    tokens,
    in_weight,
    out_weight,
    pre_gain,
    conv_kernel,
    conv_bias,
    step_bias,
    decay_log,
    skip_gain,
    gate_gain,
    segments,
    cotangent,
):
    g.place()
    heads = step_bias.shape[0]
    inner = gate_gain.shape[0]
    channels = conv_bias.shape[0]
    shared = channels - inner
    state = shared // 2
    taps = conv_kernel.shape[0]
    hd = inner // heads
    HL = heads // g.TP
    HW = HL * hd
    SW = shared // g.TP
    own_len = tokens.shape[1]
    width = tokens.shape[2]
    T = own_len * g.X
    nb = T // BLOCK
    NB = 2 * nb
    j = g.j

    series = tokens[0].astype(f32)
    scale = lax.rsqrt(jnp.mean(series * series, axis=-1, keepdims=True) + epsilon)
    normed = g.own_first((series * scale * pre_gain[None, :]).astype(bf16))
    n_all = g.gather_tp(normed).reshape(2, T, width)
    halo = g.shift_z(n_all[:, T - HALO :], 1)
    n_ext = jnp.concatenate([halo, n_all], axis=1).reshape(2 * (HALO + T), width)
    n_all = n_all.reshape(2 * T, width)
    cot_all = g.gather_tp(g.own_first(cotangent[0])).reshape(2 * T, width)

    def pick_packed(w, jj):
        a = lax.dynamic_slice_in_dim(w, inner + HW * jj, HW, 1)
        return jnp.concatenate([a, w[:, inner * 2 :]], axis=1)

    def pick_gate(w, jj):
        return lax.dynamic_slice_in_dim(w, HW * jj, HW, 1)

    w_packed = g.columns(in_weight, pick_packed)
    w_gate = g.columns(in_weight, pick_gate)
    w_out = g.columns(out_weight, pick_gate)

    s_lo, s_hi = g.by_core(segments, g.swap_core(segments))
    seg_all = jnp.concatenate([s_lo, s_hi], axis=0)
    start = g.z * T
    seg_pad = jnp.concatenate([jnp.full((2, HALO), -1, jnp.int32), seg_all], axis=1)
    seg_ext = lax.dynamic_slice_in_dim(seg_pad, start, T + HALO, 1)
    seg = seg_ext[:, HALO:]
    same = [
        (seg_ext[:, HALO - k : HALO - k + T] == seg).astype(f32)[:, :, None] for k in range(taps)
    ]
    seg_b = seg.reshape(NB, BLOCK)
    block_end = seg_b[:, BLOCK - 1]
    prior_end = seg_ext.reshape(2, T + HALO)[:, HALO - 1 :][:, : T : BLOCK].reshape(NB)

    packed = mm(n_ext, w_packed).astype(bf16).reshape(2, HALO + T, HW + shared + heads)

    def own_channels(a):
        x_part = lax.dynamic_slice_in_dim(a, HW * j, HW, a.ndim - 1)
        return jnp.concatenate([x_part, a[..., inner:]], axis=-1)

    kernel_own = own_channels(conv_kernel)
    bias_own = own_channels(conv_bias)
    CW = HW + shared
    conv_in = packed[:, :, :CW].astype(f32)
    pre = bias_own[None, None, :]
    for k in range(taps):
        pre = pre + kernel_own[k] * conv_in[:, HALO - k : HALO - k + T] * same[k]
    act = jax.nn.silu(pre)
    x = act[:, :, :HW].astype(bf16).reshape(NB, BLOCK, HW)
    keys = act[:, :, HW : HW + state].astype(bf16).reshape(NB, BLOCK, state)
    queries = act[:, :, HW + state :].astype(bf16).reshape(NB, BLOCK, state)

    def own_heads(a):
        return lax.dynamic_slice_in_dim(a, HL * j, HL, a.ndim - 1)

    raw = own_heads(packed[:, HALO:, CW:]).astype(f32) + own_heads(step_bias)
    step = jax.nn.softplus(raw).reshape(NB, BLOCK, HL)
    rate = jnp.exp(own_heads(decay_log))
    skip = own_heads(skip_gain)
    log_decay = -rate * step
    pos = lax.iota(jnp.int32, BLOCK)
    lower = (pos[:, None] >= pos[None, :]).astype(f32)
    cum = jnp.einsum("ts,bsh->bth", lower, log_decay, precision=highest)
    cum_end = cum[:, BLOCK - 1, :]
    reach = jnp.where((seg_b == prior_end[:, None])[:, :, None], jnp.exp(cum), 0.0)
    tail = jnp.where(
        (seg_b == block_end[:, None])[:, :, None], jnp.exp(cum_end[:, None, :] - cum), 0.0
    )
    carry = jnp.where((prior_end == block_end)[:, None], jnp.exp(cum_end), 0.0)

    def spread(a):
        return jnp.repeat(a, hd, axis=-1)

    def per_head(a):
        return a.reshape(a.shape[:-1] + (HL, hd)).sum(axis=-1)

    xf = x.astype(f32)
    step_wide = spread(step)
    xs = xf * step_wide
    tail_wide = spread(tail)
    reach_wide = spread(reach)
    xst = (xs * tail_wide).astype(bf16)
    s_block = jnp.einsum("bsn,bsi->bni", keys, xst, preferred_element_type=f32).reshape(
        2, nb, state, HW
    )
    carry_b = carry.reshape(2, nb, HL)
    carry_wide = spread(carry_b)[:, :, None, :]

    def exchange(cur, direction):
        cc = jnp.prod(carry_b, axis=1)
        d = 1
        while d < g.Z // 2:
            r = g.shift_z(cur.astype(bf16), direction * d).astype(f32)
            cur = cur + spread(cc)[:, None, :] * r
            if 2 * d < g.Z // 2:
                cc = cc * g.shift_z(cc, direction * d)
            d *= 2
        return g.shift_z(cur.astype(bf16), direction).astype(f32)

    s_range = s_block[:, 0]
    for b in range(1, nb):
        s_range = s_block[:, b] + carry_wide[:, b] * s_range
    enter = [exchange(s_range, 1)]
    for b in range(nb - 1):
        enter.append(s_block[:, b] + carry_wide[:, b] * enter[b])
    enter = jnp.stack(enter, axis=1).astype(bf16).reshape(NB, state, HW)

    y_local = intra_forward(keys, queries, cum, seg_b, xs.reshape(NB, BLOCK, HL, hd)).reshape(
        NB, BLOCK, HW
    )
    from_state = (
        jnp.einsum("btn,bni->bti", queries, enter, preferred_element_type=f32) * reach_wide
    )
    skip_wide = spread(skip)
    mixed = (y_local + from_state + skip_wide * xf).astype(bf16).astype(f32)

    gate = mm(n_all, w_gate).reshape(NB, BLOCK, HW)
    out_grad = mm(cot_all, w_out).reshape(NB, BLOCK, HW)
    gain_own = lax.dynamic_slice_in_dim(gate_gain, HW * j, HW, 0)
    gate_act = jax.nn.silu(gate)
    gated = mixed * gate_act
    lifted = out_grad * gain_own
    sums = jnp.stack([jnp.sum(gated * gated, axis=-1), jnp.sum(gated * lifted, axis=-1)])
    sums = g.sum_tp(sums) / inner
    r = lax.rsqrt(sums[0] + epsilon)[:, :, None]
    normed_out = (gated * r * gain_own).astype(bf16).reshape(2 * T, HW)
    gated_grad = r * lifted - gated * (r * r * r) * sums[1][:, :, None]
    gain_grad = jnp.sum(out_grad * gated * r, axis=(0, 1))
    d_out = (gated_grad * gate_act).astype(bf16)
    gate_grad = (gated_grad * mixed * silu_slope(gate)).astype(bf16).reshape(2 * T, HW)

    rows_first = (((0,), (0,)), ((), ()))
    rows_last = (((1,), (1,)), ((), ()))
    out_part = low_dot(cot_all, normed_out, rows_first).astype(bf16)
    gate_part = low_dot(n_all, gate_grad, rows_first).astype(bf16)
    out_sum = g.reduce_gradient(out_part)
    gate_sum = g.reduce_gradient(gate_part)
    branch = low_dot(normed_out, w_out, rows_last).astype(bf16)
    branch = g.own_first_back(g.scatter_tp(branch.reshape(2, g.X, own_len, width)))
    block_output = (series + branch).astype(bf16)[None]

    d_f = d_out.astype(f32)
    d_reach = (d_f * reach_wide).astype(bf16)
    de_block = jnp.einsum("btn,bti->bni", queries, d_reach, preferred_element_type=f32).reshape(
        2, nb, state, HW
    )
    d_range = de_block[:, nb - 1]
    for b in range(nb - 2, -1, -1):
        d_range = de_block[:, b] + carry_wide[:, b] * d_range
    leave = [exchange(d_range, -1)]
    for b in range(nb - 1, 0, -1):
        leave.insert(0, de_block[:, b] + carry_wide[:, b] * leave[0])
    leave = jnp.stack(leave, axis=1).astype(bf16).reshape(NB, state, HW)
    dxs, across, d_keys, d_queries = intra_backward(
        keys,
        queries,
        cum,
        step,
        seg_b,
        x.reshape(NB, BLOCK, HL, hd),
        d_out.reshape(NB, BLOCK, HL, hd),
    )
    key_leave = (
        jnp.einsum("bsn,bni->bsi", keys, leave, preferred_element_type=f32) * tail_wide
    )
    dxs = dxs.reshape(NB, BLOCK, HW) + key_leave
    d_keys = d_keys + jnp.einsum("bsi,bni->bsn", xst, leave, preferred_element_type=f32)
    d_queries = d_queries + jnp.einsum("bti,bni->btn", d_reach, enter, preferred_element_type=f32)
    x_grad = skip_wide * d_f + step_wide * dxs
    came_in = per_head(d_f * from_state)
    goes_out = per_head(xs * key_leave)
    through = carry * per_head(jnp.sum(enter.astype(f32) * leave.astype(f32), axis=1))
    decay_grad = (
        jnp.einsum("ts,bth->bsh", lower, across + came_in, precision=highest)
        + jnp.einsum("ts,bsh->bth", lower - jnp.eye(BLOCK, dtype=f32), goes_out, precision=highest)
        + through[:, None, :]
    )
    step_grad = per_head(xf * dxs) - rate * decay_grad
    decay_log_grad = -rate * jnp.sum(step * decay_grad, axis=(0, 1))
    skip_grad = jnp.sum(per_head(d_f * xf), axis=(0, 1))
    raw_grad = step_grad.reshape(2, T, HL) * jax.nn.sigmoid(raw)
    step_bias_grad = jnp.sum(raw_grad, axis=(0, 1))

    both = jnp.concatenate([d_keys, d_queries], axis=-1).astype(bf16).reshape(2, T, shared)
    both_sum = lax.dynamic_slice_in_dim(both, SW * j, SW, 2).astype(f32)
    for dx in range(g.X):
        for dc in range(2):
            if dx or dc:
                jj = (g.x + dx) % g.X * 2 + (g.c ^ dc)
                part = lax.dynamic_slice_in_dim(both, SW * jj, SW, 2)
                part = g.move(part, lambda z, x, y, c: (z, x + dx, y, c ^ dc))
                both_sum = both_sum + part.astype(f32)

    def own_shared(a):
        return lax.dynamic_slice_in_dim(a, HW + SW * j, SW, a.ndim - 1)

    def conv_back(grad, pre_own, kernel, values):
        cg = grad * silu_slope(pre_own)
        back = 0.0
        kg = []
        for k in range(taps):
            m = cg * same[k]
            kg.append(jnp.sum(m * values[:, HALO - k : HALO - k + T], axis=(0, 1)))
            back = back + jnp.pad(kernel[k] * m, ((0, 0), (HALO - k, k), (0, 0)))
        return back.astype(bf16), jnp.stack(kg), jnp.sum(cg, axis=(0, 1))

    x_back, x_kg, x_bg = conv_back(
        x_grad.reshape(2, T, HW), pre[:, :, :HW], kernel_own[:, :HW], conv_in[:, :, :HW]
    )
    s_back, s_kg, s_bg = conv_back(
        both_sum, own_shared(pre), own_shared(kernel_own), own_shared(conv_in)
    )
    raw_low = jnp.pad(raw_grad, ((0, 0), (HALO, 0), (0, 0))).astype(bf16)
    tail_back = jnp.concatenate([s_back, raw_low], axis=-1)
    x_back = x_back.reshape(2 * (HALO + T), HW)
    tail_back = tail_back.reshape(2 * (HALO + T), SW + HL)
    x_part = low_dot(n_ext, x_back, rows_first).astype(bf16)
    tail_part = low_dot(n_ext, tail_back, rows_first).astype(bf16)
    x_sum = g.reduce_gradient(x_part)
    tail_sum = g.reduce_gradient(tail_part)

    w_tail = jnp.concatenate(
        [
            lax.dynamic_slice_in_dim(w_packed, HW + SW * j, SW, 1),
            lax.dynamic_slice_in_dim(w_packed, CW + HL * j, HL, 1),
        ],
        axis=1,
    )
    packed_back = jnp.concatenate([x_back, tail_back], axis=1)
    w_back = jnp.concatenate([w_packed[:, :HW], w_tail], axis=1)
    n_grad_ext = low_dot(packed_back, w_back, rows_last).reshape(2, HALO + T, width)
    n_grad = n_grad_ext[:, HALO:] + low_dot(gate_grad, w_gate, rows_last).reshape(2, T, width)
    spill = g.shift_z(n_grad_ext[:, :HALO].astype(bf16), -1).astype(f32)
    n_grad = n_grad + jnp.pad(spill, ((0, 0), (T - HALO, 0), (0, 0)))
    n_grad = g.own_first_back(
        g.scatter_tp(n_grad.astype(bf16).reshape(2, g.X, own_len, width))
    )
    pre_grad = jnp.sum(n_grad * series * scale, axis=0)
    lifted_n = n_grad * pre_gain[None, :]
    token_gradient = (
        cotangent[0].astype(f32)
        + scale * lifted_n
        - series * scale**3 * jnp.mean(series * lifted_n, axis=-1, keepdims=True)
    )[None]

    k_all = jnp.concatenate([x_kg, s_kg], axis=1)
    b_all = jnp.concatenate([x_bg, s_bg])
    small = jnp.concatenate(
        [gain_grad, k_all.reshape(-1), b_all, step_bias_grad, decay_log_grad, skip_grad]
    )
    n_small = small.shape[0]
    small = jnp.pad(small, (0, -n_small % 1024)).reshape(-1, 128)
    small = g.sum_small(small, False)
    small = small.transpose(1, 0, 2, 3).reshape(g.TP, -1)[:, :n_small]
    pre_total = g.sum_small(pre_grad.reshape(-1, 128), True).reshape(-1)
    at = 0
    gain_total = small[:, :HW].reshape(-1)
    at = HW
    kt = small[:, at : at + taps * (HW + SW)].reshape(g.TP, taps, HW + SW).transpose(1, 0, 2)
    at += taps * (HW + SW)
    kernel_total = jnp.concatenate(
        [kt[:, :, :HW].reshape(taps, -1), kt[:, :, HW:].reshape(taps, -1)], axis=1
    )
    bt = small[:, at : at + HW + SW]
    at += HW + SW
    bias_total = jnp.concatenate([bt[:, :HW].reshape(-1), bt[:, HW:].reshape(-1)])
    step_total = small[:, at : at + HL].reshape(-1)
    decay_total = small[:, at + HL : at + 2 * HL].reshape(-1)
    skip_total = small[:, at + 2 * HL : at + 3 * HL].reshape(-1)

    def place(sums, first, size):
        parts = g.true_x([q[:, :, first : first + size] for q in sums])
        return [parts[tx, tc] for tx in range(g.X) for tc in range(2)]

    columns = (
        place(gate_sum, 0, HW)
        + place(x_sum, 0, HW)
        + place(tail_sum, 0, SW)
        + place(tail_sum, SW, HL)
    )
    in_weight_gradient = jnp.concatenate(columns, axis=1).astype(f32)
    out_weight_gradient = jnp.concatenate(place(out_sum, 0, HW), axis=1).astype(f32)
    return (
        block_output,
        token_gradient,
        in_weight_gradient,
        out_weight_gradient,
        pre_total,
        kernel_total,
        bias_total,
        step_total,
        decay_total,
        skip_total,
        gain_total,
    )


def own_first_back(self, a):
    width = a.shape[-1] // self.Y
    parts = []
    for t in range(self.Y):
        parts.append(
            lax.dynamic_slice_in_dim(a, ((self.y - t) % self.Y) * width, width, a.ndim - 1)
        )
    return jnp.concatenate(parts, axis=-1)


Slice.own_first_back = own_first_back


def solution(mesh):
    placed = (
        P("shard", "seq", None),
        P("shard", None),
        P("shard", None),
        P(),
        P(),
        P(),
        P(),
        P(),
        P(),
        P(),
        P("shard", None),
        P("shard", "seq", None),
    )
    return jax.shard_map(
        partial(body, Slice(mesh)),
        mesh=mesh,
        in_specs=placed,
        out_specs=(
            P("shard", "seq", None),
            P("shard", "seq", None),
            P("shard", None),
            P("shard", None),
            P(),
            P(),
            P(),
            P(),
            P(),
            P(),
            P(),
        ),
        check_vma=False,
    )
```

```python
from functools import partial

import jax
import jax.numpy as jnp
import numpy as np
from jax import lax
from jax.experimental import pallas as pl
from jax.experimental.pallas import tpu as pltpu
from jax.sharding import PartitionSpec as P

BLOCK = 256
HALO = 16
epsilon = 1e-05
highest = lax.Precision.HIGHEST
f32 = jnp.float32
bf16 = jnp.bfloat16
AXES = ("seq", "shard")


class Slice:
    def __init__(self, mesh):
        self.seq = mesh.shape["seq"]
        self.shard = mesh.shape["shard"]
        self.Y = self.shard // 2
        self.X = self.Y
        self.Z = self.seq // self.X
        self.TP = 2 * self.X

    def place(self):
        s, k = lax.axis_index("seq"), lax.axis_index("shard")
        self.z, self.x = s // self.X, s % self.X
        self.y, self.c = k // 2, k % 2
        self.j = self.x * 2 + self.c

    def move(self, a, target):
        pairs = []
        for z in range(self.Z):
            for x in range(self.X):
                for y in range(self.Y):
                    for c in range(2):
                        to = target(z, x, y, c)
                        if to is None:
                            continue
                        tz, tx, ty, tc = to
                        if not 0 <= tz < self.Z:
                            continue
                        src = (z * self.X + x) * self.shard + y * 2 + c
                        dst = (tz * self.X + tx % self.X) * self.shard + (ty % self.Y) * 2 + tc
                        pairs.append((src, dst))
        return lax.ppermute(a, AXES, pairs)

    def swap_core(self, a):
        return self.move(a, lambda z, x, y, c: (z, x, y, 1 - c))

    def shift_x(self, a, d):
        return self.move(a, lambda z, x, y, c: (z, x + d, y, c))

    def shift_y(self, a, d):
        return self.move(a, lambda z, x, y, c: (z, x, y + d, c))

    def shift_z(self, a, d):
        return self.move(a, lambda z, x, y, c: (z + d, x, y, c))

    def swap_z(self, a):
        return self.move(a, lambda z, x, y, c: (z ^ 1, x, y, c))

    def by_core(self, own, other):
        first = self.c == 0
        return jnp.where(first, own, other), jnp.where(first, other, own)

    def own_first(self, a):
        width = a.shape[-1] // self.Y
        parts = [
            lax.dynamic_slice_in_dim(a, ((self.y - i) % self.Y) * width, width, a.ndim - 1)
            for i in range(self.Y)
        ]
        return jnp.concatenate(parts, axis=-1)

    def own_first_back(self, a):
        width = a.shape[-1] // self.Y
        parts = [
            lax.dynamic_slice_in_dim(a, ((self.y - t) % self.Y) * width, width, a.ndim - 1)
            for t in range(self.Y)
        ]
        return jnp.concatenate(parts, axis=-1)

    def cut(self, a, axis, i, n):
        size = a.shape[axis] // n
        return lax.slice_in_dim(a, i * size, (i + 1) * size, axis=axis)


    def fetch_task(self, half, axis, out):
        n, m = half.shape
        shared = (n // 3 + 15) // 16 * 16
        direct = n - 2 * shared
        odd = self.z % 2
        sent = yield [lax.dynamic_slice_in_dim(half, direct + odd * shared, shared, 0)]
        got = yield [self.shift_y(sent[0], d) for d in range(1, self.Y)]
        sent = yield [half[:direct]] + got
        done = yield [self.shift_y(sent[0], d) for d in range(1, self.Y)] + [
            self.swap_z(r) for r in sent[1:]
        ]
        pieces = [(half, None, (n, m), (0, 0))]
        for d in range(1, self.Y):
            at = (lambda r: (r, d * m)) if axis else (lambda r: (d * n + r, 0))
            r, o = got[d - 1], done[self.Y - 2 + d]
            pieces += [
                (done[d - 1], None, (direct, m), at(0)),
                (r, None, (shared, m), at(direct + odd * shared)),
                (o, None, (shared, m), at(direct + (1 - odd) * shared)),
            ]
        shape = (n, m * self.Y) if axis else (n * self.Y, m)
        out["w"] = assemble(pieces, shape)

    def direct_task(self, half, shares, out):
        n, m = half.shape
        edges = [n * sum(shares[:i]) // sum(shares) // 16 * 16 for i in range(len(shares) + 1)]
        pieces = [(half, None, (n, m), (0, 0))]
        for a, b in zip(edges[:-1], edges[1:]):
            sent = yield [half[a:b]]
            got = yield [self.shift_y(sent[0], d) for d in range(1, self.Y)]
            for d, r in enumerate(got):
                pieces.append((r, None, (b - a, m), ((d + 1) * n + a, 0)))
        out["w"] = assemble(pieces, (n * self.Y, m))

    def gather_task(self, a, last, out):
        rows, F = a.shape
        length = self.X * rows + (0 if last is None else last.shape[0])
        sent = yield [a] + ([] if last is None else [last])
        got = yield [self.shift_x(sent[0], d) for d in range(1, self.X)] + [
            self.swap_core(sent[0])
        ] + [
            self.move(s, lambda z, x, y, c: (z + 1, t, y, c) if x == self.X - 1 else None)
            for s in sent[1:]
            for t in range(self.X)
        ]
        far = got[: self.X - 1]
        send = list(far)
        if last is not None:
            send.append(sum(got[self.X + 1 :], got[self.X]))
        if send:
            sent = yield send
            done = yield [self.swap_core(s) for s in sent]
        pieces = []
        for d in range(self.X):
            at = (self.x - d) % self.X * rows
            mine = a if d == 0 else sent[d - 1]
            other = got[self.X - 1] if d == 0 else done[d - 1]
            pieces.append((mine[None], None, (1, rows, F), (self.c, at, 0)))
            pieces.append((other[None], None, (1, rows, F), (1 - self.c, at, 0)))
        if last is not None:
            n = last.shape[0]
            pieces.append((sent[-1][None], None, (1, n, F), (self.c, self.X * rows, 0)))
            pieces.append((done[-1][None], None, (1, n, F), (1 - self.c, self.X * rows, 0)))
        out["all"] = assemble(pieces, (2, length, F))

    def y_task(self, send, own, out):
        sent = yield send
        got = yield [self.shift_y(p, -i - 1) for i, p in enumerate(sent)]
        acc = own()
        for r in got:
            acc = acc + r.astype(f32)
        out["q"] = acc.astype(bf16)

    def sum_z(self, q):
        groups = [[z * self.X + x for z in range(self.Z)] for x in range(self.X)]
        return lax.psum(q, "seq", axis_index_groups=groups)

    def spread_task(self, q, axis, out):
        keep, send = self.by_core(self.cut(q, axis, 0, 2), self.cut(q, axis, 1, 2))
        keep, send = yield [keep, send]
        moves = [(d, e) for d in range(self.X) for e in range(2) if d or e]
        got = yield [
            self.move((keep, send)[e], lambda z, x, y, c: (z, x + d, y, c ^ e)) for d, e in moves
        ]
        out["done"] = dict(zip(moves, got))
        out["done"][0, 0] = keep

    def scatter_task(self, a, out):
        keep, send = self.by_core(a[0], a[1])
        sent = yield [send]
        got = yield [self.swap_core(sent[0])]
        total = (keep.astype(f32) + got[0].astype(f32)).astype(bf16)
        parts = [
            lax.dynamic_index_in_dim(total, (self.x + d) % self.X, 0, False) for d in range(self.X)
        ]
        sent = yield parts[1:]
        got = yield [self.shift_x(p, d + 1) for d, p in enumerate(sent)]
        acc = parts[0].astype(f32)
        for r in got:
            acc = acc + r.astype(f32)
        out["sum"] = acc

    def gradient_task(self, send, own_part, axis, out):
        half = self.Z // 2
        sent = yield send
        got = yield [self.shift_y(p, -i - 1) for i, p in enumerate(sent)]
        acc = own_part()
        for r in got:
            acc = acc + r.astype(f32)
        q = acc.astype(bf16)
        for step in range(half - 1):
            (q,) = yield [q]
            got = yield [
                self.move(
                    q,
                    lambda z, x, y, c: (z + 1, x, y, c)
                    if z == step
                    else ((z - 1, x, y, c) if z == self.Z - 1 - step else None),
                )
            ]
            q = (q.astype(f32) + got[0].astype(f32)).astype(bf16)
        (q,) = yield [q]
        got = yield [
            self.move(
                q,
                lambda z, x, y, c: (z + 1, x, y, c)
                if z == half - 1
                else ((z - 1, x, y, c) if z == half else None),
            )
        ]
        q = (q.astype(f32) + got[0].astype(f32)).astype(bf16)
        for step in range(half - 1):
            a, b = half - 1 - step, half + step
            (q,) = yield [q]
            got = yield [
                self.move(
                    q,
                    lambda z, x, y, c: (z - 1, x, y, c)
                    if z == a
                    else ((z + 1, x, y, c) if z == b else None),
                )
            ]
            q = jnp.where((self.z == a - 1) | (self.z == b + 1), got[0], q)
        keep, send = self.by_core(self.cut(q, axis, 0, 2), self.cut(q, axis, 1, 2))
        keep, send = yield [keep, send]
        moves = [(d, e) for d in range(self.X) for e in range(2) if d or e]
        got = yield [
            self.move((keep, send)[e], lambda z, x, y, c: (z, x + d, y, c ^ e)) for d, e in moves
        ]
        out["done"] = dict(zip(moves, got))
        out["done"][0, 0] = keep

    def state_task(self, cur, cc, spread, direction, out):
        d = 1
        while d < self.Z // 2:
            send = [cur.astype(bf16)] + ([cc] if 2 * d < self.Z // 2 else [])
            sent = yield send
            got = yield [self.shift_z(a, direction * d) for a in sent]
            cur = cur + spread(cc)[:, None, :] * got[0].astype(f32)
            if len(got) > 1:
                cc = cc * got[1]
            d *= 2
        sent = yield [cur.astype(bf16)]
        got = yield [self.shift_z(sent[0], direction)]
        out["state"] = got[0].astype(f32)

    def small_task(self, v, over_tp, out):
        def turn_z(a, d):
            return self.move(a, lambda z, x, y, c: ((z + d) % self.Z, x, y, c))

        def turn_group(a, d):
            dx, dc = d // 2, d % 2
            return self.move(a, lambda z, x, y, c: (z, x + dx, y, c ^ dc))

        def from_group(d):
            return ((self.x - d // 2) % self.X) * 2 + (self.c ^ (d % 2))

        rounds = [
            (self.Z, lambda d: (self.z - d) % self.Z, turn_z),
            (self.Y, lambda d: (self.y - d) % self.Y, self.shift_y),
            (self.TP, from_group, turn_group),
        ]
        for i, (n, source, shift) in enumerate(rounds):
            sent = yield [v]
            got = yield [shift(sent[0], d) for d in range(1, n)]
            buf = jnp.zeros((n,) + v.shape, v.dtype)
            for d, r in enumerate([v] + got):
                buf = lax.dynamic_update_index_in_dim(buf, r, source(d), 0)
            v = jnp.sum(buf, axis=0) if i < 2 else buf
        out["sum"] = jnp.sum(v, axis=0) if over_tp else v

    def sum_tp_task(self, a, out):
        moves = [(dx, dc) for dx in range(self.X) for dc in range(2) if dx or dc]
        sent = yield [a]
        got = yield [
            self.move(sent[0], lambda z, x, y, c: (z, x + dx, y, c ^ dc)) for dx, dc in moves
        ]
        total = a
        for r in got:
            total = total + r
        out["sum"] = total

    def chunks_task(self, both, SW, out):
        moves = [(dx, dc) for dx in range(self.X) for dc in range(2)]
        parts = []
        for dx, dc in moves:
            jj = (self.x + dx) % self.X * 2 + (self.c ^ dc)
            parts.append(lax.dynamic_slice_in_dim(both, SW * jj, SW, 2))
        sent = yield parts[1:]
        got = yield [
            self.move(p, lambda z, x, y, c: (z, x + dx, y, c ^ dc))
            for p, (dx, dc) in zip(sent, moves[1:])
        ]
        total = parts[0].astype(f32)
        for r in got:
            total = total + r.astype(f32)
        out["sum"] = total

    def one_task(self, arrays, send, out):
        sent = yield arrays
        out["got"] = yield [send(a) for a in sent]


def fence(arrays):
    flat, tree = jax.tree.flatten(arrays)
    return jax.tree.unflatten(tree, lax.optimization_barrier(tuple(flat)))


class Stages:
    def __init__(self):
        self.tasks = []

    def add(self, task, *args):
        out = {}
        gen = task(*args, out)
        self.tasks.append([gen, next(gen), None])
        return out

    def settle(self, live):
        flying = [t for t in self.tasks if t[2] is not None]
        got, live = fence(([t[2] for t in flying], live))
        for t, r in zip(flying, got):
            t[2] = None
            try:
                t[1] = t[0].send(r)
            except StopIteration:
                self.tasks.remove(t)
        return live

    def launch(self, live):
        ready, live = fence(([t[1] for t in self.tasks], live))
        for t, a in zip(self.tasks, ready):
            t[2] = t[0].send(a)
        return live

    def tick(self, live):
        return self.launch(self.settle(live))


def low_dot(a, b, dims):
    return lax.dot_general(a.astype(bf16), b.astype(bf16), dims, preferred_element_type=f32)


def silu_slope(v):
    g = jax.nn.sigmoid(v)
    return g * (1.0 + v * (1.0 - g))


NT = (((1,), (1,)), ((), ()))
TN = (((0,), (0,)), ((), ()))
NN = (((1,), (0,)), ((), ()))
GH = 4
LANES = 256
FAR = -1e30
VMEM_LIMIT = 40 * 1024 * 1024


def bdot(a, b, dims):
    return lax.dot_general(a.astype(bf16), b.astype(bf16), dims, preferred_element_type=f32)


def fdot(a, b, dims):
    return lax.dot_general(a, b, dims, precision=highest, preferred_element_type=f32)


def wide(fac):
    low = lax.broadcasted_iota(jnp.int32, (fac.shape[0], 128), 1) < 64
    pairs = [jnp.where(low, fac[:, i : i + 1], fac[:, i + 1 : i + 2]) for i in (0, 2)]
    return jnp.concatenate(pairs, axis=1)


def head_sum(v):
    lane = lax.broadcasted_iota(jnp.int32, (LANES, 128), 0) // 64
    head = lax.broadcasted_iota(jnp.int32, (LANES, 128), 1)
    return bdot(v, (lane == head).astype(bf16), NN)[:, :GH]


def triangle(strict_lower=False, upper=False):
    r = lax.broadcasted_iota(jnp.int32, (BLOCK, BLOCK), 0)
    t = lax.broadcasted_iota(jnp.int32, (BLOCK, BLOCK), 1)
    keep = t >= r if upper else (t < r if strict_lower else t <= r)
    return keep.astype(f32)


def sigmoid(v):
    return 0.5 * jnp.tanh(0.5 * v) + 0.5


def turned(rows):
    pad = jnp.zeros((120, 128), f32)
    parts = []
    for i in range(rows.shape[1] // 128):
        square = jnp.concatenate([rows[:, i * 128 : (i + 1) * 128], pad], axis=0)
        parts.append(square.T[:, :8])
    return jnp.concatenate(parts, axis=0)


def turn_body(rows, out):
    out[0] = turned(rows[0])


def softplus(v):
    u = jnp.exp(-jnp.abs(v))
    w = 1.0 + u
    log1p = jnp.where(w == 1.0, u, jnp.log(w) * u / jnp.where(w == 1.0, 1.0, w - 1.0))
    return jnp.maximum(v, 0.0) + log1p


def call(kernel, grid, ins, outs, scratch=(), flops=0, name=None):
    arrays = [a for a, _, _ in ins]
    total = sum(a.size * a.dtype.itemsize for a in arrays)
    total += sum(int(np.prod(s)) * jnp.dtype(d).itemsize for s, d, _, _ in outs)
    return pl.pallas_call(
        kernel,
        grid=grid,
        in_specs=[pl.BlockSpec(b, m) for _, b, m in ins],
        out_specs=[pl.BlockSpec(b, m) for _, _, b, m in outs],
        out_shape=[jax.ShapeDtypeStruct(s, d) for s, d, _, _ in outs],
        scratch_shapes=list(scratch),
        compiler_params=pltpu.CompilerParams(vmem_limit_bytes=VMEM_LIMIT),
        cost_estimate=pl.CostEstimate(flops=flops, bytes_accessed=total, transcendentals=0),
        name=name,
    )(*arrays)


def conv_kernel_body(
    nb, pk, dt, sel, hp, marks, kern, bias, x_out, bc_out, s_out, step_out, cum_out, row_out, v_scr, keys_scr
):
    T = nb * BLOCK
    v_scr[:HALO, :] = pk[0, T:, :].astype(f32)
    v_scr[HALO:, :] = pk[0, :T, :].astype(f32)
    pre = bias[...] + kern[0:1, :] * v_scr[HALO : HALO + T, :]
    for k in range(1, 4):
        pre = pre + kern[k : k + 1, :] * (v_scr[HALO - k : HALO - k + T, :] * marks[0, :, k - 1 : k])
    act = pre * sigmoid(pre)
    chunk = pl.program_id(1)

    @pl.when(chunk == 0)
    def _():
        bc_out[...] = act.astype(bf16)
        keys_scr[...] = act[:, : keys_scr.shape[1]].astype(bf16)

    @pl.when(chunk > 0)
    def _():
        x_out[...] = act.astype(bf16)
        raw = bdot(dt[0, :T, :], sel[0], NN)[:, :GH] + hp[0, 0:1, :]
        step = softplus(raw)
        step_out[0, 0] = step
        tri = triangle()
        for b in range(nb):
            rows = slice(b * BLOCK, (b + 1) * BLOCK)
            st = step[rows]
            cum = fdot(tri, -hp[0, 1:2, :] * st, NN)
            cum_out[0, 0, rows, :] = cum
            padded = jnp.concatenate([cum, jnp.zeros((BLOCK, 128 - GH), f32)], axis=1)
            row_out[0, 0, b] = padded.T[:GH]
            tail = jnp.exp(cum[BLOCK - 1 :, :] - cum) * marks[0, rows, 3:4]
            xst = act[rows] * wide(st * tail)
            s_out[0, b] = bdot(keys_scr[rows, :], xst, TN)


def gaps_mask(seg_col, seg_row, transposed):
    r = lax.broadcasted_iota(jnp.int32, (BLOCK, BLOCK), 0)
    t = lax.broadcasted_iota(jnp.int32, (BLOCK, BLOCK), 1)
    order = t >= r if transposed else r >= t
    return jnp.where(order & (seg_col == seg_row), 0.0, FAR)


HALF = BLOCK // 2


def intra_forward_body(x, bc, cum, row, step, marks, flags, hp, y_out, gram, mask):
    @pl.when(pl.program_id(1) == 0)
    def _():
        n = bc.shape[1] // 2
        gram[...] = bdot(bc[:, n:], bc[:, :n], NT)
        mask[...] = gaps_mask(marks[0, :, 6:7], flags[0, 6:7, :], False)

    xf = x[...].astype(f32)
    xs = (xf * wide(step[0, 0])).astype(bf16)
    low = lax.broadcasted_iota(jnp.int32, (HALF, 128), 1) < 64
    c = cum[0, 0]
    for half in range(2):
        rows = slice(half * HALF, (half + 1) * HALF)
        reachable = (half + 1) * HALF
        g = gram[rows, :reachable]
        m = mask[rows, :reachable]
        parts = []
        for i in range(GH):
            d = c[rows, i : i + 1] - row[0, 0, 0, i : i + 1, :reachable] + m
            p = (jnp.exp(d) * g).astype(bf16)
            pair = i // 2 * 128
            parts.append(bdot(p, xs[:reachable, pair : pair + 128], NN))
        y = jnp.concatenate(
            [jnp.where(low, parts[0], parts[1]), jnp.where(low, parts[2], parts[3])], axis=1
        )
        y_out[rows, :] = (y + wide(hp[0, 2:3, :]) * xf[rows]).astype(bf16)


def reach_of(cum, marks):
    return jnp.exp(jnp.minimum(cum, 0.0)) * marks[:, 4:5]


def join_body(nb, y, bc, enter, cum, marks, gate, og, gain, mixed_out, sums_out):
    n = bc.shape[1] // 2
    ones = jnp.ones((16, LANES), bf16)
    first = lax.broadcasted_iota(jnp.int32, (8, BLOCK), 0) == 0
    for b in range(nb):
        rows = slice(b * BLOCK, (b + 1) * BLOCK)
        reach = wide(reach_of(cum[0, 0, rows, :], marks[0, rows, :]))
        state = bdot(bc[rows, n:], enter[0, b], NN) * reach
        mixed = (y[rows, :].astype(f32) + state).astype(bf16)
        mixed_out[rows, :] = mixed
        gv = gate[0, rows, :].astype(f32)
        gated = mixed.astype(f32) * (gv * sigmoid(gv))
        lifted = og[rows, :].astype(f32) * gain[...]
        ss = bdot(ones, gated * gated, NT)[:8]
        sg = bdot(ones, gated * lifted, NT)[:8]
        both = jnp.where(first, ss, sg)

        @pl.when(pl.program_id(1) == 0)
        def _(both=both, rows=rows):
            sums_out[0, :, rows] = both

        @pl.when(pl.program_id(1) > 0)
        def _(both=both, rows=rows):
            sums_out[0, :, rows] += both


def gates_body(
    nb, inner, mixed, gate, og, sums, gain, bc, cum, marks, no_out, gg_out, do_out, gain_out, de_out
):
    n = bc.shape[1] // 2
    T = nb * BLOCK
    total = turned(sums[0]) / inner
    part = None
    for b in range(nb):
        rows = slice(b * BLOCK, (b + 1) * BLOCK)
        gv = gate[0, rows, :].astype(f32)
        sg = sigmoid(gv)
        act = gv * sg
        mx = mixed[rows, :].astype(f32)
        ogv = og[rows, :].astype(f32)
        r = lax.rsqrt(total[rows, 0:1] + epsilon)
        gr = mx * act * r
        no_out[rows, :] = (gr * gain[...]).astype(bf16)
        p = jnp.sum(ogv * gr, axis=0, keepdims=True)
        part = p if part is None else part + p
        grad = r * (ogv * gain[...]) - gr * (r * r * total[rows, 1:2])
        d_out = (grad * act).astype(bf16)
        do_out[rows, :] = d_out
        gg_out[0, rows, :] = (grad * mx * (sg * (1.0 + gv * (1.0 - sg)))).astype(bf16)
        dr = d_out.astype(f32) * wide(reach_of(cum[0, 0, rows, :], marks[0, rows, :]))
        de_out[0, b] = bdot(bc[rows, n:], dr, TN)
    gg_out[0, T:, :] = jnp.zeros((HALO, LANES), bf16)

    @pl.when(pl.program_id(1) == 0)
    def _():
        gain_out[...] = part

    @pl.when(pl.program_id(1) > 0)
    def _():
        gain_out[...] += part


def input_grad_body(gg, xb, tb, wg, wx, wt, out):
    total = bdot(gg[...], wg[...], NN) + bdot(xb[...], wx[...], NN) + bdot(tb[...], wt[...], NN)
    out[...] = total.astype(bf16)


def intra_backward_body(
    x, bc, do, cum, row, step, enter, marks, flags, dxs_out, dec_out, dbc_out, gram, mask, zt, dq
):
    n = bc.shape[1] // 2
    keys, queries = bc[:, :n], bc[:, n:]
    g_id = pl.program_id(1)

    @pl.when(g_id == 0)
    def _():
        gram[...] = bdot(keys, queries, NT)
        mask[...] = gaps_mask(marks[0, :, 6:7], flags[0, 6:7, :], True)
        zt[...] = jnp.zeros_like(zt)
        dq[...] = jnp.zeros_like(dq)

    low = lax.broadcasted_iota(jnp.int32, (BLOCK, 128), 1) < 64
    c = cum[0, 0]
    st = step[0, 0]
    row_sums = [None] * GH
    col_sums = []
    dxs = [[], []]
    for i in range(GH):
        pair = i // 2 * 128
        mine = low if i % 2 == 0 else ~low
        dop = do[:, pair : pair + 128]
        xm = jnp.where(mine, x[:, pair : pair + 128].astype(f32), 0.0).astype(bf16)
        cols = []
        for half in range(2):
            rows = slice(half * HALF, (half + 1) * HALF)
            after = slice(half * HALF, BLOCK)
            e = bdot(xm[rows], dop[after], NT)
            d = row[0, 0, 0, i : i + 1, after] - c[rows, i : i + 1] + mask[rows, after]
            decay = jnp.exp(d)
            le = decay * e * st[rows, i : i + 1]
            zt[rows, after] += le
            gr = gram[rows, after]
            m = le * gr
            total = jnp.sum(m, axis=0, keepdims=True)
            if half == 0:
                row_sums[i] = total
            else:
                row_sums[i] = row_sums[i] + jnp.concatenate([jnp.zeros((1, HALF), f32), total], axis=1)
            cols.append(jnp.sum(m, axis=1, keepdims=True))
            dxs[half].append(bdot((decay * gr).astype(bf16), dop[after], NN))
        col_sums.append(jnp.concatenate(cols, axis=0))
    for half in range(2):
        p = dxs[half]
        lo = low[:HALF]
        dxs_out[half * HALF : (half + 1) * HALF, :] = jnp.concatenate(
            [jnp.where(lo, p[0], p[1]), jnp.where(lo, p[2], p[3])], axis=1
        ).astype(bf16)
    dof = do[...].astype(f32)
    rw = wide(reach_of(c, marks[0]))
    from_state = bdot(queries, enter[0], NN) * rw
    came = head_sum(dof * from_state)
    upper = triangle(upper=True)
    rows4 = jnp.concatenate(row_sums + [jnp.zeros((16 - GH, BLOCK), f32)], axis=0)
    cols4 = jnp.concatenate(col_sums, axis=1)
    dec_out[0, 0] = fdot(upper, rows4, NT)[:, :GH] + fdot(upper, came - cols4, NN)
    dq[...] += bdot(dof * rw, enter[0], NT)

    @pl.when(g_id == pl.num_programs(1) - 1)
    def _():
        z = zt[...].astype(bf16)
        dbc_out[:, :n] = bdot(z, queries, NN)
        dbc_out[:, n:] = dq[...] + bdot(z, keys, TN)


def finish_body(
    nb, pk, x, do, dxl, bc, leave, enter, cum, step, dec, dt, sel, hp, marks, kern, bias,
    back_out, kg_out, sm_out, raw_out, dk_out, v_scr, m_scr,
):
    T = nb * BLOCK
    n = bc.shape[1] // 2
    g_id = pl.program_id(1)
    v_scr[:HALO, :] = pk[0, T:, :].astype(f32)
    v_scr[HALO:, :] = pk[0, :T, :].astype(f32)
    pre = bias[...] + kern[0:1, :] * v_scr[HALO : HALO + T, :]
    for k in range(1, 4):
        pre = pre + kern[k : k + 1, :] * (v_scr[HALO - k : HALO - k + T, :] * marks[0, :, k - 1 : k])
    sg = sigmoid(pre)
    slope = sg * (1.0 + pre * (1.0 - sg))
    raw = bdot(dt[0, :T, :], sel[0], NN)[:, :GH] + hp[0, 0:1, :]
    rate = hp[0, 1:2, :]
    skip = wide(hp[0, 2:3, :])
    strict = triangle(strict_lower=True)
    sums = [0.0, 0.0, 0.0]
    m_scr[:HALO, :] = jnp.zeros((HALO, LANES), f32)
    m_scr[HALO + T :, :] = jnp.zeros((HALO, LANES), f32)
    grads = []
    for b in range(nb):
        rows = slice(b * BLOCK, (b + 1) * BLOCK)
        c = cum[0, 0, rows, :]
        st = step[0, 0, rows, :]
        end = c[BLOCK - 1 :, :]
        tail = wide(jnp.exp(end - c) * marks[0, rows, 3:4])
        stw = wide(st)
        keys = bc[rows, :n]
        lv = leave[0, b]
        kl = bdot(keys, lv, NN) * tail
        dxs = dxl[rows, :].astype(f32) + kl
        dof = do[rows, :].astype(f32)
        xf = x[rows, :].astype(f32)
        xs = xf * stw
        grads.append(skip * dof + stw * dxs)
        out4 = head_sum(xs * kl)
        direct = head_sum(xf * dxs)
        sums[2] = sums[2] + jnp.sum(head_sum(dof * xf), axis=0, keepdims=True)
        dk = bdot(xs * tail, lv, NT)

        @pl.when(g_id == 0)
        def _(dk=dk, rows=rows):
            dk_out[rows, :] = dk

        @pl.when(g_id > 0)
        def _(dk=dk, rows=rows):
            dk_out[rows, :] += dk

        both = jnp.sum(enter[0, b].astype(f32) * lv.astype(f32), axis=0, keepdims=True)
        both = jnp.concatenate([both, jnp.zeros((15, LANES), f32)], axis=0)
        through = head_sum(both)[:1] * jnp.exp(end) * marks[0, b * BLOCK : b * BLOCK + 1, 5:6]
        decay = dec[0, 0, rows, :] + fdot(strict, out4, NN) + through
        sums[1] = sums[1] - rate * jnp.sum(st * decay, axis=0, keepdims=True)
        rg = (direct - rate * decay) * sigmoid(raw[rows])
        sums[0] = sums[0] + jnp.sum(rg, axis=0, keepdims=True)
        raw_out[0, 0, rows, :] = rg
    cg = jnp.concatenate(grads, axis=0) * slope
    sm_out[0, 0] = jnp.concatenate(sums + [jnp.zeros((5, GH), f32)], axis=0)
    kgs = []
    back = None
    for k in range(4):
        m = cg if k == 0 else cg * marks[0, :, k - 1 : k]
        kgs.append(jnp.sum(m * v_scr[HALO - k : HALO - k + T, :], axis=0, keepdims=True))
        m_scr[HALO : HALO + T, :] = m
        part = kern[k : k + 1, :] * m_scr[k : k + T + HALO, :]
        back = part if back is None else back + part
    kgs.append(jnp.sum(cg, axis=0, keepdims=True))
    kg_out[0] = jnp.concatenate(kgs + [jnp.zeros((3, LANES), f32)], axis=0)
    back = back.astype(bf16)
    back_out[0, :T, :] = back[HALO:]
    back_out[0, T:, :] = back[:HALO]

def offsets(index, starts, sizes, steps):
    window = []
    for s, n, step in zip(starts, sizes, steps):
        if not isinstance(s, int):
            s = pl.multiple_of(index[s[0]], step)
        window.append(pl.ds(s, n))
    return tuple(window)


def tabled(moves):
    table = []

    def entry(v):
        if isinstance(v, (int, np.integer)):
            return int(v)
        table.append(jnp.asarray(v, jnp.int32))
        return (len(table) - 1,)

    moves = [tuple(tuple(entry(v) for v in part) for part in m) for m in moves]
    table = table or [jnp.zeros((), jnp.int32)]
    return moves, jnp.stack(table)


def assemble(pieces, shape):
    arrays = [p[0] for p in pieces]
    zero = (0,) * len(shape)
    moves, table = tabled([(zero if s is None else s, at) for _, s, _, at in pieces])
    steps = (1,) * (len(shape) - 2) + (16, 128)

    n = len(arrays)

    def kernel(index, *refs):
        out, held, sems = refs[n], refs[n + 1 : -1], refs[-1]
        loads, stores = [], []
        for i, (source, _) in enumerate(moves):
            window = offsets(index, source, pieces[i][2], steps)
            loads.append(pltpu.make_async_copy(refs[i].at[window], held[i], sems.at[0, i]))
            loads[-1].start()
        for i, (_, target) in enumerate(moves):
            loads[i].wait()
            window = offsets(index, target, pieces[i][2], steps)
            stores.append(pltpu.make_async_copy(held[i], out.at[window], sems.at[1, i]))
            stores[-1].start()
        for c in stores:
            c.wait()

    size = 4 * int(np.prod(shape))
    return pl.pallas_call(
        kernel,
        in_specs=[pl.BlockSpec(memory_space=pltpu.SMEM)]
        + [pl.BlockSpec(memory_space=pl.ANY)] * len(arrays),
        out_specs=pl.BlockSpec(memory_space=pl.ANY),
        out_shape=jax.ShapeDtypeStruct(shape, arrays[0].dtype),
        scratch_shapes=[pltpu.VMEM(p[2], p[0].dtype) for p in pieces]
        + [pltpu.SemaphoreType.DMA((2, n))],
        compiler_params=pltpu.CompilerParams(vmem_limit_bytes=VMEM_LIMIT),
        cost_estimate=pl.CostEstimate(flops=0, bytes_accessed=size, transcendentals=0),
        name="assemble",
    )(table, *arrays)


def place(pieces, moves, shape, buf):
    spots, table = tabled([(s, at) for _, s, _, at in moves])
    n = len(pieces)

    def kernel(index, *refs):
        out, wide_refs, sems = refs[-n - 2], refs[-n - 1 : -1], refs[-1]
        copies = []
        for i in range(n):
            wide_refs[i][...] = refs[i][...].astype(f32)
            for k, (source, target) in enumerate(spots):
                if moves[k][0] != i:
                    continue
                sizes = moves[k][2]
                copies.append(
                    pltpu.make_async_copy(
                        wide_refs[i].at[offsets(index, source, sizes, (8, 128))],
                        out.at[offsets(index, target, sizes, (8, 128))],
                        sems.at[k],
                    )
                )
                copies[-1].start()
        for c in copies:
            c.wait()

    size = sum(6 * p.size for p in pieces)
    extra = [] if buf is None else [buf]
    return pl.pallas_call(
        kernel,
        in_specs=[pl.BlockSpec(memory_space=pltpu.SMEM)]
        + [pl.BlockSpec(memory_space=pltpu.VMEM)] * n
        + [pl.BlockSpec(memory_space=pl.ANY)] * len(extra),
        out_specs=pl.BlockSpec(memory_space=pl.ANY),
        out_shape=jax.ShapeDtypeStruct(shape, f32),
        scratch_shapes=[pltpu.VMEM(p.shape, f32) for p in pieces]
        + [pltpu.SemaphoreType.DMA((len(moves),))],
        input_output_aliases={} if buf is None else {1 + n: 0},
        compiler_params=pltpu.CompilerParams(vmem_limit_bytes=VMEM_LIMIT),
        cost_estimate=pl.CostEstimate(flops=0, bytes_accessed=size, transcendentals=0),
        name="place",
    )(table, *pieces, *extra)


def body(
    g,
    tokens,
    in_weight,
    out_weight,
    pre_gain,
    conv_kernel,
    conv_bias,
    step_bias,
    decay_log,
    skip_gain,
    gate_gain,
    segments,
    cotangent,
):
    g.place()
    heads = step_bias.shape[0]
    inner = gate_gain.shape[0]
    channels = conv_bias.shape[0]
    shared = channels - inner
    state = shared // 2
    taps = conv_kernel.shape[0]
    hd = inner // heads
    HL = heads // g.TP
    HW = HL * hd
    SW = shared // g.TP
    CW = HW + shared
    own_len = tokens.shape[1]
    width = tokens.shape[2]
    own_d = in_weight.shape[0]
    T = own_len * g.X
    TE = T + HALO
    nb = T // BLOCK
    NB = 2 * nb
    G = HW // LANES
    KW = HW + shared + 128
    j = g.j
    other_j = g.x * 2 + 1 - g.c

    w_t = in_weight.T
    rest = jnp.pad(w_t[2 * inner :], ((0, KW - CW - heads), (0, 0)))
    far = g.swap_core(lax.dynamic_slice_in_dim(w_t, inner + HW * other_j, HW, 0))
    far_rest = g.swap_core(rest)
    n_rest = KW - HW
    half_packed = assemble(
        [
            (w_t, (inner + HW * j, 0), (HW, own_d), (0, g.c * own_d)),
            (rest, None, (n_rest, own_d), (HW, g.c * own_d)),
            (far, None, (HW, own_d), (0, (1 - g.c) * own_d)),
            (far_rest, None, (n_rest, own_d), (HW, (1 - g.c) * own_d)),
        ],
        (KW, 2 * own_d),
    )

    series = tokens[0].astype(f32)
    scale = lax.rsqrt(jnp.mean(series * series, axis=-1, keepdims=True) + epsilon)
    normed = g.own_first((series * scale * pre_gain[None, :]).astype(bf16))

    stages = Stages()
    at_n = stages.add(g.gather_task, normed, normed[own_len - HALO :])
    at_packed = stages.add(g.fetch_task, half_packed, 1)
    in_weight, out_weight, cotangent = stages.launch([in_weight, out_weight, cotangent])
    w_t = in_weight.T
    far_gate = g.swap_core(lax.dynamic_slice_in_dim(w_t, HW * other_j, HW, 0))
    far_out = g.swap_core(lax.dynamic_slice_in_dim(out_weight, HW * other_j, HW, 1))
    at_cot = stages.add(g.gather_task, g.own_first(cotangent[0]), None)
    half_gate = assemble(
        [
            (w_t, (HW * j, 0), (HW, own_d), (0, g.c * own_d)),
            (far_gate, None, (HW, own_d), (0, (1 - g.c) * own_d)),
        ],
        (HW, 2 * own_d),
    )
    half_out = assemble(
        [
            (out_weight, (0, HW * j), (own_d, HW), (g.c * own_d, 0)),
            (far_out, None, (own_d, HW), ((1 - g.c) * own_d, 0)),
        ],
        (2 * own_d, HW),
    )

    s_lo, s_hi = g.by_core(segments, g.swap_core(segments))
    seg_all = jnp.concatenate([s_lo, s_hi], axis=0)
    seg_pad = jnp.concatenate([jnp.full((2, HALO), -1, jnp.int32), seg_all], axis=1)
    seg_ext = lax.dynamic_slice_in_dim(seg_pad, g.z * T, T + HALO, 1)
    seg = seg_ext[:, HALO:]
    ends = [seg[:, (b + 1) * BLOCK - 1 : (b + 1) * BLOCK] for b in range(nb)]
    begins = [seg_ext[:, HALO - 1 + b * BLOCK : HALO + b * BLOCK] for b in range(nb)]
    block_end = jnp.concatenate(ends, axis=1)
    prior_end = jnp.concatenate(begins, axis=1)
    carry_flag = (prior_end == block_end).astype(f32)

    def across(cols):
        return jnp.concatenate([jnp.broadcast_to(v, (2, BLOCK)) for v in cols], axis=1)

    end_row, prior_row = across(ends), across(begins)
    flags = [(seg_ext[:, HALO - k : HALO - k + T] == seg) for k in range(1, taps)]
    flags += [seg == end_row, seg == prior_row, end_row == prior_row, seg, jnp.zeros_like(seg)]
    flags = jnp.stack([v.astype(f32) for v in flags], axis=1)

    def own_channels(a):
        x_part = lax.dynamic_slice_in_dim(a, HW * j, HW, a.ndim - 1)
        return jnp.concatenate([x_part, a[..., inner:]], axis=-1)

    def own_heads(a):
        return lax.dynamic_slice_in_dim(a, HL * j, HL, a.ndim - 1)

    kernel_own = own_channels(conv_kernel)
    bias_own = own_channels(conv_bias)[None, :]
    rate = jnp.exp(own_heads(decay_log))
    hp = jnp.stack([own_heads(step_bias), rate, own_heads(skip_gain)]).reshape(3, G, GH)
    hp = jnp.pad(hp.transpose(1, 0, 2), ((0, 0), (0, 5), (0, 0)))
    ids = HL * j + GH * lax.broadcasted_iota(jnp.int32, (G, 128, 128), 0)
    lane = lax.broadcasted_iota(jnp.int32, (G, 128, 128), 2)
    sel = (lax.broadcasted_iota(jnp.int32, (G, 128, 128), 1) == ids + lane) & (lane < GH)
    sel = sel.astype(bf16)
    gain_own = lax.dynamic_slice_in_dim(gate_gain, HW * j, HW, 0)[None, :]
    (marks,) = call(
        turn_body,
        (2,),
        [(flags, (1, 8, T), lambda s: (s, 0, 0))],
        [((2, T, 8), f32, (1, T, 8), lambda s: (s, 0, 0))],
        name="turn",
    )
    held = stages.settle([half_gate, half_out, marks, flags, kernel_own, bias_own, hp, sel, gain_own])
    half_gate, half_out, marks, flags, kernel_own, bias_own, hp, sel, gain_own = held
    stages.launch([])
    half_gate, half_out = stages.settle([half_gate, half_out])
    n_ext = at_n["all"].reshape(2 * TE, width)
    w_packed = at_packed["w"]
    at_gate = stages.add(g.fetch_task, half_gate, 1)
    n_ext, w_packed, half_out = stages.launch([n_ext, w_packed, half_out])

    packed = low_dot(n_ext, w_packed, NT).astype(bf16)
    (packed,) = stages.settle([packed])
    at_out = stages.add(g.direct_task, half_out, [4, 6, 6])
    (packed,) = stages.launch([packed])
    packed = packed.reshape(2, TE, KW)
    marks_b = marks.reshape(NB, BLOCK, 8)

    def seq_block(b):
        return lax.div(b, nb), lax.rem(b, nb)

    def late(c):
        return jnp.maximum(c - 1, 0)

    def shared_first(c):
        return jnp.where(c == 0, G, c - 1)

    dt_block = CW // 128
    x, bc, s_block, step, cum, row = call(
        partial(conv_kernel_body, nb),
        (2, G + 1),
        [
            (packed, (1, TE, LANES), lambda s, c: (s, 0, shared_first(c))),
            (packed, (1, TE, 128), lambda s, c: (s, 0, dt_block)),
            (sel, (1, 128, 128), lambda s, c: (late(c), 0, 0)),
            (hp, (1, 8, GH), lambda s, c: (late(c), 0, 0)),
            (marks, (1, T, 8), lambda s, c: (s, 0, 0)),
            (kernel_own, (taps, LANES), lambda s, c: (0, shared_first(c))),
            (bias_own, (1, LANES), lambda s, c: (0, shared_first(c))),
        ],
        [
            ((2 * T, HW), bf16, (T, LANES), lambda s, c: (s, late(c))),
            ((2 * T, shared), bf16, (T, shared), lambda s, c: (s, 0)),
            ((2, nb, state, HW), f32, (1, nb, state, LANES), lambda s, c: (s, 0, 0, late(c))),
            ((2, G, T, GH), f32, (1, 1, T, GH), lambda s, c: (s, late(c), 0, 0)),
            ((2, G, T, GH), f32, (1, 1, T, GH), lambda s, c: (s, late(c), 0, 0)),
            ((2, G, nb, GH, BLOCK), f32, (1, 1, nb, GH, BLOCK), lambda s, c: (s, late(c), 0, 0, 0)),
        ],
        [pltpu.VMEM((TE, LANES), f32), pltpu.VMEM((T, state), bf16)],
        flops=2 * T * HW * state * 20,
        name="convolve",
    )

    end = jnp.exp(row[..., BLOCK - 1]).transpose(0, 2, 1, 3).reshape(2, nb, HL)
    carry_b = end * carry_flag[:, :, None]

    def spread(a):
        return jnp.repeat(a, hd, axis=-1)

    carry_wide = spread(carry_b)[:, :, None, :]
    carry_range = jnp.prod(carry_b, axis=1)
    s_range = s_block[:, 0]
    for b in range(1, nb):
        s_range = s_block[:, b] + carry_wide[:, b] * s_range
    s_range, x, bc, cum, row, step = stages.settle([s_range, x, bc, cum, row, step])
    at_enter = stages.add(g.state_task, s_range, carry_range, spread, 1)
    x, bc, cum, row, step = stages.launch([x, bc, cum, row, step])

    def tile(a):
        return (a, (BLOCK, LANES), lambda b, k: (b, k))

    def whole(a):
        return (a, (BLOCK, a.shape[1]), lambda b, k: (b, 0))

    def small_tile(a):
        def at(b, k):
            s, m = seq_block(b)
            return s, k, m, 0

        return (a, (1, 1, BLOCK, GH), at)

    def row_tile(b, k):
        s, m = seq_block(b)
        return s, k, m, 0, 0

    def flag_tile(b, k):
        s, m = seq_block(b)
        return s, 0, m

    pair_flops = 2 * 2 * T * BLOCK * HW
    (y_local,) = call(
        intra_forward_body,
        (NB, G),
        [
            tile(x),
            whole(bc),
            small_tile(cum),
            (row, (1, 1, 1, GH, BLOCK), row_tile),
            small_tile(step),
            (marks_b, (1, BLOCK, 8), lambda b, k: (b, 0, 0)),
            (flags, (1, 8, BLOCK), flag_tile),
            (hp, (1, 8, GH), lambda b, k: (k, 0, 0)),
        ],
        [((2 * T, HW), bf16, (BLOCK, LANES), lambda b, k: (b, k))],
        [pltpu.VMEM((BLOCK, BLOCK), f32)] * 2,
        flops=pair_flops * 8,
        name="intra_forward",
    )
    (y_local,) = stages.settle([y_local])
    w_gate = at_gate["w"]
    n_ext, w_gate = stages.launch([n_ext, w_gate])
    gate = low_dot(n_ext, w_gate, NT).astype(bf16)
    (gate,) = stages.settle([gate])
    while "state" not in at_enter or "w" not in at_out:
        stages.launch([])
        stages.settle([])
    enter = [at_enter["state"]]
    for b in range(nb - 1):
        enter.append(s_block[:, b] + carry_wide[:, b] * enter[b])
    enter = jnp.stack(enter, axis=1).astype(bf16)
    w_out = at_out["w"]
    cot_all = at_cot["all"].reshape(2 * T, width)
    out_grad = low_dot(cot_all, w_out, NN).astype(bf16)
    gate = gate.reshape(2, TE, HW)

    def seq_tile(a):
        return (a, (T, LANES), lambda s, k: (s, k))

    def seq_small(a):
        return (a, (1, 1, T, GH), lambda s, k: (s, k, 0, 0))

    def seq_state(a):
        return (a, (1, nb, state, LANES), lambda s, k: (s, 0, 0, k))

    def seq_whole(a):
        return (a, (1,) + a.shape[1:], lambda s, k: (s, 0, 0))

    def lane_tile(a):
        return (a, (a.shape[0], LANES), lambda s, k: (0, k))

    bc_seq = (bc, (T, shared), lambda s, k: (s, 0))
    main_tile = (gate, (1, T, LANES), lambda s, k: (s, 0, k))
    mixed, sums = call(
        partial(join_body, nb),
        (2, G),
        [
            seq_tile(y_local),
            bc_seq,
            seq_state(enter),
            seq_small(cum),
            seq_whole(marks),
            main_tile,
            seq_tile(out_grad),
            lane_tile(gain_own),
        ],
        [
            ((2 * T, HW), bf16, (T, LANES), lambda s, k: (s, k)),
            ((2, 8, T), f32, (1, 8, T), lambda s, k: (s, 0, 0)),
        ],
        flops=pair_flops,
        name="join",
    )
    at_sums = stages.add(g.sum_tp_task, sums)
    stages.launch([])
    stages.settle([])

    def turn(spec):
        a, block, at = spec
        return (a, block, lambda k, s: at(s, k))

    normed_out, gate_grad, d_out, gain_grad, de_block = call(
        partial(gates_body, nb, inner),
        (G, 2),
        [
            turn(v)
            for v in [
                seq_tile(mixed),
                main_tile,
                seq_tile(out_grad),
                seq_whole(at_sums["sum"]),
                lane_tile(gain_own),
                bc_seq,
                seq_small(cum),
                seq_whole(marks),
            ]
        ],
        [
            ((2 * T, HW), bf16, (T, LANES), lambda k, s: (s, k)),
            ((2, TE, HW), bf16, (1, TE, LANES), lambda k, s: (s, 0, k)),
            ((2 * T, HW), bf16, (T, LANES), lambda k, s: (s, k)),
            ((1, HW), f32, (1, LANES), lambda k, s: (0, k)),
            ((2, nb, state, HW), f32, (1, nb, state, LANES), lambda k, s: (s, 0, 0, k)),
        ],
        flops=pair_flops,
        name="gates",
    )
    gate_grad = gate_grad.reshape(2 * TE, HW)

    def far_rows(f, n):
        return [f(i).astype(bf16) for i in range(1, n)]

    def out_part(i):
        return low_dot(g.cut(cot_all, 1, i, g.Y), normed_out, TN)

    def in_part(a, i):
        return low_dot(a, g.cut(n_ext, 1, i, g.Y), TN)

    d_range = de_block[:, nb - 1]
    for b in range(nb - 2, -1, -1):
        d_range = de_block[:, b] + carry_wide[:, b] * d_range
    at_leave = stages.add(g.state_task, d_range, carry_range, spread, -1)
    at_outy = stages.add(g.y_task, far_rows(out_part, g.Y), lambda: out_part(0))
    x, d_out, normed_out, gate_grad = stages.launch([x, d_out, normed_out, gate_grad])
    dxs, dec, dbc = call(
        intra_backward_body,
        (NB, G),
        [
            tile(x),
            whole(bc),
            tile(d_out),
            small_tile(cum),
            (row, (1, 1, 1, GH, BLOCK), row_tile),
            small_tile(step),
            (
                enter.reshape(NB, state, HW),
                (1, state, LANES),
                lambda b, k: (b, 0, k),
            ),
            (marks_b, (1, BLOCK, 8), lambda b, k: (b, 0, 0)),
            (flags, (1, 8, BLOCK), flag_tile),
        ],
        [
            ((2 * T, HW), bf16, (BLOCK, LANES), lambda b, k: (b, k)),
            ((2, G, T, GH), f32) + small_tile(cum)[1:],
            ((2 * T, shared), f32, (BLOCK, shared), lambda b, k: (b, 0)),
        ],
        [pltpu.VMEM((BLOCK, BLOCK), f32)] * 3 + [pltpu.VMEM((BLOCK, state), f32)],
        flops=pair_flops * 16,
        name="intra_backward",
    )
    gate_far = far_rows(lambda i: in_part(gate_grad, i), g.Y)
    dxs, gate_far, normed_out = stages.settle([dxs, gate_far, normed_out])
    out_sum = g.sum_z(at_outy["q"])
    at_gatey = stages.add(g.y_task, gate_far, lambda: in_part(gate_grad, 0))
    dxs, normed_out, gate_grad = stages.launch([dxs, normed_out, gate_grad])
    branch = low_dot(normed_out, w_out, NT).astype(bf16)
    dxs, branch = stages.settle([dxs, branch])
    gate_sum = g.sum_z(at_gatey["q"])
    at_branch = stages.add(g.scatter_task, branch.reshape(2, g.X, own_len, width))
    while "state" not in at_leave:
        stages.launch([])
        stages.settle([])
    leave = [at_leave["state"]]
    for b in range(nb - 1, 0, -1):
        leave.insert(0, de_block[:, b] + carry_wide[:, b] * leave[0])
    leave = jnp.stack(leave, axis=1).astype(bf16)
    leave, dxs = stages.launch([leave, dxs])

    x_back, kg, sm, raw_grad, d_keys = call(
        partial(finish_body, nb),
        (2, G),
        [
            (packed, (1, TE, LANES), lambda s, k: (s, 0, k)),
            seq_tile(x),
            seq_tile(d_out),
            seq_tile(dxs),
            bc_seq,
            seq_state(leave),
            seq_state(enter),
            seq_small(cum),
            seq_small(step),
            seq_small(dec),
            (packed, (1, TE, 128), lambda s, k: (s, 0, dt_block)),
            (sel, (1, 128, 128), lambda s, k: (k, 0, 0)),
            (hp, (1, 8, GH), lambda s, k: (k, 0, 0)),
            seq_whole(marks),
            lane_tile(kernel_own),
            lane_tile(bias_own),
        ],
        [
            ((2, TE, HW), bf16, (1, TE, LANES), lambda s, k: (s, 0, k)),
            ((2, 8, HW), f32, (1, 8, LANES), lambda s, k: (s, 0, k)),
            ((2, G, 8, GH), f32, (1, 1, 8, GH), lambda s, k: (s, k, 0, 0)),
            ((2, G, T, GH), f32, (1, 1, T, GH), lambda s, k: (s, k, 0, 0)),
            ((2 * T, state), f32, (T, state), lambda s, k: (s, 0)),
        ],
        [pltpu.VMEM((TE, LANES), f32), pltpu.VMEM((HALO + TE, LANES), f32)],
        flops=pair_flops * 16,
        name="finish",
    )
    x_back = x_back.reshape(2 * TE, HW)
    cols = min(HW, 512)
    NC = HW // cols

    def x_cut(k):
        return lax.slice_in_dim(x_back, k * cols, (k + 1) * cols, axis=1)

    def x_task(k):
        return (
            g.gradient_task,
            far_rows(lambda i: in_part(x_cut(k), i), g.Y),
            lambda: in_part(x_cut(k), 0),
            1,
        )

    kg = jnp.sum(kg, axis=0)
    x_kg, x_bg = kg[:taps], kg[taps]
    sm = jnp.sum(sm, axis=0)[:, :3].transpose(1, 0, 2).reshape(3, HL)

    both = jnp.concatenate([dbc[:, :state] + d_keys, dbc[:, state:]], axis=-1)
    both = both.astype(bf16).reshape(2, T, shared)
    task = x_task(0)
    task, both, x_back = stages.settle([task[1], both, x_back])
    task = (g.gradient_task, task, lambda: in_part(x_cut(0), 0), 1)
    at_xs = [stages.add(*task)]
    at_both = stages.add(g.chunks_task, both, SW)
    x_back, raw_grad = stages.launch([x_back, raw_grad])
    later = [x_task(k) for k in range(1, NC)]
    later_far, raw_grad = stages.settle([[t[1] for t in later], raw_grad])
    for k in range(1, NC):
        at_xs.append(
            stages.add(g.gradient_task, later_far[k - 1], lambda k=k: in_part(x_cut(k), 0), 1)
        )
    (raw_grad,) = stages.launch([raw_grad])
    both_sum = at_both["sum"]

    def own_shared(a):
        return lax.dynamic_slice_in_dim(a, HW + SW * j, SW, a.ndim - 1)

    sh_in = own_shared(packed).astype(f32)
    sh_in = jnp.concatenate([sh_in[:, T:], sh_in[:, :T]], axis=1)
    sh_kernel = own_shared(kernel_own)
    sh_pre = own_shared(bias_own)[None]
    same = [None] + [marks[:, :, k - 1 : k] for k in range(1, taps)]
    moved = [sh_in[:, HALO - k : HALO - k + T] for k in range(taps)]
    for k in range(taps):
        moved[k] = moved[k] if k == 0 else moved[k] * same[k]
        sh_pre = sh_pre + sh_kernel[k] * moved[k]
    cg = both_sum * silu_slope(sh_pre)
    s_back = 0.0
    s_kg = []
    for k in range(taps):
        m = cg if k == 0 else cg * same[k]
        s_kg.append(jnp.sum(cg * moved[k], axis=(0, 1)))
        s_back = s_back + jnp.pad(sh_kernel[k] * m, ((0, 0), (HALO - k, k), (0, 0)))
    s_kg, s_bg = jnp.stack(s_kg), jnp.sum(cg, axis=(0, 1))
    s_back = jnp.concatenate([s_back[:, HALO:], s_back[:, :HALO]], axis=1)
    raw_low = raw_grad.transpose(0, 2, 1, 3).reshape(2, T, HL)
    raw_low = jnp.pad(raw_low, ((0, 0), (0, HALO), (0, 0)))
    tail_w = SW + HL
    pad_w = 128 - tail_w
    tail_back = jnp.concatenate([s_back, raw_low, jnp.zeros((2, TE, pad_w), f32)], axis=-1)
    tail_back = tail_back.astype(bf16).reshape(2 * TE, 128)
    tail_cut = tail_back[:, :tail_w]
    w_tail = jnp.concatenate(
        [
            lax.dynamic_slice_in_dim(w_packed, HW + SW * j, SW, 0),
            lax.dynamic_slice_in_dim(w_packed, CW + HL * j, HL, 0),
            jnp.zeros((pad_w, width), bf16),
        ],
        axis=0,
    )
    k_all = jnp.concatenate([x_kg, s_kg], axis=1)
    b_all = jnp.concatenate([x_bg, s_bg])
    small = jnp.concatenate([gain_grad.reshape(-1), k_all.reshape(-1), b_all, sm.reshape(-1)])
    n_small = small.shape[0]
    small = jnp.pad(small, (0, -n_small % 1024)).reshape(-1, 128)
    tail_far = far_rows(lambda i: in_part(tail_cut, i), g.Y)
    tail_far, small = stages.settle([tail_far, small])
    at_tail = stages.add(g.gradient_task, tail_far, lambda: in_part(tail_cut, 0), 1)
    at_small = stages.add(g.small_task, small, False)
    x_back, tail_back, gate_grad = stages.launch([x_back, tail_back, gate_grad])

    NW = 512
    (n_grad,) = call(
        input_grad_body,
        (width // NW,),
        [
            (gate_grad, (2 * TE, HW), lambda n: (0, 0)),
            (x_back, (2 * TE, HW), lambda n: (0, 0)),
            (tail_back, (2 * TE, 128), lambda n: (0, 0)),
            (w_gate, (HW, NW), lambda n: (0, n)),
            (w_packed, (HW, NW), lambda n: (0, n)),
            (w_tail, (128, NW), lambda n: (0, n)),
        ],
        [((2 * TE, width), bf16, (2 * TE, NW), lambda n: (0, n))],
        flops=2 * 2 * TE * width * (2 * HW + 128),
        name="input_grad",
    )
    n_grad = n_grad.reshape(2, TE, width)
    (n_grad,) = stages.settle([n_grad])
    at_spill = stages.add(g.one_task, [n_grad[:, T:]], lambda a: g.shift_z(a, -1))
    at_gates = stages.add(g.spread_task, gate_sum, 1)
    (n_grad,) = stages.launch([n_grad])
    (n_grad,) = stages.settle([n_grad])
    last = n_grad[:, T - HALO : T].astype(f32) + at_spill["got"][0].astype(f32)
    n_grad = jnp.concatenate([n_grad[:, : T - HALO], last.astype(bf16)], axis=1)
    at_ngrad = stages.add(g.scatter_task, n_grad.reshape(2, g.X, own_len, width))
    at_outs = stages.add(g.spread_task, out_sum, 0)
    stages.launch([])

    in_shape = (2 * inner + shared + heads, own_d)
    out_shape = (own_d, inner)
    dest = {(d, e): (g.x - d) % g.X * 2 + (g.c ^ e) for d in range(g.X) for e in range(2)}

    def place_rows(done, first, buf):
        keys = list(done)
        moves = [
            (i, (0, 0), done[k].shape, (first + HW * dest[k], 0)) for i, k in enumerate(keys)
        ]
        return place([done[k] for k in keys], moves, in_shape, buf)

    in_buf = place_rows(at_gates["done"], 0, None)
    (in_buf,) = stages.settle([in_buf])
    stages.launch([])
    keys = list(at_outs["done"])
    moves = [(i, (0, 0), (own_d, HW), (0, HW * dest[k])) for i, k in enumerate(keys)]
    out_weight_gradient = place([at_outs["done"][k] for k in keys], moves, out_shape, None)
    (out_weight_gradient,) = stages.settle([out_weight_gradient])
    while "sum" not in at_ngrad:
        stages.launch([])
        stages.settle([])
    stages.launch([])
    n_grad = g.own_first_back(at_ngrad["sum"])
    pre_grad = jnp.sum(n_grad * series * scale, axis=0)
    lifted_n = n_grad * pre_gain[None, :]
    token_gradient = (
        cotangent[0].astype(f32)
        + scale * lifted_n
        - series * scale**3 * jnp.mean(series * lifted_n, axis=-1, keepdims=True)
    )[None]
    block_output = (series + g.own_first_back(at_branch["sum"])).astype(bf16)[None]
    at_pre = stages.add(g.small_task, pre_grad.reshape(-1, 128), True)
    flying = {"x": list(enumerate(at_xs)), "tail": True}
    while stages.tasks or flying["x"] or flying["tail"]:
        if stages.tasks:
            (in_buf,) = stages.settle([in_buf])
            if stages.tasks:
                stages.launch([])
        for k, a in list(flying["x"]):
            if "done" in a:
                in_buf = place_rows(a["done"], inner + k * cols, in_buf)
                flying["x"].remove((k, a))
        if flying["tail"] and "done" in at_tail:
            keys = list(at_tail["done"])
            moves = []
            for i, k in enumerate(keys):
                moves.append((i, (0, 0), (SW, own_d), (2 * inner + SW * dest[k], 0)))
                moves.append((i, (SW, 0), (HL, own_d), (2 * inner + shared + HL * dest[k], 0)))
            in_buf = place([at_tail["done"][k] for k in keys], moves, in_shape, in_buf)
            flying["tail"] = False
    in_weight_gradient = in_buf.T

    small = at_small["sum"].reshape(g.TP, -1)[:, :n_small]
    pre_total = at_pre["sum"].reshape(-1)
    gain_total = small[:, :HW].reshape(-1)
    at = HW
    kt = small[:, at : at + taps * (HW + SW)].reshape(g.TP, taps, HW + SW).transpose(1, 0, 2)
    at += taps * (HW + SW)
    kernel_total = jnp.concatenate(
        [kt[:, :, :HW].reshape(taps, -1), kt[:, :, HW:].reshape(taps, -1)], axis=1
    )
    bt = small[:, at : at + HW + SW]
    at += HW + SW
    bias_total = jnp.concatenate([bt[:, :HW].reshape(-1), bt[:, HW:].reshape(-1)])
    step_total = small[:, at : at + HL].reshape(-1)
    decay_total = small[:, at + HL : at + 2 * HL].reshape(-1)
    skip_total = small[:, at + 2 * HL : at + 3 * HL].reshape(-1)
    return (
        block_output,
        token_gradient,
        in_weight_gradient,
        out_weight_gradient,
        pre_total,
        kernel_total,
        bias_total,
        step_total,
        decay_total,
        skip_total,
        gain_total,
    )


def solution(mesh):
    placed = (
        P("shard", "seq", None),
        P("shard", None),
        P("shard", None),
        P(),
        P(),
        P(),
        P(),
        P(),
        P(),
        P(),
        P("shard", None),
        P("shard", "seq", None),
    )
    results = (P("shard", "seq", None),) * 2 + (P("shard", None),) * 2 + (P(),) * 7
    return jax.shard_map(
        partial(body, Slice(mesh)),
        mesh=mesh,
        in_specs=placed,
        out_specs=results,
        check_vma=False,
    )
```

```python
from functools import partial

import jax
import jax.numpy as jnp
import numpy as np
from jax import lax
from jax.experimental import pallas as pl
from jax.experimental.pallas import tpu as pltpu
from jax.sharding import PartitionSpec as P

BLOCK = 256
HALO = 16
epsilon = 1e-05
highest = lax.Precision.HIGHEST
f32 = jnp.float32
bf16 = jnp.bfloat16
AXES = ("seq", "shard")


class Slice:
    def __init__(self, mesh):
        self.seq = mesh.shape["seq"]
        self.shard = mesh.shape["shard"]
        self.Y = self.shard // 2
        self.W = 4
        self.Z = self.seq // self.W
        self.TP = 2 * self.W

    def place(self):
        s, k = lax.axis_index("seq"), lax.axis_index("shard")
        self.z, self.w = s // self.W, s % self.W
        self.y, self.c = k // 2, k % 2
        self.j = self.w * 2 + self.c

    def move(self, a, target):
        pairs = []
        for z in range(self.Z):
            for w in range(self.W):
                for y in range(self.Y):
                    for c in range(2):
                        to = target(z, w, y, c)
                        if to is None or not 0 <= to[0] < self.Z:
                            continue
                        tz, tw, ty, tc = to
                        src = (z * self.W + w) * self.shard + y * 2 + c
                        dst = (tz * self.W + tw) * self.shard + (ty % self.Y) * 2 + tc
                        pairs.append((src, dst))
        return lax.ppermute(a, AXES, pairs)

    def flip(self, a, d, e=0):
        return self.move(a, lambda z, w, y, c: (z, w ^ d, y, c ^ e))

    def bit(self, d, e):
        return self.c if e else (self.w // d) % 2

    def flip_core(self, a):
        return self.flip(a, 0, 1)

    def shift_y(self, a, d):
        return self.move(a, lambda z, w, y, c: (z, w, y + d, c))

    def shift_z(self, a, d):
        return self.move(a, lambda z, w, y, c: (z + d, w, y, c))

    def by_core(self, own, other):
        first = self.c == 0
        return jnp.where(first, own, other), jnp.where(first, other, own)

    def own_first(self, a):
        width = a.shape[-1] // self.Y
        parts = [
            lax.dynamic_slice_in_dim(a, ((self.y - i) % self.Y) * width, width, a.ndim - 1)
            for i in range(self.Y)
        ]
        return jnp.concatenate(parts, axis=-1)

    def own_first_back(self, a):
        width = a.shape[-1] // self.Y
        parts = [
            lax.dynamic_slice_in_dim(a, ((self.y - t) % self.Y) * width, width, a.ndim - 1)
            for t in range(self.Y)
        ]
        return jnp.concatenate(parts, axis=-1)

    def cut(self, a, axis, i, n):
        size = a.shape[axis] // n
        return lax.slice_in_dim(a, i * size, (i + 1) * size, axis=axis)


    def direct_task(self, half, shares, axis, out):
        n, m = half.shape
        edges = [n * sum(shares[:i]) // sum(shares) // 16 * 16 for i in range(len(shares) + 1)]
        pieces = [(half, None, (n, m), (0, 0))]
        for a, b in zip(edges[:-1], edges[1:]):
            sent = yield [half[a:b] if len(shares) > 1 else half]
            got = yield [self.shift_y(sent[0], d) for d in range(1, self.Y)]
            for d, r in enumerate(got):
                at = (a, (d + 1) * m) if axis else ((d + 1) * n + a, 0)
                pieces.append((r, None, (b - a, m), at))
        out["w"] = assemble(pieces, (n, m * self.Y) if axis else (n * self.Y, m))

    def gather_task(self, a, last, out):
        rows, F = a.shape
        half = rows // 2
        sent = yield [a] + ([] if last is None else [last])
        got = yield [self.flip(sent[0], 1), self.flip(sent[0], 2)] + [
            self.move(s, lambda z, w, y, c: (z + 1, t, y, c) if w == self.W - 1 else None)
            for s in sent[1:]
            for t in range(2)
        ]
        r1, r2 = got[:2]
        n = 0
        up, across = r1[:half], r2[half:]
        if last is not None:
            n = last.shape[0]
            edge = got[2] + got[3]
            up = jnp.concatenate([up, edge], axis=0)
        sent = yield [up, across, jnp.stack([a, r1, r2])]
        up, across, others = yield [
            self.flip(sent[0], 2),
            self.flip(sent[1], 1),
            self.flip_core(sent[2]),
        ]
        far = jnp.concatenate([up[:half], across], axis=0)
        if last is not None:
            edge = jnp.where(self.w < 2, edge, up[half:])
            far = jnp.concatenate([far, edge], axis=0)
        (far,) = yield [far]
        (far_other,) = yield [self.flip_core(far)]
        pieces = []
        for i, (d, mine) in enumerate(((0, a), (1, r1), (2, r2))):
            at = (self.w ^ d) * rows
            pieces.append((mine[None], None, (1, rows, F), (self.c, at, 0)))
            pieces.append((others, (i, 0, 0), (1, rows, F), (1 - self.c, at, 0)))
        length = self.W * rows
        for c, part in ((self.c, far[None]), (1 - self.c, far_other[None])):
            pieces.append((part, (0, 0, 0), (1, rows, F), (c, (self.w ^ 3) * rows, 0)))
            if n:
                pieces.append((part, (0, rows, 0), (1, n, F), (c, length, 0)))
        out["all"] = assemble(pieces, (2, length + n, F))

    def scatter_task(self, a, order, out):
        keep, send = self.by_core(a[0], a[1])
        sent = yield [send]
        got = yield [self.flip(sent[0], 0, 1)]
        total = (keep.astype(f32) + got[0].astype(f32)).astype(bf16)

        def part(d):
            return lax.dynamic_index_in_dim(total, self.w ^ d, 0, False)

        d1, d2 = order
        sent = yield [jnp.stack([part(d1), part(3)])]
        got = yield [self.flip(sent[0], d1)]
        mine = part(0).astype(f32) + got[0][0].astype(f32)
        pass_on = (part(d2).astype(f32) + got[0][1].astype(f32)).astype(bf16)
        sent = yield [pass_on]
        got = yield [self.flip(sent[0], d2)]
        out["sum"] = mine + got[0].astype(f32)

    def gradient_task(self, send, own_part, axis, order, out):
        half = self.Z // 2
        over_group = order is None
        halvings = [(0, 1), (1, 0), (2, 0)]
        sent = yield send
        got = yield [self.shift_y(p, -i - 1) for i, p in enumerate(sent)]
        acc = own_part()
        for r in got:
            acc = acc + r.astype(f32)
        q = acc.astype(bf16)
        if over_group:
            for d, e in halvings:
                n = q.shape[0] // 2
                b = self.bit(d, e)
                keep = lax.dynamic_slice_in_dim(q, b * n, n, 0)
                (send,) = yield [lax.dynamic_slice_in_dim(q, (1 - b) * n, n, 0)]
                (got,) = yield [self.flip(send, d, e)]
                q = (keep.astype(f32) + got.astype(f32)).astype(bf16)
        for step in range(half - 1):
            (q,) = yield [q]
            got = yield [
                self.move(
                    q,
                    lambda z, w, y, c: (z + 1, w, y, c)
                    if z == step
                    else ((z - 1, w, y, c) if z == self.Z - 1 - step else None),
                )
            ]
            q = (q.astype(f32) + got[0].astype(f32)).astype(bf16)
        (q,) = yield [q]
        got = yield [
            self.move(
                q,
                lambda z, w, y, c: (z + 1, w, y, c)
                if z == half - 1
                else ((z - 1, w, y, c) if z == half else None),
            )
        ]
        q = (q.astype(f32) + got[0].astype(f32)).astype(bf16)
        for step in range(half - 1):
            a, b = half - 1 - step, half + step
            (q,) = yield [q]
            got = yield [
                self.move(
                    q,
                    lambda z, w, y, c: (z - 1, w, y, c)
                    if z == a
                    else ((z + 1, w, y, c) if z == b else None),
                )
            ]
            q = jnp.where((self.z == a - 1) | (self.z == b + 1), got[0], q)
        if over_group:
            for d, e in reversed(halvings):
                (q,) = yield [q]
                if e:
                    keep, send = self.by_core(self.cut(q, 1, 0, 2), self.cut(q, 1, 1, 2))
                    (got,) = yield [self.flip(send, d, e)]
                    q = keep
                else:
                    (got,) = yield [self.flip(q, d, e)]
                low = self.bit(d, e) == 0
                q = jnp.concatenate([jnp.where(low, q, got), jnp.where(low, got, q)], axis=0)
            out["done"] = q
            return
        keep, send = self.by_core(self.cut(q, axis, 0, 2), self.cut(q, axis, 1, 2))
        (send,) = yield [send]
        got = yield [self.flip(send, 0, 1)]
        pair = jnp.concatenate([keep, got[0]], axis=1 - axis)
        (pair,) = yield [pair]
        got = yield [self.flip(pair, order[0])]
        quad = jnp.concatenate([pair, got[0]], axis=1 - axis)
        (quad,) = yield [quad]
        got = yield [self.flip(quad, order[1])]
        out["done"] = [quad, got[0]]
        a, b = order
        out["from"] = [(0, 0), (0, 1), (a, 0), (a, 1), (b, 0), (b, 1), (a ^ b, 0), (a ^ b, 1)]

    def state_task(self, cur, cc, spread, direction, out):
        d = 1
        while d < self.Z // 2:
            send = [cur.astype(bf16)] + ([cc] if 2 * d < self.Z // 2 else [])
            sent = yield send
            got = yield [self.shift_z(a, direction * d) for a in sent]
            cur = cur + spread(cc)[:, None, :] * got[0].astype(f32)
            if len(got) > 1:
                cc = cc * got[1]
            d *= 2
        sent = yield [cur.astype(bf16)]
        got = yield [self.shift_z(sent[0], direction)]
        out["state"] = got[0].astype(f32)

    def sum_tp_task(self, a, out):
        sent = yield [a]
        got = yield [self.flip_core(sent[0])]
        (a,) = yield [a + got[0]]
        got = yield [self.flip(a, d) for d in range(1, self.W)]
        for r in got:
            a = a + r
        out["sum"] = a

    def one_task(self, arrays, send, out):
        sent = yield arrays
        out["got"] = yield [send(a) for a in sent]


def fence(arrays):
    flat, tree = jax.tree.flatten(arrays)
    return jax.tree.unflatten(tree, lax.optimization_barrier(tuple(flat)))


class Stages:
    def __init__(self):
        self.tasks = []

    def add(self, task, *args):
        out = {}
        gen = task(*args, out)
        self.tasks.append([gen, next(gen), None, out])
        return out

    def settle(self, live, leave=()):
        flying = [t for t in self.tasks if t[2] is not None and not any(t[3] is o for o in leave)]
        got, live = fence(([t[2] for t in flying], live))
        for t, r in zip(flying, got):
            t[2] = None
            try:
                t[1] = t[0].send(r)
            except StopIteration:
                self.tasks.remove(t)
        return live

    def launch(self, live):
        waiting = [t for t in self.tasks if t[2] is None]
        ready, live = fence(([t[1] for t in waiting], live))
        for t, a in zip(waiting, ready):
            t[2] = t[0].send(a)
        return live


def low_dot(a, b, dims):
    return lax.dot_general(a.astype(bf16), b.astype(bf16), dims, preferred_element_type=f32)


NT = (((1,), (1,)), ((), ()))
TN = (((0,), (0,)), ((), ()))
NN = (((1,), (0,)), ((), ()))
GH = 4
LANES = 256
FAR = -1e30
VMEM_LIMIT = 40 * 1024 * 1024


def bdot(a, b, dims):
    return lax.dot_general(a.astype(bf16), b.astype(bf16), dims, preferred_element_type=f32)


def fdot(a, b, dims):
    return lax.dot_general(a, b, dims, precision=highest, preferred_element_type=f32)


def wide(fac):
    low = lax.broadcasted_iota(jnp.int32, (fac.shape[0], 128), 1) < 64
    pairs = [jnp.where(low, fac[:, i : i + 1], fac[:, i + 1 : i + 2]) for i in (0, 2)]
    return jnp.concatenate(pairs, axis=1)


def head_sum(v):
    lane = lax.broadcasted_iota(jnp.int32, (LANES, 128), 0) // 64
    head = lax.broadcasted_iota(jnp.int32, (LANES, 128), 1)
    return bdot(v, (lane == head).astype(bf16), NN)[:, :GH]


def triangle(strict_lower=False, upper=False):
    r = lax.broadcasted_iota(jnp.int32, (BLOCK, BLOCK), 0)
    t = lax.broadcasted_iota(jnp.int32, (BLOCK, BLOCK), 1)
    keep = t >= r if upper else (t < r if strict_lower else t <= r)
    return keep.astype(f32)


def sigmoid(v):
    return 0.5 * jnp.tanh(0.5 * v) + 0.5


def turned(rows):
    pad = jnp.zeros((120, 128), f32)
    parts = []
    for i in range(rows.shape[1] // 128):
        square = jnp.concatenate([rows[:, i * 128 : (i + 1) * 128], pad], axis=0)
        parts.append(square.T[:, :8])
    return jnp.concatenate(parts, axis=0)


def turn_body(rows, out):
    out[0] = turned(rows[0])


def softplus(v):
    u = jnp.exp(-jnp.abs(v))
    w = 1.0 + u
    log1p = jnp.where(w == 1.0, u, jnp.log(w) * u / jnp.where(w == 1.0, 1.0, w - 1.0))
    return jnp.maximum(v, 0.0) + log1p


def call(kernel, grid, ins, outs, scratch=(), flops=0, name=None):
    arrays = [a for a, _, _ in ins]
    total = sum(a.size * a.dtype.itemsize for a in arrays)
    total += sum(int(np.prod(s)) * jnp.dtype(d).itemsize for s, d, _, _ in outs)
    return pl.pallas_call(
        kernel,
        grid=grid,
        in_specs=[pl.BlockSpec(b, m) for _, b, m in ins],
        out_specs=[pl.BlockSpec(b, m) for _, _, b, m in outs],
        out_shape=[jax.ShapeDtypeStruct(s, d) for s, d, _, _ in outs],
        scratch_shapes=list(scratch),
        compiler_params=pltpu.CompilerParams(vmem_limit_bytes=VMEM_LIMIT),
        cost_estimate=pl.CostEstimate(flops=flops, bytes_accessed=total, transcendentals=0),
        name=name,
    )(*arrays)


def conv_kernel_body(
    nb, pk, dt, sel, hp, marks, kern, bias, x_out, bc_out, s_out, step_out, cum_out, row_out, v_scr, keys_scr
):
    T = nb * BLOCK
    v_scr[:HALO, :] = pk[0, T:, :].astype(f32)
    v_scr[HALO:, :] = pk[0, :T, :].astype(f32)
    pre = bias[...] + kern[0:1, :] * v_scr[HALO : HALO + T, :]
    for k in range(1, 4):
        pre = pre + kern[k : k + 1, :] * (v_scr[HALO - k : HALO - k + T, :] * marks[0, :, k - 1 : k])
    act = pre * sigmoid(pre)
    chunk = pl.program_id(1)

    @pl.when(chunk == 0)
    def _():
        bc_out[...] = act.astype(bf16)
        keys_scr[...] = act[:, : keys_scr.shape[1]].astype(bf16)

    @pl.when(chunk > 0)
    def _():
        x_out[...] = act.astype(bf16)
        raw = bdot(dt[0, :T, :], sel[0], NN)[:, :GH] + hp[0, 0:1, :]
        step = softplus(raw)
        step_out[0, 0] = step
        tri = triangle()
        for b in range(nb):
            rows = slice(b * BLOCK, (b + 1) * BLOCK)
            st = step[rows]
            cum = fdot(tri, -hp[0, 1:2, :] * st, NN)
            cum_out[0, 0, rows, :] = cum
            padded = jnp.concatenate([cum, jnp.zeros((BLOCK, 128 - GH), f32)], axis=1)
            row_out[0, 0, b] = padded.T[:GH]
            tail = jnp.exp(cum[BLOCK - 1 :, :] - cum) * marks[0, rows, 3:4]
            xst = act[rows] * wide(st * tail)
            s_out[0, b] = bdot(keys_scr[rows, :], xst, TN)


def gaps_mask(seg_col, seg_row, transposed):
    r = lax.broadcasted_iota(jnp.int32, (BLOCK, BLOCK), 0)
    t = lax.broadcasted_iota(jnp.int32, (BLOCK, BLOCK), 1)
    order = t >= r if transposed else r >= t
    return jnp.where(order & (seg_col == seg_row), 0.0, FAR)


HALF = BLOCK // 2


def intra_forward_body(x, bc, cum, row, step, marks, flags, hp, y_out, gram, mask):
    @pl.when(pl.program_id(1) == 0)
    def _():
        n = bc.shape[1] // 2
        gram[...] = bdot(bc[:, n:], bc[:, :n], NT)
        mask[...] = gaps_mask(marks[0, :, 6:7], flags[0, 6:7, :], False)

    xf = x[...].astype(f32)
    xs = (xf * wide(step[0, 0])).astype(bf16)
    low = lax.broadcasted_iota(jnp.int32, (HALF, 128), 1) < 64
    c = cum[0, 0]
    for half in range(2):
        rows = slice(half * HALF, (half + 1) * HALF)
        reachable = (half + 1) * HALF
        g = gram[rows, :reachable]
        m = mask[rows, :reachable]
        parts = []
        for i in range(GH):
            d = c[rows, i : i + 1] - row[0, 0, 0, i : i + 1, :reachable] + m
            p = (jnp.exp(d) * g).astype(bf16)
            pair = i // 2 * 128
            parts.append(bdot(p, xs[:reachable, pair : pair + 128], NN))
        y = jnp.concatenate(
            [jnp.where(low, parts[0], parts[1]), jnp.where(low, parts[2], parts[3])], axis=1
        )
        y_out[rows, :] = (y + wide(hp[0, 2:3, :]) * xf[rows]).astype(bf16)


def reach_of(cum, marks):
    return jnp.exp(jnp.minimum(cum, 0.0)) * marks[:, 4:5]


def join_body(nb, y, bc, enter, cum, marks, gate, og, gain, mixed_out, sums_out):
    n = bc.shape[1] // 2
    ones = jnp.ones((16, LANES), bf16)
    first = lax.broadcasted_iota(jnp.int32, (8, BLOCK), 0) == 0
    for b in range(nb):
        rows = slice(b * BLOCK, (b + 1) * BLOCK)
        reach = wide(reach_of(cum[0, 0, rows, :], marks[0, rows, :]))
        state = bdot(bc[rows, n:], enter[0, b], NN) * reach
        mixed = (y[rows, :].astype(f32) + state).astype(bf16)
        mixed_out[rows, :] = mixed
        gv = gate[0, rows, :].astype(f32)
        gated = mixed.astype(f32) * (gv * sigmoid(gv))
        lifted = og[rows, :].astype(f32) * gain[...]
        ss = bdot(ones, gated * gated, NT)[:8]
        sg = bdot(ones, gated * lifted, NT)[:8]
        both = jnp.where(first, ss, sg)

        @pl.when(pl.program_id(1) == 0)
        def _(both=both, rows=rows):
            sums_out[0, :, rows] = both

        @pl.when(pl.program_id(1) > 0)
        def _(both=both, rows=rows):
            sums_out[0, :, rows] += both


def gates_body(
    nb, inner, mixed, gate, og, sums, gain, bc, cum, marks, no_out, gg_out, do_out, gain_out, de_out
):
    n = bc.shape[1] // 2
    T = nb * BLOCK
    total = turned(sums[0]) / inner
    part = None
    for b in range(nb):
        rows = slice(b * BLOCK, (b + 1) * BLOCK)
        gv = gate[0, rows, :].astype(f32)
        sg = sigmoid(gv)
        act = gv * sg
        mx = mixed[rows, :].astype(f32)
        ogv = og[rows, :].astype(f32)
        r = lax.rsqrt(total[rows, 0:1] + epsilon)
        gr = mx * act * r
        no_out[rows, :] = (gr * gain[...]).astype(bf16)
        p = jnp.sum(ogv * gr, axis=0, keepdims=True)
        part = p if part is None else part + p
        grad = r * (ogv * gain[...]) - gr * (r * r * total[rows, 1:2])
        d_out = (grad * act).astype(bf16)
        do_out[rows, :] = d_out
        gg_out[0, rows, :] = (grad * mx * (sg * (1.0 + gv * (1.0 - sg)))).astype(bf16)
        dr = d_out.astype(f32) * wide(reach_of(cum[0, 0, rows, :], marks[0, rows, :]))
        de_out[0, b] = bdot(bc[rows, n:], dr, TN)
    gg_out[0, T:, :] = jnp.zeros((HALO, LANES), bf16)

    @pl.when(pl.program_id(1) == 0)
    def _():
        gain_out[...] = part

    @pl.when(pl.program_id(1) > 0)
    def _():
        gain_out[...] += part


def input_grad_body(gg, xb, tb, wg, wx, wt, spill, rows, out, gain_out):
    total = bdot(gg[...], wg[...], NN) + bdot(xb[...], wx[...], NN) + bdot(tb[...], wt[...], NN)
    T = out.shape[1]
    out[0, : T - HALO, :] = total[: T - HALO].astype(bf16)
    out[0, T - HALO :, :] = (total[T - HALO : T] + spill[0].astype(f32)).astype(bf16)
    part = jnp.sum(total * rows[...].astype(f32), axis=0, keepdims=True)
    gain_out[0] = jnp.concatenate([part, jnp.zeros((7, part.shape[1]), f32)], axis=0)


def intra_backward_body(
    x, bc, do, cum, row, step, enter, marks, flags, dxs_out, dec_out, dbc_out, gram, mask, zt, dq
):
    n = bc.shape[1] // 2
    keys, queries = bc[:, :n], bc[:, n:]
    g_id = pl.program_id(1)

    @pl.when(g_id == 0)
    def _():
        gram[...] = bdot(keys, queries, NT)
        mask[...] = gaps_mask(marks[0, :, 6:7], flags[0, 6:7, :], True)
        zt[...] = jnp.zeros_like(zt)
        dq[...] = jnp.zeros_like(dq)

    low = lax.broadcasted_iota(jnp.int32, (BLOCK, 128), 1) < 64
    c = cum[0, 0]
    st = step[0, 0]
    row_sums = [None] * GH
    col_sums = []
    dxs = [[], []]
    for i in range(GH):
        pair = i // 2 * 128
        mine = low if i % 2 == 0 else ~low
        dop = do[:, pair : pair + 128]
        xm = jnp.where(mine, x[:, pair : pair + 128].astype(f32), 0.0).astype(bf16)
        cols = []
        for half in range(2):
            rows = slice(half * HALF, (half + 1) * HALF)
            after = slice(half * HALF, BLOCK)
            e = bdot(xm[rows], dop[after], NT)
            d = row[0, 0, 0, i : i + 1, after] - c[rows, i : i + 1] + mask[rows, after]
            decay = jnp.exp(d)
            le = decay * e * st[rows, i : i + 1]
            zt[rows, after] += le
            gr = gram[rows, after]
            m = le * gr
            total = jnp.sum(m, axis=0, keepdims=True)
            if half == 0:
                row_sums[i] = total
            else:
                row_sums[i] = row_sums[i] + jnp.concatenate([jnp.zeros((1, HALF), f32), total], axis=1)
            cols.append(jnp.sum(m, axis=1, keepdims=True))
            dxs[half].append(bdot((decay * gr).astype(bf16), dop[after], NN))
        col_sums.append(jnp.concatenate(cols, axis=0))
    for half in range(2):
        p = dxs[half]
        lo = low[:HALF]
        dxs_out[half * HALF : (half + 1) * HALF, :] = jnp.concatenate(
            [jnp.where(lo, p[0], p[1]), jnp.where(lo, p[2], p[3])], axis=1
        ).astype(bf16)
    dof = do[...].astype(f32)
    rw = wide(reach_of(c, marks[0]))
    from_state = bdot(queries, enter[0], NN) * rw
    came = head_sum(dof * from_state)
    upper = triangle(upper=True)
    rows4 = jnp.concatenate(row_sums + [jnp.zeros((16 - GH, BLOCK), f32)], axis=0)
    cols4 = jnp.concatenate(col_sums, axis=1)
    dec_out[0, 0] = fdot(upper, rows4, NT)[:, :GH] + fdot(upper, came - cols4, NN)
    dq[...] += bdot(dof * rw, enter[0], NT)

    @pl.when(g_id == pl.num_programs(1) - 1)
    def _():
        z = zt[...].astype(bf16)
        dbc_out[:, :n] = bdot(z, queries, NN)
        dbc_out[:, n:] = dq[...] + bdot(z, keys, TN)


def finish_body(
    nb, pk, x, do, dxl, bc, dbc, leave, enter, cum, step, dec, dt, sel, hp, marks, kern, bias,
    back_out, dt_out, kg_out, sm_out, v_scr, m_scr, grad, dk,
):
    T = nb * BLOCK
    n = bc.shape[1] // 2
    g_id = pl.program_id(1)
    last = pl.num_programs(1) - 1

    @pl.when(g_id == 0)
    def _():
        dk[...] = jnp.zeros_like(dk)
        dt_out[0] = jnp.zeros((T + HALO, 128), bf16)

    @pl.when(g_id < last)
    def _():
        rate = hp[0, 1:2, :]
        skip = wide(hp[0, 2:3, :])
        strict = triangle(strict_lower=True)
        sums = [0.0, 0.0, 0.0]
        for b in range(nb):
            rows = slice(b * BLOCK, (b + 1) * BLOCK)
            c = cum[0, 0, rows, :]
            st = step[0, 0, rows, :]
            end = c[BLOCK - 1 :, :]
            tail = wide(jnp.exp(end - c) * marks[0, rows, 3:4])
            stw = wide(st)
            lv = leave[0, b]
            kl = bdot(bc[rows, :n], lv, NN) * tail
            dxs = dxl[rows, :].astype(f32) + kl
            dof = do[rows, :].astype(f32)
            xf = x[rows, :].astype(f32)
            xs = xf * stw
            grad[rows, :] = skip * dof + stw * dxs
            out4 = head_sum(xs * kl)
            direct = head_sum(xf * dxs)
            sums[2] = sums[2] + jnp.sum(head_sum(dof * xf), axis=0, keepdims=True)
            dk[rows, :] += bdot(xs * tail, lv, NT)
            both = jnp.sum(enter[0, b].astype(f32) * lv.astype(f32), axis=0, keepdims=True)
            both = jnp.concatenate([both, jnp.zeros((15, LANES), f32)], axis=0)
            through = head_sum(both)[:1] * jnp.exp(end) * marks[0, b * BLOCK : b * BLOCK + 1, 5:6]
            decay = dec[0, 0, rows, :] + fdot(strict, out4, NN) + through
            sums[1] = sums[1] - rate * jnp.sum(st * decay, axis=0, keepdims=True)
            raw = bdot(dt[0, rows, :], sel[0], NN)[:, :GH] + hp[0, 0:1, :]
            rg = (direct - rate * decay) * sigmoid(raw)
            sums[0] = sums[0] + jnp.sum(rg, axis=0, keepdims=True)
            padded = jnp.concatenate([rg, jnp.zeros((BLOCK, 128 - GH), f32)], axis=1)
            spot = bdot(padded, sel[0], NT)
            dt_out[0, rows, :] = (dt_out[0, rows, :].astype(f32) + spot).astype(bf16)
        sm_out[0, 0] = jnp.concatenate(sums + [jnp.zeros((5, GH), f32)], axis=0)

    @pl.when(g_id == last)
    def _():
        grad[...] = jnp.concatenate([dbc[:, :n] + dk[...], dbc[:, n:]], axis=1)

    v_scr[:HALO, :] = pk[0, T:, :].astype(f32)
    v_scr[HALO:, :] = pk[0, :T, :].astype(f32)
    pre = bias[...] + kern[0:1, :] * v_scr[HALO : HALO + T, :]
    for k in range(1, 4):
        pre = pre + kern[k : k + 1, :] * (v_scr[HALO - k : HALO - k + T, :] * marks[0, :, k - 1 : k])
    sg = sigmoid(pre)
    cg = grad[...] * (sg * (1.0 + pre * (1.0 - sg)))
    m_scr[:HALO, :] = jnp.zeros((HALO, LANES), f32)
    m_scr[HALO + T :, :] = jnp.zeros((HALO, LANES), f32)
    kgs = []
    back = None
    for k in range(4):
        m = cg if k == 0 else cg * marks[0, :, k - 1 : k]
        kgs.append(jnp.sum(m * v_scr[HALO - k : HALO - k + T, :], axis=0, keepdims=True))
        m_scr[HALO : HALO + T, :] = m
        part = kern[k : k + 1, :] * m_scr[k : k + T + HALO, :]
        back = part if back is None else back + part
    kgs.append(jnp.sum(cg, axis=0, keepdims=True))
    kg_out[0] = jnp.concatenate(kgs + [jnp.zeros((3, LANES), f32)], axis=0)
    back = back.astype(bf16)
    back_out[0, :T, :] = back[HALO:]
    back_out[0, T:, :] = back[:HALO]

def offsets(index, starts, sizes, steps):
    window = []
    for s, n, step in zip(starts, sizes, steps):
        if not isinstance(s, int):
            s = pl.multiple_of(index[s[0]], step)
        window.append(pl.ds(s, n))
    return tuple(window)


def tabled(moves):
    table = []

    def entry(v):
        if isinstance(v, (int, np.integer)):
            return int(v)
        table.append(jnp.asarray(v, jnp.int32))
        return (len(table) - 1,)

    moves = [tuple(tuple(entry(v) for v in part) for part in m) for m in moves]
    table = table or [jnp.zeros((), jnp.int32)]
    return moves, jnp.stack(table)


def assemble(pieces, shape):
    arrays = [p[0] for p in pieces]
    zero = (0,) * len(shape)
    moves, table = tabled([(zero if s is None else s, at) for _, s, _, at in pieces])
    steps = (1,) * (len(shape) - 2) + (16, 128)

    n = len(arrays)

    def kernel(index, *refs):
        out, held, sems = refs[n], refs[n + 1 : -1], refs[-1]
        loads, stores = [], []
        for i, (source, _) in enumerate(moves):
            window = offsets(index, source, pieces[i][2], steps)
            loads.append(pltpu.make_async_copy(refs[i].at[window], held[i], sems.at[0, i]))
            loads[-1].start()
        for i, (_, target) in enumerate(moves):
            loads[i].wait()
            window = offsets(index, target, pieces[i][2], steps)
            stores.append(pltpu.make_async_copy(held[i], out.at[window], sems.at[1, i]))
            stores[-1].start()
        for c in stores:
            c.wait()

    size = 4 * int(np.prod(shape))
    return pl.pallas_call(
        kernel,
        in_specs=[pl.BlockSpec(memory_space=pltpu.SMEM)]
        + [pl.BlockSpec(memory_space=pltpu.HBM)] * len(arrays),
        out_specs=pl.BlockSpec(memory_space=pl.ANY),
        out_shape=jax.ShapeDtypeStruct(shape, arrays[0].dtype),
        scratch_shapes=[pltpu.VMEM(p[2], p[0].dtype) for p in pieces]
        + [pltpu.SemaphoreType.DMA((2, n))],
        compiler_params=pltpu.CompilerParams(vmem_limit_bytes=VMEM_LIMIT),
        cost_estimate=pl.CostEstimate(flops=0, bytes_accessed=size, transcendentals=0),
        name="assemble",
    )(table, *arrays)


def place(pieces, moves, shape, buf):
    spots, table = tabled([(s, at) for _, s, _, at in moves])
    n = len(pieces)

    def kernel(index, *refs):
        out, wide_refs, sems = refs[-n - 2], refs[-n - 1 : -1], refs[-1]
        copies = []
        for i in range(n):
            wide_refs[i][...] = refs[i][...].astype(f32)
            for k, (source, target) in enumerate(spots):
                if moves[k][0] != i:
                    continue
                sizes = moves[k][2]
                copies.append(
                    pltpu.make_async_copy(
                        wide_refs[i].at[offsets(index, source, sizes, (8, 128))],
                        out.at[offsets(index, target, sizes, (8, 128))],
                        sems.at[k],
                    )
                )
                copies[-1].start()
        for c in copies:
            c.wait()

    size = sum(6 * p.size for p in pieces)
    extra = [] if buf is None else [buf]
    return pl.pallas_call(
        kernel,
        in_specs=[pl.BlockSpec(memory_space=pltpu.SMEM)]
        + [pl.BlockSpec(memory_space=pltpu.VMEM)] * n
        + [pl.BlockSpec(memory_space=pl.ANY)] * len(extra),
        out_specs=pl.BlockSpec(memory_space=pl.ANY),
        out_shape=jax.ShapeDtypeStruct(shape, f32),
        scratch_shapes=[pltpu.VMEM(p.shape, f32) for p in pieces]
        + [pltpu.SemaphoreType.DMA((len(moves),))],
        input_output_aliases={} if buf is None else {1 + n: 0},
        compiler_params=pltpu.CompilerParams(vmem_limit_bytes=VMEM_LIMIT),
        cost_estimate=pl.CostEstimate(flops=0, bytes_accessed=size, transcendentals=0),
        name="place",
    )(table, *pieces, *extra)


def body(
    g,
    tokens,
    in_weight,
    out_weight,
    pre_gain,
    conv_kernel,
    conv_bias,
    step_bias,
    decay_log,
    skip_gain,
    gate_gain,
    segments,
    cotangent,
):
    g.place()
    heads = step_bias.shape[0]
    inner = gate_gain.shape[0]
    channels = conv_bias.shape[0]
    shared = channels - inner
    state = shared // 2
    taps = conv_kernel.shape[0]
    hd = inner // heads
    HL = heads // g.TP
    HW = HL * hd
    CW = HW + shared
    own_len = tokens.shape[1]
    width = tokens.shape[2]
    own_d = in_weight.shape[0]
    T = own_len * g.W
    TE = T + HALO
    nb = T // BLOCK
    NB = 2 * nb
    G = HW // LANES
    KW = HW + shared + 128
    j = g.j
    other_j = g.w * 2 + 1 - g.c

    w_t = in_weight.T
    n_rest = KW - HW
    rest = jnp.pad(w_t[2 * inner :], ((0, KW - CW - heads), (0, 0)))

    def with_rest(jj):
        return jnp.concatenate([lax.dynamic_slice_in_dim(w_t, inner + HW * jj, HW, 0), rest], axis=0)

    far = g.flip_core(with_rest(other_j))
    half_packed = assemble(
        [
            (w_t, (inner + HW * j, 0), (HW, own_d), (0, g.c * own_d)),
            (rest, None, (n_rest, own_d), (HW, g.c * own_d)),
            (far, None, (KW, own_d), (0, (1 - g.c) * own_d)),
        ],
        (KW, 2 * own_d),
    )

    series = tokens[0].astype(f32)
    scale = lax.rsqrt(jnp.mean(series * series, axis=-1, keepdims=True) + epsilon)
    normed = g.own_first((series * scale * pre_gain[None, :]).astype(bf16))

    stages = Stages()
    at_n = stages.add(g.gather_task, normed, normed[own_len - HALO :])
    at_packed = stages.add(g.direct_task, half_packed, [9, 5], 1)
    in_weight, out_weight, cotangent = stages.launch([in_weight, out_weight, cotangent])
    w_t = in_weight.T
    cot_own = g.own_first(cotangent[0])
    near_gate = lax.dynamic_slice_in_dim(w_t, HW * j, HW, 0)
    far_gate = lax.dynamic_slice_in_dim(w_t, HW * other_j, HW, 0)
    near_out = lax.dynamic_slice_in_dim(out_weight, HW * j, HW, 1)
    far_out = lax.dynamic_slice_in_dim(out_weight, HW * other_j, HW, 1)
    at_seg = stages.add(g.one_task, [segments], g.flip_core)
    at_far = stages.add(g.one_task, [far_gate, far_out], g.flip_core)
    stages.settle([])
    stages.launch([])
    stages.settle([], leave=[at_n, at_packed])
    far_gate, far_out = at_far["got"]
    half_gate = assemble(
        [
            (near_gate, None, (HW, own_d), (0, g.c * own_d)),
            (far_gate, None, (HW, own_d), (0, (1 - g.c) * own_d)),
        ],
        (HW, 2 * own_d),
    )
    half_out = assemble(
        [
            (near_out, None, (own_d, HW), (g.c * own_d, 0)),
            (far_out, None, (own_d, HW), ((1 - g.c) * own_d, 0)),
        ],
        (2 * own_d, HW),
    )

    s_lo, s_hi = g.by_core(segments, at_seg["got"][0])
    seg_all = jnp.concatenate([s_lo, s_hi], axis=0)
    seg_pad = jnp.concatenate([jnp.full((2, HALO), -1, jnp.int32), seg_all], axis=1)
    seg_ext = lax.dynamic_slice_in_dim(seg_pad, g.z * T, T + HALO, 1)
    seg = seg_ext[:, HALO:]
    ends = [seg[:, (b + 1) * BLOCK - 1 : (b + 1) * BLOCK] for b in range(nb)]
    begins = [seg_ext[:, HALO - 1 + b * BLOCK : HALO + b * BLOCK] for b in range(nb)]
    block_end = jnp.concatenate(ends, axis=1)
    prior_end = jnp.concatenate(begins, axis=1)
    carry_flag = (prior_end == block_end).astype(f32)

    def across(cols):
        return jnp.concatenate([jnp.broadcast_to(v, (2, BLOCK)) for v in cols], axis=1)

    end_row, prior_row = across(ends), across(begins)
    flags = [(seg_ext[:, HALO - k : HALO - k + T] == seg) for k in range(1, taps)]
    flags += [seg == end_row, seg == prior_row, end_row == prior_row, seg, jnp.zeros_like(seg)]
    flags = jnp.stack([v.astype(f32) for v in flags], axis=1)

    def own_channels(a):
        x_part = lax.dynamic_slice_in_dim(a, HW * j, HW, a.ndim - 1)
        return jnp.concatenate([x_part, a[..., inner:]], axis=-1)

    def own_heads(a):
        return lax.dynamic_slice_in_dim(a, HL * j, HL, a.ndim - 1)

    kernel_own = own_channels(conv_kernel)
    bias_own = own_channels(conv_bias)[None, :]
    rate = jnp.exp(own_heads(decay_log))
    hp = jnp.stack([own_heads(step_bias), rate, own_heads(skip_gain)]).reshape(3, G, GH)
    hp = jnp.pad(hp.transpose(1, 0, 2), ((0, 0), (0, 5), (0, 0)))
    ids = HL * j + GH * lax.broadcasted_iota(jnp.int32, (G, 128, 128), 0)
    lane = lax.broadcasted_iota(jnp.int32, (G, 128, 128), 2)
    sel = (lax.broadcasted_iota(jnp.int32, (G, 128, 128), 1) == ids + lane) & (lane < GH)
    sel = sel.astype(bf16)
    gain_own = lax.dynamic_slice_in_dim(gate_gain, HW * j, HW, 0)[None, :]
    (marks,) = call(
        turn_body,
        (2,),
        [(flags, (1, 8, T), lambda s: (s, 0, 0))],
        [((2, T, 8), f32, (1, T, 8), lambda s: (s, 0, 0))],
        name="turn",
    )
    held = [half_gate, half_out, cot_own, marks, flags, kernel_own, bias_own, hp, sel, gain_own]
    held = stages.settle(held)
    half_gate, half_out, cot_own, marks, flags, kernel_own, bias_own, hp, sel, gain_own = held
    at_gate = stages.add(g.direct_task, half_gate, [1], 1)
    at_cot = stages.add(g.gather_task, cot_own, None)
    stages.launch([])
    stages.settle([], leave=[at_gate, at_cot])
    n_ext = at_n["all"].reshape(2 * TE, width)
    w_packed = at_packed["w"]
    packed = low_dot(n_ext, w_packed, NT).astype(bf16)
    (packed,) = stages.settle([packed], leave=[at_gate])
    (packed,) = stages.launch([packed])
    packed = packed.reshape(2, TE, KW)
    marks_b = marks.reshape(NB, BLOCK, 8)

    def seq_block(b):
        return lax.div(b, nb), lax.rem(b, nb)

    def late(c):
        return jnp.maximum(c - 1, 0)

    def shared_first(c):
        return jnp.where(c == 0, G, c - 1)

    dt_block = CW // 128
    x, bc, s_block, step, cum, row = call(
        partial(conv_kernel_body, nb),
        (2, G + 1),
        [
            (packed, (1, TE, LANES), lambda s, c: (s, 0, shared_first(c))),
            (packed, (1, TE, 128), lambda s, c: (s, 0, dt_block)),
            (sel, (1, 128, 128), lambda s, c: (late(c), 0, 0)),
            (hp, (1, 8, GH), lambda s, c: (late(c), 0, 0)),
            (marks, (1, T, 8), lambda s, c: (s, 0, 0)),
            (kernel_own, (taps, LANES), lambda s, c: (0, shared_first(c))),
            (bias_own, (1, LANES), lambda s, c: (0, shared_first(c))),
        ],
        [
            ((2 * T, HW), bf16, (T, LANES), lambda s, c: (s, late(c))),
            ((2 * T, shared), bf16, (T, shared), lambda s, c: (s, 0)),
            ((2, nb, state, HW), f32, (1, nb, state, LANES), lambda s, c: (s, 0, 0, late(c))),
            ((2, G, T, GH), f32, (1, 1, T, GH), lambda s, c: (s, late(c), 0, 0)),
            ((2, G, T, GH), f32, (1, 1, T, GH), lambda s, c: (s, late(c), 0, 0)),
            ((2, G, nb, GH, BLOCK), f32, (1, 1, nb, GH, BLOCK), lambda s, c: (s, late(c), 0, 0, 0)),
        ],
        [pltpu.VMEM((TE, LANES), f32), pltpu.VMEM((T, state), bf16)],
        flops=2 * T * HW * state * 20,
        name="convolve",
    )

    end = jnp.exp(row[..., BLOCK - 1]).transpose(0, 2, 1, 3).reshape(2, nb, HL)
    carry_b = end * carry_flag[:, :, None]

    def spread(a):
        return jnp.repeat(a, hd, axis=-1)

    carry_wide = spread(carry_b)[:, :, None, :]
    carry_range = jnp.prod(carry_b, axis=1)
    s_range = s_block[:, 0]
    for b in range(1, nb):
        s_range = s_block[:, b] + carry_wide[:, b] * s_range
    s_range, x, bc, cum, row, step = stages.settle([s_range, x, bc, cum, row, step])
    at_out = stages.add(g.direct_task, half_out, [1], 0)
    at_enter = stages.add(g.state_task, s_range, carry_range, spread, 1)
    x, bc, cum, row, step = stages.launch([x, bc, cum, row, step])

    def tile(a):
        return (a, (BLOCK, LANES), lambda b, k: (b, k))

    def whole(a):
        return (a, (BLOCK, a.shape[1]), lambda b, k: (b, 0))

    def small_tile(a):
        def at(b, k):
            s, m = seq_block(b)
            return s, k, m, 0

        return (a, (1, 1, BLOCK, GH), at)

    def row_tile(b, k):
        s, m = seq_block(b)
        return s, k, m, 0, 0

    def flag_tile(b, k):
        s, m = seq_block(b)
        return s, 0, m

    pair_flops = 2 * 2 * T * BLOCK * HW
    (y_local,) = call(
        intra_forward_body,
        (NB, G),
        [
            tile(x),
            whole(bc),
            small_tile(cum),
            (row, (1, 1, 1, GH, BLOCK), row_tile),
            small_tile(step),
            (marks_b, (1, BLOCK, 8), lambda b, k: (b, 0, 0)),
            (flags, (1, 8, BLOCK), flag_tile),
            (hp, (1, 8, GH), lambda b, k: (k, 0, 0)),
        ],
        [((2 * T, HW), bf16, (BLOCK, LANES), lambda b, k: (b, k))],
        [pltpu.VMEM((BLOCK, BLOCK), f32)] * 2,
        flops=pair_flops * 8,
        name="intra_forward",
    )
    w_gate = at_gate["w"]
    gate = low_dot(n_ext, w_gate, NT).astype(bf16)
    y_local, gate = stages.settle([y_local, gate])
    while "state" not in at_enter or "w" not in at_out or "all" not in at_cot:
        stages.launch([])
        stages.settle([])
    enter = [at_enter["state"]]
    for b in range(nb - 1):
        enter.append(s_block[:, b] + carry_wide[:, b] * enter[b])
    enter = jnp.stack(enter, axis=1).astype(bf16)
    w_out = at_out["w"]
    cot_all = at_cot["all"].reshape(2 * T, width)
    out_grad = low_dot(cot_all, w_out, NN).astype(bf16)
    gate = gate.reshape(2, TE, HW)

    def seq_tile(a):
        return (a, (T, LANES), lambda s, k: (s, k))

    def seq_small(a):
        return (a, (1, 1, T, GH), lambda s, k: (s, k, 0, 0))

    def seq_state(a):
        return (a, (1, nb, state, LANES), lambda s, k: (s, 0, 0, k))

    def seq_whole(a):
        return (a, (1,) + a.shape[1:], lambda s, k: (s, 0, 0))

    def lane_tile(a):
        return (a, (a.shape[0], LANES), lambda s, k: (0, k))

    bc_seq = (bc, (T, shared), lambda s, k: (s, 0))
    main_tile = (gate, (1, T, LANES), lambda s, k: (s, 0, k))
    mixed, sums = call(
        partial(join_body, nb),
        (2, G),
        [
            seq_tile(y_local),
            bc_seq,
            seq_state(enter),
            seq_small(cum),
            seq_whole(marks),
            main_tile,
            seq_tile(out_grad),
            lane_tile(gain_own),
        ],
        [
            ((2 * T, HW), bf16, (T, LANES), lambda s, k: (s, k)),
            ((2, 8, T), f32, (1, 8, T), lambda s, k: (s, 0, 0)),
        ],
        flops=pair_flops,
        name="join",
    )
    at_sums = stages.add(g.sum_tp_task, sums)
    while "sum" not in at_sums:
        stages.launch([])
        stages.settle([])

    def turn(spec):
        a, block, at = spec
        return (a, block, lambda k, s: at(s, k))

    normed_out, gate_grad, d_out, gain_grad, de_block = call(
        partial(gates_body, nb, inner),
        (G, 2),
        [
            turn(v)
            for v in [
                seq_tile(mixed),
                main_tile,
                seq_tile(out_grad),
                seq_whole(at_sums["sum"]),
                lane_tile(gain_own),
                bc_seq,
                seq_small(cum),
                seq_whole(marks),
            ]
        ],
        [
            ((2 * T, HW), bf16, (T, LANES), lambda k, s: (s, k)),
            ((2, TE, HW), bf16, (1, TE, LANES), lambda k, s: (s, 0, k)),
            ((2 * T, HW), bf16, (T, LANES), lambda k, s: (s, k)),
            ((1, HW), f32, (1, LANES), lambda k, s: (0, k)),
            ((2, nb, state, HW), f32, (1, nb, state, LANES), lambda k, s: (s, 0, 0, k)),
        ],
        flops=pair_flops,
        name="gates",
    )
    gate_grad = gate_grad.reshape(2 * TE, HW)

    def far_rows(f, n):
        return [f(i).astype(bf16) for i in range(1, n)]

    def out_part(i):
        return low_dot(g.cut(cot_all, 1, i, g.Y), normed_out, TN)

    def in_part(a, i):
        return low_dot(a, g.cut(n_ext, 1, i, g.Y), TN)

    d_range = de_block[:, nb - 1]
    for b in range(nb - 2, -1, -1):
        d_range = de_block[:, b] + carry_wide[:, b] * d_range
    at_leave = stages.add(g.state_task, d_range, carry_range, spread, -1)
    at_outs = stages.add(
        g.gradient_task, far_rows(out_part, g.Y), lambda: out_part(0), 0, (2, 1)
    )
    x, d_out, normed_out, gate_grad = stages.launch([x, d_out, normed_out, gate_grad])
    branch = low_dot(normed_out, w_out, NT).astype(bf16)
    at_branch = stages.add(g.scatter_task, branch.reshape(2, g.W, own_len, width), (1, 2))
    x, d_out = stages.launch([x, d_out])
    dxs, dec, dbc = call(
        intra_backward_body,
        (NB, G),
        [
            tile(x),
            whole(bc),
            tile(d_out),
            small_tile(cum),
            (row, (1, 1, 1, GH, BLOCK), row_tile),
            small_tile(step),
            (
                enter.reshape(NB, state, HW),
                (1, state, LANES),
                lambda b, k: (b, 0, k),
            ),
            (marks_b, (1, BLOCK, 8), lambda b, k: (b, 0, 0)),
            (flags, (1, 8, BLOCK), flag_tile),
        ],
        [
            ((2 * T, HW), bf16, (BLOCK, LANES), lambda b, k: (b, k)),
            ((2, G, T, GH), f32) + small_tile(cum)[1:],
            ((2 * T, shared), f32, (BLOCK, shared), lambda b, k: (b, 0)),
        ],
        [pltpu.VMEM((BLOCK, BLOCK), f32)] * 3 + [pltpu.VMEM((BLOCK, state), f32)],
        flops=pair_flops * 16,
        name="intra_backward",
    )
    gate_far = far_rows(lambda i: in_part(gate_grad, i), g.Y)
    dxs, gate_far = stages.settle([dxs, gate_far])
    at_gates = stages.add(
        g.gradient_task, gate_far, lambda: in_part(gate_grad, 0), 1, (2, 1)
    )
    while "state" not in at_leave:
        stages.launch([])
        stages.settle([])
    leave = [at_leave["state"]]
    for b in range(nb - 1, 0, -1):
        leave.insert(0, de_block[:, b] + carry_wide[:, b] * leave[0])
    leave = jnp.stack(leave, axis=1).astype(bf16)
    leave, dxs = stages.launch([leave, dxs])

    def held(s, k):
        return s, jnp.minimum(k, G - 1)

    def late_tile(a):
        return (a, (T, LANES), lambda s, k: held(s, k))

    def late_small(a):
        return (a, (1, 1, T, GH), lambda s, k: (*held(s, k), 0, 0))

    def late_state(a):
        return (a, (1, nb, state, LANES), lambda s, k: (s, 0, 0, jnp.minimum(k, G - 1)))

    x_back, dt_back, kg, sm = call(
        partial(finish_body, nb),
        (2, G + 1),
        [
            (packed, (1, TE, LANES), lambda s, k: (s, 0, k)),
            late_tile(x),
            late_tile(d_out),
            late_tile(dxs),
            bc_seq,
            (dbc, (T, shared), lambda s, k: (s, 0)),
            late_state(leave),
            late_state(enter),
            late_small(cum),
            late_small(step),
            late_small(dec),
            (packed, (1, TE, 128), lambda s, k: (s, 0, dt_block)),
            (sel, (1, 128, 128), lambda s, k: (jnp.minimum(k, G - 1), 0, 0)),
            (hp, (1, 8, GH), lambda s, k: (jnp.minimum(k, G - 1), 0, 0)),
            seq_whole(marks),
            lane_tile(kernel_own),
            lane_tile(bias_own),
        ],
        [
            ((2, TE, CW), bf16, (1, TE, LANES), lambda s, k: (s, 0, k)),
            ((2, TE, 128), bf16, (1, TE, 128), lambda s, k: (s, 0, 0)),
            ((2, 8, CW), f32, (1, 8, LANES), lambda s, k: (s, 0, k)),
            ((2, G, 8, GH), f32, (1, 1, 8, GH), lambda s, k: (*held(s, k), 0, 0)),
        ],
        [
            pltpu.VMEM((TE, LANES), f32),
            pltpu.VMEM((HALO + TE, LANES), f32),
            pltpu.VMEM((T, LANES), f32),
            pltpu.VMEM((T, state), f32),
        ],
        flops=pair_flops * 16,
        name="finish",
    )
    edge = jnp.concatenate([x_back[:, T:], dt_back[:, T:]], axis=-1).reshape(2 * HALO, KW)
    spill = low_dot(edge, w_packed, NN).astype(bf16).reshape(2, HALO, width)
    x_flat = x_back.reshape(2 * TE, CW)
    dt_flat = dt_back.reshape(2 * TE, 128)

    def x_part(i):
        return in_part(x_flat[:, :HW], i)

    x_far = far_rows(x_part, g.Y)
    x_far, spill, x_flat, dt_flat, kg, sm = stages.settle([x_far, spill, x_flat, dt_flat, kg, sm])
    at_x = stages.add(g.gradient_task, x_far, lambda: x_part(0), 1, (2, 1))
    at_spill = stages.add(g.one_task, [spill], lambda a: g.shift_z(a, -1))
    x_flat, dt_flat = stages.launch([x_flat, dt_flat])
    rest_back = jnp.concatenate([x_flat[:, HW:], dt_flat[:, :heads]], axis=1)
    rest = [in_part(rest_back, i) for i in range(g.Y)]
    (rest,) = stages.settle([rest], leave=[at_gates, at_x, at_branch])
    spill = at_spill["got"][0]
    spill, gate_grad, x_flat, dt_flat = stages.launch([spill, gate_grad, x_flat, dt_flat])

    NW = 512
    n_grad, pre_grad = call(
        input_grad_body,
        (2, width // NW),
        [
            (gate_grad, (TE, HW), lambda s, n: (s, 0)),
            (x_flat, (TE, CW), lambda s, n: (s, 0)),
            (dt_flat, (TE, 128), lambda s, n: (s, 0)),
            (w_gate, (HW, NW), lambda s, n: (0, n)),
            (w_packed, (CW, NW), lambda s, n: (0, n)),
            (w_packed, (128, NW), lambda s, n: (CW // 128, n)),
            (spill, (1, HALO, NW), lambda s, n: (s, 0, n)),
            (n_ext, (TE, NW), lambda s, n: (s, n)),
        ],
        [
            ((2, T, width), bf16, (1, T, NW), lambda s, n: (s, 0, n)),
            ((2, 8, width), f32, (1, 8, NW), lambda s, n: (s, 0, n)),
        ],
        flops=2 * 2 * TE * width * (2 * HW + 128),
        name="input_grad",
    )

    def lay(a, lines):
        flat = a.reshape(-1)
        return jnp.pad(flat, (0, lines * own_d - flat.shape[0])).reshape(lines, own_d)

    per = HW // own_d
    lines = inner // own_d
    pre_part = g.own_first_back(jnp.sum(pre_grad, axis=(0, 1))) / pre_gain
    kg = jnp.sum(kg, axis=0)[:5]
    sm = jnp.sum(sm, axis=0)[:, :3].transpose(1, 0, 2).reshape(3, HL)
    heads_all = lax.dynamic_update_slice(jnp.zeros((3, heads), f32), sm, (0, HL * j))
    wide_rows = jnp.concatenate([gain_grad, kg[:, :HW]], axis=0).reshape(6, per, own_d)
    wide_rows = lax.dynamic_update_slice(
        jnp.zeros((6, lines, own_d), f32), wide_rows, (0, per * j, 0)
    )
    shared_lines = -(-5 * shared // own_d)
    pre_lines = width // own_d
    small = jnp.concatenate(
        [
            wide_rows.reshape(6 * lines, own_d),
            lay(kg[:, HW:], shared_lines),
            lay(heads_all, 1),
            pre_part.reshape(pre_lines, own_d),
        ],
        axis=0,
    )
    n_rest = shared + heads
    small = jnp.pad(small, ((0, -(n_rest + small.shape[0]) % 128), (0, 0)))
    copies = jnp.concatenate([small] * 2, axis=1)
    rest = [jnp.concatenate([p, copies], axis=0) for p in rest]
    rest_far = [p.astype(bf16) for p in rest[1:]]
    n_grad, rest_far = stages.settle([n_grad, rest_far], leave=[at_gates, at_outs])
    at_rest = stages.add(g.gradient_task, rest_far, lambda: rest[0], 1, None)
    at_ngrad = stages.add(g.scatter_task, n_grad.reshape(2, g.W, own_len, width), (1, 2))
    stages.launch([])

    in_shape = (2 * inner + shared + heads, own_d)

    def moves_of(a, first, axis):
        n = a["done"][0].shape[axis] // 4
        moves = []
        for i, (d, e) in enumerate(a["from"]):
            source, target, sizes = [0, 0], [0, 0], [own_d, own_d]
            source[axis], sizes[axis] = i % 4 * n, n
            target[axis] = first + HW * ((g.w ^ d) * 2 + (g.c ^ e))
            moves.append((i // 4, tuple(source), tuple(sizes), tuple(target)))
        return moves

    in_buf, out_weight_gradient = None, None
    todo = [(at_gates, 0), (at_x, inner)]
    plan = iter(
        [
            ([at_x, at_outs, at_gates], []),
            ([at_x], [at_rest]),
            ([at_x, at_outs, at_ngrad], [at_rest]),
            ([at_x, at_outs, at_ngrad, at_gates], []),
        ]
    )
    while stages.tasks:
        leave_now, _ = next(plan, ([], []))
        stages.settle([], leave=leave_now)
        if not stages.tasks:
            break
        stages.launch([])
        if out_weight_gradient is None and "done" in at_outs:
            out_weight_gradient = place(
                at_outs["done"], moves_of(at_outs, 0, 1), (own_d, inner), None
            )
        for a, first in list(todo):
            if "done" in a:
                in_buf = place(a["done"], moves_of(a, first, 0), in_shape, in_buf)
                todo.remove((a, first))
    for a, first in todo:
        in_buf = place(a["done"], moves_of(a, first, 0), in_shape, in_buf)
    if out_weight_gradient is None:
        out_weight_gradient = place(at_outs["done"], moves_of(at_outs, 0, 1), (own_d, inner), None)
    rest_done = at_rest["done"]
    in_buf = place(
        [rest_done], [(0, (0, 0), (n_rest, own_d), (2 * inner, 0))], in_shape, in_buf
    )
    n_own = g.own_first_back(at_ngrad["sum"])
    lifted_n = n_own * pre_gain[None, :]
    token_gradient = (
        cotangent[0].astype(f32)
        + scale * lifted_n
        - series * scale**3 * jnp.mean(series * lifted_n, axis=-1, keepdims=True)
    )[None]
    block_output = (series + g.own_first_back(at_branch["sum"])).astype(bf16)[None]
    in_weight_gradient = in_buf.T

    small = rest_done[n_rest:].astype(f32)
    gain_total = small[:lines].reshape(-1)
    kb = small[lines : 6 * lines].reshape(5, inner)
    at = 6 * lines
    shared_kb = small[at : at + shared_lines].reshape(-1)[: 5 * shared].reshape(5, shared)
    kb = jnp.concatenate([kb, shared_kb], axis=1)
    kernel_total, bias_total = kb[:taps], kb[taps]
    at += shared_lines
    step_total, decay_total, skip_total = small[at, : 3 * heads].reshape(3, heads)
    pre_total = small[at + 1 : at + 1 + pre_lines].reshape(-1)
    return (
        block_output,
        token_gradient,
        in_weight_gradient,
        out_weight_gradient,
        pre_total,
        kernel_total,
        bias_total,
        step_total,
        decay_total,
        skip_total,
        gain_total,
    )


def solution(mesh):
    placed = (
        P("shard", "seq", None),
        P("shard", None),
        P("shard", None),
        P(),
        P(),
        P(),
        P(),
        P(),
        P(),
        P(),
        P("shard", None),
        P("shard", "seq", None),
    )
    results = (P("shard", "seq", None),) * 2 + (P("shard", None),) * 2 + (P(),) * 7
    return jax.shard_map(
        partial(body, Slice(mesh)),
        mesh=mesh,
        in_specs=placed,
        out_specs=results,
        check_vma=False,
    )
```

```python
from functools import partial

import jax
import jax.numpy as jnp
import numpy as np
from jax import lax
from jax.experimental import pallas as pl
from jax.experimental.pallas import tpu as pltpu
from jax.sharding import PartitionSpec as P

BLOCK = 256
HALO = 16
epsilon = 1e-05
highest = lax.Precision.HIGHEST
f32 = jnp.float32
bf16 = jnp.bfloat16
AXES = ("seq", "shard")


class Slice:
    def __init__(self, mesh):
        self.seq = mesh.shape["seq"]
        self.shard = mesh.shape["shard"]
        self.Y = self.shard // 2
        self.W = 4
        self.Z = self.seq // self.W
        self.TP = 2 * self.W

    def place(self):
        s, k = lax.axis_index("seq"), lax.axis_index("shard")
        self.z, self.w = s // self.W, s % self.W
        self.y, self.c = k // 2, k % 2
        self.j = self.w * 2 + self.c

    def move(self, a, target):
        pairs = []
        for z in range(self.Z):
            for w in range(self.W):
                for y in range(self.Y):
                    for c in range(2):
                        to = target(z, w, y, c)
                        if to is None or not 0 <= to[0] < self.Z:
                            continue
                        tz, tw, ty, tc = to
                        src = (z * self.W + w) * self.shard + y * 2 + c
                        dst = (tz * self.W + tw) * self.shard + (ty % self.Y) * 2 + tc
                        pairs.append((src, dst))
        return lax.ppermute(a, AXES, pairs)

    def flip(self, a, d, e=0):
        return self.move(a, lambda z, w, y, c: (z, w ^ d, y, c ^ e))

    def bit(self, d, e):
        return self.c if e else (self.w // d) % 2

    def flip_core(self, a):
        return self.flip(a, 0, 1)

    def shift_y(self, a, d):
        return self.move(a, lambda z, w, y, c: (z, w, y + d, c))

    def shift_z(self, a, d):
        return self.move(a, lambda z, w, y, c: (z + d, w, y, c))

    def by_core(self, own, other):
        first = self.c == 0
        return jnp.where(first, own, other), jnp.where(first, other, own)

    def own_first(self, a):
        width = a.shape[-1] // self.Y
        parts = [
            lax.dynamic_slice_in_dim(a, ((self.y - i) % self.Y) * width, width, a.ndim - 1)
            for i in range(self.Y)
        ]
        return jnp.concatenate(parts, axis=-1)

    def own_first_back(self, a):
        width = a.shape[-1] // self.Y
        parts = [
            lax.dynamic_slice_in_dim(a, ((self.y - t) % self.Y) * width, width, a.ndim - 1)
            for t in range(self.Y)
        ]
        return jnp.concatenate(parts, axis=-1)

    def cut(self, a, axis, i, n):
        size = a.shape[axis] // n
        return lax.slice_in_dim(a, i * size, (i + 1) * size, axis=axis)


    def direct_task(self, half, shares, axis, out):
        n, m = half.shape
        edges = [n * sum(shares[:i]) // sum(shares) // 16 * 16 for i in range(len(shares) + 1)]
        pieces = [(half, None, (n, m), (0, 0))]
        for a, b in zip(edges[:-1], edges[1:]):
            sent = yield [half[a:b] if len(shares) > 1 else half]
            got = yield [self.shift_y(sent[0], d) for d in range(1, self.Y)]
            for d, r in enumerate(got):
                at = (a, (d + 1) * m) if axis else ((d + 1) * n + a, 0)
                pieces.append((r, None, (b - a, m), at))
        out["w"] = assemble(pieces, (n, m * self.Y) if axis else (n * self.Y, m))

    def gather_task(self, a, last, out):
        rows, F = a.shape
        half = rows // 2
        sent = yield [a] + ([] if last is None else [last])
        got = yield [self.flip(sent[0], 1), self.flip(sent[0], 2)] + [
            self.move(s, lambda z, w, y, c: (z + 1, t, y, c) if w == self.W - 1 else None)
            for s in sent[1:]
            for t in range(2)
        ]
        r1, r2 = got[:2]
        n = 0
        up, across = r1[:half], r2[half:]
        if last is not None:
            n = last.shape[0]
            edge = got[2] + got[3]
            up = jnp.concatenate([up, edge], axis=0)
        sent = yield [up, across, jnp.stack([a, r1, r2])]
        up, across, others = yield [
            self.flip(sent[0], 2),
            self.flip(sent[1], 1),
            self.flip_core(sent[2]),
        ]
        far = jnp.concatenate([up[:half], across], axis=0)
        if last is not None:
            edge = jnp.where(self.w < 2, edge, up[half:])
            far = jnp.concatenate([far, edge], axis=0)
        (far,) = yield [far]
        (far_other,) = yield [self.flip_core(far)]
        pieces = []
        for i, (d, mine) in enumerate(((0, a), (1, r1), (2, r2))):
            at = (self.w ^ d) * rows
            pieces.append((mine[None], None, (1, rows, F), (self.c, at, 0)))
            pieces.append((others, (i, 0, 0), (1, rows, F), (1 - self.c, at, 0)))
        length = self.W * rows
        for c, part in ((self.c, far[None]), (1 - self.c, far_other[None])):
            pieces.append((part, (0, 0, 0), (1, rows, F), (c, (self.w ^ 3) * rows, 0)))
            if n:
                pieces.append((part, (0, rows, 0), (1, n, F), (c, length, 0)))
        out["all"] = assemble(pieces, (2, length + n, F))

    def scatter_task(self, a, order, out):
        keep, send = self.by_core(a[0], a[1])
        sent = yield [send]
        got = yield [self.flip(sent[0], 0, 1)]
        total = (keep.astype(f32) + got[0].astype(f32)).astype(bf16)

        def part(d):
            return lax.dynamic_index_in_dim(total, self.w ^ d, 0, False)

        d1, d2 = order
        sent = yield [jnp.stack([part(d1), part(3)])]
        got = yield [self.flip(sent[0], d1)]
        mine = part(0).astype(f32) + got[0][0].astype(f32)
        pass_on = (part(d2).astype(f32) + got[0][1].astype(f32)).astype(bf16)
        sent = yield [pass_on]
        got = yield [self.flip(sent[0], d2)]
        out["sum"] = mine + got[0].astype(f32)

    def gradient_task(self, send, own_part, axis, order, out):
        half = self.Z // 2
        over_group = order is None
        halvings = [(0, 1), (2, 0), (1, 0)]
        sent = yield send
        got = yield [self.shift_y(p, -i - 1) for i, p in enumerate(sent)]
        acc = own_part()
        for r in got:
            acc = acc + r.astype(f32)
        q = acc.astype(bf16)
        if over_group:
            for d, e in halvings:
                n = q.shape[0] // 2
                b = self.bit(d, e)
                keep = lax.dynamic_slice_in_dim(q, b * n, n, 0)
                (send,) = yield [lax.dynamic_slice_in_dim(q, (1 - b) * n, n, 0)]
                (got,) = yield [self.flip(send, d, e)]
                q = (keep.astype(f32) + got.astype(f32)).astype(bf16)
        for step in range(half - 1):
            (q,) = yield [q]
            got = yield [
                self.move(
                    q,
                    lambda z, w, y, c: (z + 1, w, y, c)
                    if z == step
                    else ((z - 1, w, y, c) if z == self.Z - 1 - step else None),
                )
            ]
            q = (q.astype(f32) + got[0].astype(f32)).astype(bf16)
        (q,) = yield [q]
        got = yield [
            self.move(
                q,
                lambda z, w, y, c: (z + 1, w, y, c)
                if z == half - 1
                else ((z - 1, w, y, c) if z == half else None),
            )
        ]
        q = (q.astype(f32) + got[0].astype(f32)).astype(bf16)
        for step in range(half - 1):
            a, b = half - 1 - step, half + step
            (q,) = yield [q]
            got = yield [
                self.move(
                    q,
                    lambda z, w, y, c: (z - 1, w, y, c)
                    if z == a
                    else ((z + 1, w, y, c) if z == b else None),
                )
            ]
            q = jnp.where((self.z == a - 1) | (self.z == b + 1), got[0], q)
        if over_group:
            for d, e in reversed(halvings):
                (q,) = yield [q]
                if e:
                    keep, send = self.by_core(self.cut(q, 1, 0, 2), self.cut(q, 1, 1, 2))
                    (got,) = yield [self.flip(send, d, e)]
                    q = keep
                else:
                    (got,) = yield [self.flip(q, d, e)]
                low = self.bit(d, e) == 0
                q = jnp.concatenate([jnp.where(low, q, got), jnp.where(low, got, q)], axis=0)
            out["done"] = q
            return
        keep, send = self.by_core(self.cut(q, axis, 0, 2), self.cut(q, axis, 1, 2))
        (send,) = yield [send]
        got = yield [self.flip(send, 0, 1)]
        pair = jnp.concatenate([keep, got[0]], axis=1 - axis)
        (pair,) = yield [pair]
        got = yield [self.flip(pair, order[0])]
        quad = jnp.concatenate([pair, got[0]], axis=1 - axis)
        (quad,) = yield [quad]
        got = yield [self.flip(quad, order[1])]
        out["done"] = [quad, got[0]]
        a, b = order
        out["from"] = [(0, 0), (0, 1), (a, 0), (a, 1), (b, 0), (b, 1), (a ^ b, 0), (a ^ b, 1)]

    def state_task(self, cur, cc, spread, direction, out):
        d = 1
        while d < self.Z // 2:
            send = [cur.astype(bf16)] + ([cc] if 2 * d < self.Z // 2 else [])
            sent = yield send
            got = yield [self.shift_z(a, direction * d) for a in sent]
            cur = cur + spread(cc)[:, None, :] * got[0].astype(f32)
            if len(got) > 1:
                cc = cc * got[1]
            d *= 2
        sent = yield [cur.astype(bf16)]
        got = yield [self.shift_z(sent[0], direction)]
        out["state"] = got[0].astype(f32)

    def sum_tp_task(self, a, out):
        sent = yield [a]
        got = yield [self.flip_core(sent[0])]
        (a,) = yield [a + got[0]]
        got = yield [self.flip(a, d) for d in range(1, self.W)]
        for r in got:
            a = a + r
        out["sum"] = a

    def one_task(self, arrays, send, out):
        sent = yield arrays
        out["got"] = yield [send(a) for a in sent]


def fence(arrays):
    flat, tree = jax.tree.flatten(arrays)
    return jax.tree.unflatten(tree, lax.optimization_barrier(tuple(flat)))


class Stages:
    def __init__(self):
        self.tasks = []

    def add(self, task, *args):
        out = {}
        gen = task(*args, out)
        self.tasks.append([gen, next(gen), None, out])
        return out

    def settle(self, live, leave=()):
        flying = [t for t in self.tasks if t[2] is not None and not any(t[3] is o for o in leave)]
        got, live = fence(([t[2] for t in flying], live))
        for t, r in zip(flying, got):
            t[2] = None
            try:
                t[1] = t[0].send(r)
            except StopIteration:
                self.tasks.remove(t)
        return live

    def launch(self, live, hold=()):
        waiting = [t for t in self.tasks if t[2] is None and not any(t[3] is o for o in hold)]
        ready, live = fence(([t[1] for t in waiting], live))
        for t, a in zip(waiting, ready):
            t[2] = t[0].send(a)
        return live


def low_dot(a, b, dims):
    return lax.dot_general(a.astype(bf16), b.astype(bf16), dims, preferred_element_type=f32)


NT = (((1,), (1,)), ((), ()))
TN = (((0,), (0,)), ((), ()))
NN = (((1,), (0,)), ((), ()))
GH = 4
LANES = 256
FAR = -1e30
VMEM_LIMIT = 40 * 1024 * 1024


def bdot(a, b, dims):
    return lax.dot_general(a.astype(bf16), b.astype(bf16), dims, preferred_element_type=f32)


def fdot(a, b, dims):
    return lax.dot_general(a, b, dims, precision=highest, preferred_element_type=f32)


def wide(fac):
    low = lax.broadcasted_iota(jnp.int32, (fac.shape[0], 128), 1) < 64
    pairs = [jnp.where(low, fac[:, i : i + 1], fac[:, i + 1 : i + 2]) for i in (0, 2)]
    return jnp.concatenate(pairs, axis=1)


def head_sum(v):
    lane = lax.broadcasted_iota(jnp.int32, (LANES, 128), 0) // 64
    head = lax.broadcasted_iota(jnp.int32, (LANES, 128), 1)
    return bdot(v, (lane == head).astype(bf16), NN)[:, :GH]


def triangle(strict_lower=False, upper=False):
    r = lax.broadcasted_iota(jnp.int32, (BLOCK, BLOCK), 0)
    t = lax.broadcasted_iota(jnp.int32, (BLOCK, BLOCK), 1)
    keep = t >= r if upper else (t < r if strict_lower else t <= r)
    return keep.astype(f32)


def sigmoid(v):
    return 0.5 * jnp.tanh(0.5 * v) + 0.5


def turned(rows):
    pad = jnp.zeros((120, 128), f32)
    parts = []
    for i in range(rows.shape[1] // 128):
        square = jnp.concatenate([rows[:, i * 128 : (i + 1) * 128], pad], axis=0)
        parts.append(square.T[:, :8])
    return jnp.concatenate(parts, axis=0)


def turn_body(rows, out):
    out[0] = turned(rows[0])


def softplus(v):
    u = jnp.exp(-jnp.abs(v))
    w = 1.0 + u
    log1p = jnp.where(w == 1.0, u, jnp.log(w) * u / jnp.where(w == 1.0, 1.0, w - 1.0))
    return jnp.maximum(v, 0.0) + log1p


def call(kernel, grid, ins, outs, scratch=(), flops=0, name=None):
    arrays = [a for a, _, _ in ins]
    total = sum(a.size * a.dtype.itemsize for a in arrays)
    total += sum(int(np.prod(s)) * jnp.dtype(d).itemsize for s, d, _, _ in outs)
    return pl.pallas_call(
        kernel,
        grid=grid,
        in_specs=[pl.BlockSpec(b, m) for _, b, m in ins],
        out_specs=[pl.BlockSpec(b, m) for _, _, b, m in outs],
        out_shape=[jax.ShapeDtypeStruct(s, d) for s, d, _, _ in outs],
        scratch_shapes=list(scratch),
        compiler_params=pltpu.CompilerParams(vmem_limit_bytes=VMEM_LIMIT),
        cost_estimate=pl.CostEstimate(flops=0, bytes_accessed=1024, transcendentals=0),
        name=name,
    )(*arrays)


def conv_kernel_body(
    nb, pk, dt, sel, hp, marks, kern, bias, x_out, bc_out, s_out, step_out, cum_out, row_out, v_scr, keys_scr
):
    T = nb * BLOCK
    v_scr[:HALO, :] = pk[0, T:, :].astype(f32)
    v_scr[HALO:, :] = pk[0, :T, :].astype(f32)
    pre = bias[...] + kern[0:1, :] * v_scr[HALO : HALO + T, :]
    for k in range(1, 4):
        pre = pre + kern[k : k + 1, :] * (v_scr[HALO - k : HALO - k + T, :] * marks[0, :, k - 1 : k])
    act = pre * sigmoid(pre)
    chunk = pl.program_id(1)

    @pl.when(chunk == 0)
    def _():
        bc_out[...] = act.astype(bf16)
        keys_scr[...] = act[:, : keys_scr.shape[1]].astype(bf16)

    @pl.when(chunk > 0)
    def _():
        x_out[...] = act.astype(bf16)
        raw = bdot(dt[0, :T, :], sel[0], NN)[:, :GH] + hp[0, 0:1, :]
        step = softplus(raw)
        step_out[0, 0] = step
        tri = triangle()
        for b in range(nb):
            rows = slice(b * BLOCK, (b + 1) * BLOCK)
            st = step[rows]
            cum = fdot(tri, -hp[0, 1:2, :] * st, NN)
            cum_out[0, 0, rows, :] = cum
            padded = jnp.concatenate([cum, jnp.zeros((BLOCK, 128 - GH), f32)], axis=1)
            row_out[0, 0, b] = padded.T[:GH]
            tail = jnp.exp(cum[BLOCK - 1 :, :] - cum) * marks[0, rows, 3:4]
            xst = act[rows] * wide(st * tail)
            s_out[0, b] = bdot(keys_scr[rows, :], xst, TN)


def gaps_mask(seg_col, seg_row, transposed):
    r = lax.broadcasted_iota(jnp.int32, (BLOCK, BLOCK), 0)
    t = lax.broadcasted_iota(jnp.int32, (BLOCK, BLOCK), 1)
    order = t >= r if transposed else r >= t
    return jnp.where(order & (seg_col == seg_row), 0.0, FAR)


HALF = BLOCK // 2


def intra_forward_body(x, bc, cum, row, step, marks, flags, hp, y_out, gram, mask):
    @pl.when(pl.program_id(1) == 0)
    def _():
        n = bc.shape[1] // 2
        gram[...] = bdot(bc[:, n:], bc[:, :n], NT)
        mask[...] = gaps_mask(marks[0, :, 6:7], flags[0, 6:7, :], False)

    xf = x[...].astype(f32)
    xs = (xf * wide(step[0, 0])).astype(bf16)
    low = lax.broadcasted_iota(jnp.int32, (HALF, 128), 1) < 64
    c = cum[0, 0]
    for half in range(2):
        rows = slice(half * HALF, (half + 1) * HALF)
        reachable = (half + 1) * HALF
        g = gram[rows, :reachable]
        m = mask[rows, :reachable]
        parts = []
        for i in range(GH):
            d = c[rows, i : i + 1] - row[0, 0, 0, i : i + 1, :reachable] + m
            p = (jnp.exp(d) * g).astype(bf16)
            pair = i // 2 * 128
            parts.append(bdot(p, xs[:reachable, pair : pair + 128], NN))
        y = jnp.concatenate(
            [jnp.where(low, parts[0], parts[1]), jnp.where(low, parts[2], parts[3])], axis=1
        )
        y_out[rows, :] = (y + wide(hp[0, 2:3, :]) * xf[rows]).astype(bf16)


def reach_of(cum, marks):
    return jnp.exp(jnp.minimum(cum, 0.0)) * marks[:, 4:5]


def join_body(nb, y, bc, enter, cum, marks, gate, og, gain, mixed_out, sums_out):
    n = bc.shape[1] // 2
    ones = jnp.ones((16, LANES), bf16)
    first = lax.broadcasted_iota(jnp.int32, (8, BLOCK), 0) == 0
    for b in range(nb):
        rows = slice(b * BLOCK, (b + 1) * BLOCK)
        reach = wide(reach_of(cum[0, 0, rows, :], marks[0, rows, :]))
        state = bdot(bc[rows, n:], enter[0, b], NN) * reach
        mixed = (y[rows, :].astype(f32) + state).astype(bf16)
        mixed_out[rows, :] = mixed
        gv = gate[0, rows, :].astype(f32)
        gated = mixed.astype(f32) * (gv * sigmoid(gv))
        lifted = og[rows, :].astype(f32) * gain[...]
        ss = bdot(ones, gated * gated, NT)[:8]
        sg = bdot(ones, gated * lifted, NT)[:8]
        both = jnp.where(first, ss, sg)

        @pl.when(pl.program_id(1) == 0)
        def _(both=both, rows=rows):
            sums_out[0, :, rows] = both

        @pl.when(pl.program_id(1) > 0)
        def _(both=both, rows=rows):
            sums_out[0, :, rows] += both


def gates_body(
    nb, inner, mixed, gate, og, sums, gain, bc, cum, marks, no_out, gg_out, do_out, gain_out, de_out
):
    n = bc.shape[1] // 2
    T = nb * BLOCK
    total = turned(sums[0]) / inner
    part = None
    for b in range(nb):
        rows = slice(b * BLOCK, (b + 1) * BLOCK)
        gv = gate[0, rows, :].astype(f32)
        sg = sigmoid(gv)
        act = gv * sg
        mx = mixed[rows, :].astype(f32)
        ogv = og[rows, :].astype(f32)
        r = lax.rsqrt(total[rows, 0:1] + epsilon)
        gr = mx * act * r
        no_out[rows, :] = (gr * gain[...]).astype(bf16)
        p = jnp.sum(ogv * gr, axis=0, keepdims=True)
        part = p if part is None else part + p
        grad = r * (ogv * gain[...]) - gr * (r * r * total[rows, 1:2])
        d_out = (grad * act).astype(bf16)
        do_out[rows, :] = d_out
        gg_out[0, rows, :] = (grad * mx * (sg * (1.0 + gv * (1.0 - sg)))).astype(bf16)
        dr = d_out.astype(f32) * wide(reach_of(cum[0, 0, rows, :], marks[0, rows, :]))
        de_out[0, b] = bdot(bc[rows, n:], dr, TN)
    gg_out[0, T:, :] = jnp.zeros((HALO, LANES), bf16)

    @pl.when(pl.program_id(1) == 0)
    def _():
        gain_out[...] = part

    @pl.when(pl.program_id(1) > 0)
    def _():
        gain_out[...] += part


def input_grad_body(gg, xb, tb, wg, wx, wt, spill, out):
    total = bdot(gg[...], wg[...], NN) + bdot(xb[...], wx[...], NN) + bdot(tb[...], wt[...], NN)
    T = out.shape[1]
    out[0, : T - HALO, :] = total[: T - HALO].astype(bf16)
    out[0, T - HALO :, :] = (total[T - HALO : T] + spill[0].astype(f32)).astype(bf16)


def intra_backward_body(
    x, bc, do, cum, row, step, enter, marks, flags, dxs_out, dec_out, dbc_out, gram, mask, zt, dq
):
    n = bc.shape[1] // 2
    keys, queries = bc[:, :n], bc[:, n:]
    g_id = pl.program_id(1)

    @pl.when(g_id == 0)
    def _():
        gram[...] = bdot(keys, queries, NT)
        mask[...] = gaps_mask(marks[0, :, 6:7], flags[0, 6:7, :], True)
        zt[...] = jnp.zeros_like(zt)
        dq[...] = jnp.zeros_like(dq)

    low = lax.broadcasted_iota(jnp.int32, (BLOCK, 128), 1) < 64
    c = cum[0, 0]
    st = step[0, 0]
    row_sums = [None] * GH
    col_sums = []
    dxs = [[], []]
    for i in range(GH):
        pair = i // 2 * 128
        mine = low if i % 2 == 0 else ~low
        dop = do[:, pair : pair + 128]
        xm = jnp.where(mine, x[:, pair : pair + 128].astype(f32), 0.0).astype(bf16)
        cols = []
        for half in range(2):
            rows = slice(half * HALF, (half + 1) * HALF)
            after = slice(half * HALF, BLOCK)
            e = bdot(xm[rows], dop[after], NT)
            d = row[0, 0, 0, i : i + 1, after] - c[rows, i : i + 1] + mask[rows, after]
            decay = jnp.exp(d)
            le = decay * e * st[rows, i : i + 1]
            zt[rows, after] += le
            gr = gram[rows, after]
            m = le * gr
            total = jnp.sum(m, axis=0, keepdims=True)
            if half == 0:
                row_sums[i] = total
            else:
                row_sums[i] = row_sums[i] + jnp.concatenate([jnp.zeros((1, HALF), f32), total], axis=1)
            cols.append(jnp.sum(m, axis=1, keepdims=True))
            dxs[half].append(bdot((decay * gr).astype(bf16), dop[after], NN))
        col_sums.append(jnp.concatenate(cols, axis=0))
    for half in range(2):
        p = dxs[half]
        lo = low[:HALF]
        dxs_out[half * HALF : (half + 1) * HALF, :] = jnp.concatenate(
            [jnp.where(lo, p[0], p[1]), jnp.where(lo, p[2], p[3])], axis=1
        ).astype(bf16)
    dof = do[...].astype(f32)
    rw = wide(reach_of(c, marks[0]))
    from_state = bdot(queries, enter[0], NN) * rw
    came = head_sum(dof * from_state)
    upper = triangle(upper=True)
    rows4 = jnp.concatenate(row_sums + [jnp.zeros((16 - GH, BLOCK), f32)], axis=0)
    cols4 = jnp.concatenate(col_sums, axis=1)
    dec_out[0, 0] = fdot(upper, rows4, NT)[:, :GH] + fdot(upper, came - cols4, NN)
    dq[...] += bdot(dof * rw, enter[0], NT)

    @pl.when(g_id == pl.num_programs(1) - 1)
    def _():
        z = zt[...].astype(bf16)
        dbc_out[:, :n] = bdot(z, queries, NN)
        dbc_out[:, n:] = dq[...] + bdot(z, keys, TN)


def finish_body(
    nb, pk, x, do, dxl, bc, dbc, leave, enter, cum, step, dec, dt, sel, hp, marks, kern, bias,
    back_out, dt_out, kg_out, sm_out, v_scr, m_scr, grad, dk,
):
    T = nb * BLOCK
    n = bc.shape[1] // 2
    g_id = pl.program_id(1)
    last = pl.num_programs(1) - 1

    @pl.when(g_id == 0)
    def _():
        dk[...] = jnp.zeros_like(dk)
        dt_out[0] = jnp.zeros((T + HALO, 128), bf16)

    @pl.when(g_id < last)
    def _():
        rate = hp[0, 1:2, :]
        skip = wide(hp[0, 2:3, :])
        strict = triangle(strict_lower=True)
        sums = [0.0, 0.0, 0.0]
        for b in range(nb):
            rows = slice(b * BLOCK, (b + 1) * BLOCK)
            c = cum[0, 0, rows, :]
            st = step[0, 0, rows, :]
            end = c[BLOCK - 1 :, :]
            tail = wide(jnp.exp(end - c) * marks[0, rows, 3:4])
            stw = wide(st)
            lv = leave[0, b]
            kl = bdot(bc[rows, :n], lv, NN) * tail
            dxs = dxl[rows, :].astype(f32) + kl
            dof = do[rows, :].astype(f32)
            xf = x[rows, :].astype(f32)
            xs = xf * stw
            grad[rows, :] = skip * dof + stw * dxs
            out4 = head_sum(xs * kl)
            direct = head_sum(xf * dxs)
            sums[2] = sums[2] + jnp.sum(head_sum(dof * xf), axis=0, keepdims=True)
            dk[rows, :] += bdot(xs * tail, lv, NT)
            both = jnp.sum(enter[0, b].astype(f32) * lv.astype(f32), axis=0, keepdims=True)
            both = jnp.concatenate([both, jnp.zeros((15, LANES), f32)], axis=0)
            through = head_sum(both)[:1] * jnp.exp(end) * marks[0, b * BLOCK : b * BLOCK + 1, 5:6]
            decay = dec[0, 0, rows, :] + fdot(strict, out4, NN) + through
            sums[1] = sums[1] - rate * jnp.sum(st * decay, axis=0, keepdims=True)
            raw = bdot(dt[0, rows, :], sel[0], NN)[:, :GH] + hp[0, 0:1, :]
            rg = (direct - rate * decay) * sigmoid(raw)
            sums[0] = sums[0] + jnp.sum(rg, axis=0, keepdims=True)
            padded = jnp.concatenate([rg, jnp.zeros((BLOCK, 128 - GH), f32)], axis=1)
            spot = bdot(padded, sel[0], NT)
            dt_out[0, rows, :] = (dt_out[0, rows, :].astype(f32) + spot).astype(bf16)
        sm_out[0, 0] = jnp.concatenate(sums + [jnp.zeros((5, GH), f32)], axis=0)

    @pl.when(g_id == last)
    def _():
        grad[...] = jnp.concatenate([dbc[:, :n] + dk[...], dbc[:, n:]], axis=1)

    v_scr[:HALO, :] = pk[0, T:, :].astype(f32)
    v_scr[HALO:, :] = pk[0, :T, :].astype(f32)
    pre = bias[...] + kern[0:1, :] * v_scr[HALO : HALO + T, :]
    for k in range(1, 4):
        pre = pre + kern[k : k + 1, :] * (v_scr[HALO - k : HALO - k + T, :] * marks[0, :, k - 1 : k])
    sg = sigmoid(pre)
    cg = grad[...] * (sg * (1.0 + pre * (1.0 - sg)))
    m_scr[:HALO, :] = jnp.zeros((HALO, LANES), f32)
    m_scr[HALO + T :, :] = jnp.zeros((HALO, LANES), f32)
    kgs = []
    back = None
    for k in range(4):
        m = cg if k == 0 else cg * marks[0, :, k - 1 : k]
        kgs.append(jnp.sum(m * v_scr[HALO - k : HALO - k + T, :], axis=0, keepdims=True))
        m_scr[HALO : HALO + T, :] = m
        part = kern[k : k + 1, :] * m_scr[k : k + T + HALO, :]
        back = part if back is None else back + part
    kgs.append(jnp.sum(cg, axis=0, keepdims=True))
    kg_out[0] = jnp.concatenate(kgs + [jnp.zeros((3, LANES), f32)], axis=0)
    back = back.astype(bf16)
    back_out[0, :T, :] = back[HALO:]
    back_out[0, T:, :] = back[:HALO]

def offsets(index, starts, sizes, steps):
    window = []
    for s, n, step in zip(starts, sizes, steps):
        if not isinstance(s, int):
            s = pl.multiple_of(index[s[0]], step)
        window.append(pl.ds(s, n))
    return tuple(window)


def tabled(moves):
    table = []

    def entry(v):
        if isinstance(v, (int, np.integer)):
            return int(v)
        table.append(jnp.asarray(v, jnp.int32))
        return (len(table) - 1,)

    moves = [tuple(tuple(entry(v) for v in part) for part in m) for m in moves]
    table = table or [jnp.zeros((), jnp.int32)]
    return moves, jnp.stack(table)


def assemble(pieces, shape):
    arrays = [p[0] for p in pieces]
    zero = (0,) * len(shape)
    moves, table = tabled([(zero if s is None else s, at) for _, s, _, at in pieces])
    steps = (1,) * (len(shape) - 2) + (16, 128)

    n = len(arrays)

    def kernel(index, *refs):
        out, held, sems = refs[n], refs[n + 1 : -1], refs[-1]
        loads, stores = [], []
        for i, (source, _) in enumerate(moves):
            window = offsets(index, source, pieces[i][2], steps)
            loads.append(pltpu.make_async_copy(refs[i].at[window], held[i], sems.at[0, i]))
            loads[-1].start()
        for i, (_, target) in enumerate(moves):
            loads[i].wait()
            window = offsets(index, target, pieces[i][2], steps)
            stores.append(pltpu.make_async_copy(held[i], out.at[window], sems.at[1, i]))
            stores[-1].start()
        for c in stores:
            c.wait()

    size = 4 * int(np.prod(shape))
    return pl.pallas_call(
        kernel,
        in_specs=[pl.BlockSpec(memory_space=pltpu.SMEM)]
        + [pl.BlockSpec(memory_space=pltpu.HBM)] * len(arrays),
        out_specs=pl.BlockSpec(memory_space=pl.ANY),
        out_shape=jax.ShapeDtypeStruct(shape, arrays[0].dtype),
        scratch_shapes=[pltpu.VMEM(p[2], p[0].dtype) for p in pieces]
        + [pltpu.SemaphoreType.DMA((2, n))],
        compiler_params=pltpu.CompilerParams(vmem_limit_bytes=VMEM_LIMIT),
        cost_estimate=pl.CostEstimate(flops=0, bytes_accessed=size, transcendentals=0),
        name="assemble",
    )(table, *arrays)


def place(pieces, moves, shape, buf):
    spots, table = tabled([(s, at) for _, s, _, at in moves])
    n = len(pieces)

    def kernel(index, *refs):
        out, wide_refs, sems = refs[-n - 2], refs[-n - 1 : -1], refs[-1]
        copies = []
        for i in range(n):
            wide_refs[i][...] = refs[i][...].astype(f32)
            for k, (source, target) in enumerate(spots):
                if moves[k][0] != i:
                    continue
                sizes = moves[k][2]
                copies.append(
                    pltpu.make_async_copy(
                        wide_refs[i].at[offsets(index, source, sizes, (8, 128))],
                        out.at[offsets(index, target, sizes, (8, 128))],
                        sems.at[k],
                    )
                )
                copies[-1].start()
        for c in copies:
            c.wait()

    size = sum(6 * p.size for p in pieces)
    extra = [] if buf is None else [buf]
    return pl.pallas_call(
        kernel,
        in_specs=[pl.BlockSpec(memory_space=pltpu.SMEM)]
        + [pl.BlockSpec(memory_space=pltpu.VMEM)] * n
        + [pl.BlockSpec(memory_space=pl.ANY)] * len(extra),
        out_specs=pl.BlockSpec(memory_space=pl.ANY),
        out_shape=jax.ShapeDtypeStruct(shape, f32),
        scratch_shapes=[pltpu.VMEM(p.shape, f32) for p in pieces]
        + [pltpu.SemaphoreType.DMA((len(moves),))],
        input_output_aliases={} if buf is None else {1 + n: 0},
        compiler_params=pltpu.CompilerParams(vmem_limit_bytes=VMEM_LIMIT),
        cost_estimate=pl.CostEstimate(flops=0, bytes_accessed=size, transcendentals=0),
        name="place",
    )(table, *pieces, *extra)


def body(
    g,
    tokens,
    in_weight,
    out_weight,
    pre_gain,
    conv_kernel,
    conv_bias,
    step_bias,
    decay_log,
    skip_gain,
    gate_gain,
    segments,
    cotangent,
):
    g.place()
    heads = step_bias.shape[0]
    inner = gate_gain.shape[0]
    channels = conv_bias.shape[0]
    shared = channels - inner
    state = shared // 2
    taps = conv_kernel.shape[0]
    hd = inner // heads
    HL = heads // g.TP
    HW = HL * hd
    CW = HW + shared
    own_len = tokens.shape[1]
    width = tokens.shape[2]
    own_d = in_weight.shape[0]
    T = own_len * g.W
    TE = T + HALO
    nb = T // BLOCK
    NB = 2 * nb
    G = HW // LANES
    KW = HW + shared + 128
    j = g.j
    other_j = g.w * 2 + 1 - g.c

    w_t = in_weight.T
    n_rest = KW - HW
    rest = jnp.pad(w_t[2 * inner :], ((0, KW - CW - heads), (0, 0)))

    def with_rest(jj):
        return jnp.concatenate([lax.dynamic_slice_in_dim(w_t, inner + HW * jj, HW, 0), rest], axis=0)

    far = g.flip_core(with_rest(other_j))
    half_packed = assemble(
        [
            (w_t, (inner + HW * j, 0), (HW, own_d), (0, g.c * own_d)),
            (rest, None, (n_rest, own_d), (HW, g.c * own_d)),
            (far, None, (KW, own_d), (0, (1 - g.c) * own_d)),
        ],
        (KW, 2 * own_d),
    )

    series = tokens[0].astype(f32)
    scale = lax.rsqrt(jnp.mean(series * series, axis=-1, keepdims=True) + epsilon)
    normed = g.own_first((series * scale * pre_gain[None, :]).astype(bf16))

    stages = Stages()
    at_n = stages.add(g.gather_task, normed, normed[own_len - HALO :])
    at_packed = stages.add(g.direct_task, half_packed, [9, 5], 1)
    in_weight, out_weight, cotangent = stages.launch([in_weight, out_weight, cotangent])
    w_t = in_weight.T
    cot_own = g.own_first(cotangent[0])
    near_gate = lax.dynamic_slice_in_dim(w_t, HW * j, HW, 0)
    far_gate = lax.dynamic_slice_in_dim(w_t, HW * other_j, HW, 0)
    near_out = lax.dynamic_slice_in_dim(out_weight, HW * j, HW, 1)
    far_out = lax.dynamic_slice_in_dim(out_weight, HW * other_j, HW, 1)
    at_seg = stages.add(g.one_task, [segments], g.flip_core)
    at_far = stages.add(g.one_task, [far_gate, far_out], g.flip_core)
    stages.settle([])
    stages.launch([])
    stages.settle([], leave=[at_n, at_packed])
    far_gate, far_out = at_far["got"]
    half_gate = assemble(
        [
            (near_gate, None, (HW, own_d), (0, g.c * own_d)),
            (far_gate, None, (HW, own_d), (0, (1 - g.c) * own_d)),
        ],
        (HW, 2 * own_d),
    )
    half_out = assemble(
        [
            (near_out, None, (own_d, HW), (g.c * own_d, 0)),
            (far_out, None, (own_d, HW), ((1 - g.c) * own_d, 0)),
        ],
        (2 * own_d, HW),
    )

    s_lo, s_hi = g.by_core(segments, at_seg["got"][0])
    seg_all = jnp.concatenate([s_lo, s_hi], axis=0)
    seg_pad = jnp.concatenate([jnp.full((2, HALO), -1, jnp.int32), seg_all], axis=1)
    seg_ext = lax.dynamic_slice_in_dim(seg_pad, g.z * T, T + HALO, 1)
    seg = seg_ext[:, HALO:]
    ends = [seg[:, (b + 1) * BLOCK - 1 : (b + 1) * BLOCK] for b in range(nb)]
    begins = [seg_ext[:, HALO - 1 + b * BLOCK : HALO + b * BLOCK] for b in range(nb)]
    block_end = jnp.concatenate(ends, axis=1)
    prior_end = jnp.concatenate(begins, axis=1)
    carry_flag = (prior_end == block_end).astype(f32)

    def across(cols):
        return jnp.concatenate([jnp.broadcast_to(v, (2, BLOCK)) for v in cols], axis=1)

    end_row, prior_row = across(ends), across(begins)
    flags = [(seg_ext[:, HALO - k : HALO - k + T] == seg) for k in range(1, taps)]
    flags += [seg == end_row, seg == prior_row, end_row == prior_row, seg, jnp.zeros_like(seg)]
    flags = jnp.stack([v.astype(f32) for v in flags], axis=1)

    def own_channels(a):
        x_part = lax.dynamic_slice_in_dim(a, HW * j, HW, a.ndim - 1)
        return jnp.concatenate([x_part, a[..., inner:]], axis=-1)

    def own_heads(a):
        return lax.dynamic_slice_in_dim(a, HL * j, HL, a.ndim - 1)

    kernel_own = own_channels(conv_kernel)
    bias_own = own_channels(conv_bias)[None, :]
    rate = jnp.exp(own_heads(decay_log))
    hp = jnp.stack([own_heads(step_bias), rate, own_heads(skip_gain)]).reshape(3, G, GH)
    hp = jnp.pad(hp.transpose(1, 0, 2), ((0, 0), (0, 5), (0, 0)))
    ids = HL * j + GH * lax.broadcasted_iota(jnp.int32, (G, 128, 128), 0)
    lane = lax.broadcasted_iota(jnp.int32, (G, 128, 128), 2)
    sel = (lax.broadcasted_iota(jnp.int32, (G, 128, 128), 1) == ids + lane) & (lane < GH)
    sel = sel.astype(bf16)
    gain_own = lax.dynamic_slice_in_dim(gate_gain, HW * j, HW, 0)[None, :]
    (marks,) = call(
        turn_body,
        (2,),
        [(flags, (1, 8, T), lambda s: (s, 0, 0))],
        [((2, T, 8), f32, (1, T, 8), lambda s: (s, 0, 0))],
        name="turn",
    )
    held = [half_gate, half_out, cot_own, marks, flags, kernel_own, bias_own, hp, sel, gain_own]
    held = stages.settle(held)
    half_gate, half_out, cot_own, marks, flags, kernel_own, bias_own, hp, sel, gain_own = held
    at_gate = stages.add(g.direct_task, half_gate, [1], 1)
    at_cot = stages.add(g.gather_task, cot_own, None)
    stages.launch([])
    stages.settle([], leave=[at_gate, at_cot])
    n_ext = at_n["all"].reshape(2 * TE, width)
    w_packed = at_packed["w"]
    packed = low_dot(n_ext, w_packed, NT).astype(bf16)
    (packed,) = stages.settle([packed], leave=[at_gate])
    (packed,) = stages.launch([packed])
    packed = packed.reshape(2, TE, KW)
    marks_b = marks.reshape(NB, BLOCK, 8)

    def seq_block(b):
        return lax.div(b, nb), lax.rem(b, nb)

    def late(c):
        return jnp.maximum(c - 1, 0)

    def shared_first(c):
        return jnp.where(c == 0, G, c - 1)

    dt_block = CW // 128
    x, bc, s_block, step, cum, row = call(
        partial(conv_kernel_body, nb),
        (2, G + 1),
        [
            (packed, (1, TE, LANES), lambda s, c: (s, 0, shared_first(c))),
            (packed, (1, TE, 128), lambda s, c: (s, 0, dt_block)),
            (sel, (1, 128, 128), lambda s, c: (late(c), 0, 0)),
            (hp, (1, 8, GH), lambda s, c: (late(c), 0, 0)),
            (marks, (1, T, 8), lambda s, c: (s, 0, 0)),
            (kernel_own, (taps, LANES), lambda s, c: (0, shared_first(c))),
            (bias_own, (1, LANES), lambda s, c: (0, shared_first(c))),
        ],
        [
            ((2 * T, HW), bf16, (T, LANES), lambda s, c: (s, late(c))),
            ((2 * T, shared), bf16, (T, shared), lambda s, c: (s, 0)),
            ((2, nb, state, HW), f32, (1, nb, state, LANES), lambda s, c: (s, 0, 0, late(c))),
            ((2, G, T, GH), f32, (1, 1, T, GH), lambda s, c: (s, late(c), 0, 0)),
            ((2, G, T, GH), f32, (1, 1, T, GH), lambda s, c: (s, late(c), 0, 0)),
            ((2, G, nb, GH, BLOCK), f32, (1, 1, nb, GH, BLOCK), lambda s, c: (s, late(c), 0, 0, 0)),
        ],
        [pltpu.VMEM((TE, LANES), f32), pltpu.VMEM((T, state), bf16)],
        flops=2 * T * HW * state * 20,
        name="convolve",
    )

    end = jnp.exp(row[..., BLOCK - 1]).transpose(0, 2, 1, 3).reshape(2, nb, HL)
    carry_b = end * carry_flag[:, :, None]

    def spread(a):
        return jnp.repeat(a, hd, axis=-1)

    carry_wide = spread(carry_b)[:, :, None, :]
    carry_range = jnp.prod(carry_b, axis=1)
    s_range = s_block[:, 0]
    for b in range(1, nb):
        s_range = s_block[:, b] + carry_wide[:, b] * s_range
    s_range, x, bc, cum, row, step = stages.settle(
        [s_range, x, bc, cum, row, step], leave=[at_cot]
    )
    at_out = stages.add(g.direct_task, half_out, [1], 0)
    at_enter = stages.add(g.state_task, s_range, carry_range, spread, 1)
    x, bc, cum, row, step = stages.launch([x, bc, cum, row, step])

    def tile(a):
        return (a, (BLOCK, LANES), lambda b, k: (b, k))

    def whole(a):
        return (a, (BLOCK, a.shape[1]), lambda b, k: (b, 0))

    def small_tile(a):
        def at(b, k):
            s, m = seq_block(b)
            return s, k, m, 0

        return (a, (1, 1, BLOCK, GH), at)

    def row_tile(b, k):
        s, m = seq_block(b)
        return s, k, m, 0, 0

    def flag_tile(b, k):
        s, m = seq_block(b)
        return s, 0, m

    pair_flops = 2 * 2 * T * BLOCK * HW
    (y_local,) = call(
        intra_forward_body,
        (NB, G),
        [
            tile(x),
            whole(bc),
            small_tile(cum),
            (row, (1, 1, 1, GH, BLOCK), row_tile),
            small_tile(step),
            (marks_b, (1, BLOCK, 8), lambda b, k: (b, 0, 0)),
            (flags, (1, 8, BLOCK), flag_tile),
            (hp, (1, 8, GH), lambda b, k: (k, 0, 0)),
        ],
        [((2 * T, HW), bf16, (BLOCK, LANES), lambda b, k: (b, k))],
        [pltpu.VMEM((BLOCK, BLOCK), f32)] * 2,
        flops=pair_flops * 8,
        name="intra_forward",
    )
    w_gate = at_gate["w"]
    gate = low_dot(n_ext, w_gate, NT).astype(bf16)
    y_local, gate = stages.settle([y_local, gate])
    while "state" not in at_enter or "w" not in at_out or "all" not in at_cot:
        stages.launch([])
        stages.settle([])
    enter = [at_enter["state"]]
    for b in range(nb - 1):
        enter.append(s_block[:, b] + carry_wide[:, b] * enter[b])
    enter = jnp.stack(enter, axis=1).astype(bf16)
    w_out = at_out["w"]
    cot_all = at_cot["all"].reshape(2 * T, width)
    out_grad = low_dot(cot_all, w_out, NN).astype(bf16)
    gate = gate.reshape(2, TE, HW)

    def seq_tile(a):
        return (a, (T, LANES), lambda s, k: (s, k))

    def seq_small(a):
        return (a, (1, 1, T, GH), lambda s, k: (s, k, 0, 0))

    def seq_state(a):
        return (a, (1, nb, state, LANES), lambda s, k: (s, 0, 0, k))

    def seq_whole(a):
        return (a, (1,) + a.shape[1:], lambda s, k: (s, 0, 0))

    def lane_tile(a):
        return (a, (a.shape[0], LANES), lambda s, k: (0, k))

    bc_seq = (bc, (T, shared), lambda s, k: (s, 0))
    main_tile = (gate, (1, T, LANES), lambda s, k: (s, 0, k))
    mixed, sums = call(
        partial(join_body, nb),
        (2, G),
        [
            seq_tile(y_local),
            bc_seq,
            seq_state(enter),
            seq_small(cum),
            seq_whole(marks),
            main_tile,
            seq_tile(out_grad),
            lane_tile(gain_own),
        ],
        [
            ((2 * T, HW), bf16, (T, LANES), lambda s, k: (s, k)),
            ((2, 8, T), f32, (1, 8, T), lambda s, k: (s, 0, 0)),
        ],
        flops=pair_flops,
        name="join",
    )
    at_sums = stages.add(g.sum_tp_task, sums)
    while "sum" not in at_sums:
        stages.launch([])
        stages.settle([])

    def turn(spec):
        a, block, at = spec
        return (a, block, lambda k, s: at(s, k))

    normed_out, gate_grad, d_out, gain_grad, de_block = call(
        partial(gates_body, nb, inner),
        (G, 2),
        [
            turn(v)
            for v in [
                seq_tile(mixed),
                main_tile,
                seq_tile(out_grad),
                seq_whole(at_sums["sum"]),
                lane_tile(gain_own),
                bc_seq,
                seq_small(cum),
                seq_whole(marks),
            ]
        ],
        [
            ((2 * T, HW), bf16, (T, LANES), lambda k, s: (s, k)),
            ((2, TE, HW), bf16, (1, TE, LANES), lambda k, s: (s, 0, k)),
            ((2 * T, HW), bf16, (T, LANES), lambda k, s: (s, k)),
            ((1, HW), f32, (1, LANES), lambda k, s: (0, k)),
            ((2, nb, state, HW), f32, (1, nb, state, LANES), lambda k, s: (s, 0, 0, k)),
        ],
        flops=pair_flops,
        name="gates",
    )
    gate_grad = gate_grad.reshape(2 * TE, HW)

    def far_rows(f, n):
        return [f(i).astype(bf16) for i in range(1, n)]

    def out_part(i):
        return low_dot(g.cut(cot_all, 1, i, g.Y), normed_out, TN)

    def in_part(a, i):
        return low_dot(a, g.cut(n_ext, 1, i, g.Y), TN)

    d_range = de_block[:, nb - 1]
    for b in range(nb - 2, -1, -1):
        d_range = de_block[:, b] + carry_wide[:, b] * d_range
    at_leave = stages.add(g.state_task, d_range, carry_range, spread, -1)
    at_outs = stages.add(
        g.gradient_task, far_rows(out_part, g.Y), lambda: out_part(0), 0, (2, 1)
    )
    x, d_out, normed_out, gate_grad = stages.launch([x, d_out, normed_out, gate_grad])
    branch = low_dot(normed_out, w_out, NT).astype(bf16)
    at_branch = stages.add(g.scatter_task, branch.reshape(2, g.W, own_len, width), (1, 2))
    x, d_out = stages.launch([x, d_out])
    dxs, dec, dbc = call(
        intra_backward_body,
        (NB, G),
        [
            tile(x),
            whole(bc),
            tile(d_out),
            small_tile(cum),
            (row, (1, 1, 1, GH, BLOCK), row_tile),
            small_tile(step),
            (
                enter.reshape(NB, state, HW),
                (1, state, LANES),
                lambda b, k: (b, 0, k),
            ),
            (marks_b, (1, BLOCK, 8), lambda b, k: (b, 0, 0)),
            (flags, (1, 8, BLOCK), flag_tile),
        ],
        [
            ((2 * T, HW), bf16, (BLOCK, LANES), lambda b, k: (b, k)),
            ((2, G, T, GH), f32) + small_tile(cum)[1:],
            ((2 * T, shared), f32, (BLOCK, shared), lambda b, k: (b, 0)),
        ],
        [pltpu.VMEM((BLOCK, BLOCK), f32)] * 3 + [pltpu.VMEM((BLOCK, state), f32)],
        flops=pair_flops * 16,
        name="intra_backward",
    )
    gate_far = far_rows(lambda i: in_part(gate_grad, i), g.Y)
    dxs, gate_far = stages.settle([dxs, gate_far])
    kept = {}

    def gate_first():
        kept["gate"] = in_part(gate_grad, 0)
        return kept["gate"]

    at_gates = stages.add(g.gradient_task, gate_far, gate_first, 1, (2, 1))

    def gain_part(own, far, w):
        parts = []
        for i, p in enumerate([own] + far):
            parts.append(jnp.sum(p.astype(f32) * g.cut(w, 1, i, g.Y).astype(f32), axis=0))
        return jnp.concatenate(parts)

    while "state" not in at_leave:
        stages.launch([])
        stages.settle([])
    leave = [at_leave["state"]]
    for b in range(nb - 1, 0, -1):
        leave.insert(0, de_block[:, b] + carry_wide[:, b] * leave[0])
    leave = jnp.stack(leave, axis=1).astype(bf16)
    leave, dxs = stages.launch([leave, dxs])

    def held(s, k):
        return s, jnp.minimum(k, G - 1)

    def late_tile(a):
        return (a, (T, LANES), lambda s, k: held(s, k))

    def late_small(a):
        return (a, (1, 1, T, GH), lambda s, k: (*held(s, k), 0, 0))

    def late_state(a):
        return (a, (1, nb, state, LANES), lambda s, k: (s, 0, 0, jnp.minimum(k, G - 1)))

    x_back, dt_back, kg, sm = call(
        partial(finish_body, nb),
        (2, G + 1),
        [
            (packed, (1, TE, LANES), lambda s, k: (s, 0, k)),
            late_tile(x),
            late_tile(d_out),
            late_tile(dxs),
            bc_seq,
            (dbc, (T, shared), lambda s, k: (s, 0)),
            late_state(leave),
            late_state(enter),
            late_small(cum),
            late_small(step),
            late_small(dec),
            (packed, (1, TE, 128), lambda s, k: (s, 0, dt_block)),
            (sel, (1, 128, 128), lambda s, k: (jnp.minimum(k, G - 1), 0, 0)),
            (hp, (1, 8, GH), lambda s, k: (jnp.minimum(k, G - 1), 0, 0)),
            seq_whole(marks),
            lane_tile(kernel_own),
            lane_tile(bias_own),
        ],
        [
            ((2, TE, CW), bf16, (1, TE, LANES), lambda s, k: (s, 0, k)),
            ((2, TE, 128), bf16, (1, TE, 128), lambda s, k: (s, 0, 0)),
            ((2, 8, CW), f32, (1, 8, LANES), lambda s, k: (s, 0, k)),
            ((2, G, 8, GH), f32, (1, 1, 8, GH), lambda s, k: (*held(s, k), 0, 0)),
        ],
        [
            pltpu.VMEM((TE, LANES), f32),
            pltpu.VMEM((HALO + TE, LANES), f32),
            pltpu.VMEM((T, LANES), f32),
            pltpu.VMEM((T, state), f32),
        ],
        flops=pair_flops * 16,
        name="finish",
    )
    edge = jnp.concatenate([x_back[:, T:], dt_back[:, T:]], axis=-1).reshape(2 * HALO, KW)
    spill = low_dot(edge, w_packed, NN).astype(bf16).reshape(2, HALO, width)
    x_flat = x_back.reshape(2 * TE, CW)
    dt_flat = dt_back.reshape(2 * TE, 128)

    def x_part(i):
        return in_part(x_flat[:, :HW], i)

    x_far = far_rows(x_part, g.Y)
    x_far, spill, x_flat, dt_flat, kg, sm = stages.settle([x_far, spill, x_flat, dt_flat, kg, sm])
    at_x = stages.add(g.gradient_task, x_far, lambda: x_own, 1, (2, 1))
    at_spill = stages.add(g.one_task, [spill], lambda a: g.shift_z(a, -1))
    x_flat, dt_flat, kg, sm = stages.launch([x_flat, dt_flat, kg, sm])
    x_own = x_part(0)
    rest_back = jnp.concatenate([x_flat[:, HW:], dt_flat[:, :heads]], axis=1)
    rest = [in_part(rest_back, i) for i in range(g.Y)]
    gate_own = kept["gate"]

    def lay(a, lines):
        flat = a.reshape(-1)
        return jnp.pad(flat, (0, lines * own_d - flat.shape[0])).reshape(lines, own_d)

    per = HW // own_d
    lines = inner // own_d
    pre_part = (
        gain_part(gate_own, gate_far, w_gate)
        + gain_part(x_own, x_far, w_packed[:HW])
        + gain_part(rest[0], rest[1:], w_packed[HW : HW + shared + heads])
    )
    pre_part = g.own_first_back(pre_part) / pre_gain
    kg = jnp.sum(kg, axis=0)[:5]
    sm = jnp.sum(sm, axis=0)[:, :3].transpose(1, 0, 2).reshape(3, HL)
    heads_all = lax.dynamic_update_slice(jnp.zeros((3, heads), f32), sm, (0, HL * j))
    wide_rows = jnp.concatenate([gain_grad, kg[:, :HW]], axis=0).reshape(6, per, own_d)
    wide_rows = lax.dynamic_update_slice(
        jnp.zeros((6, lines, own_d), f32), wide_rows, (0, per * j, 0)
    )
    shared_lines = -(-5 * shared // own_d)
    pre_lines = width // own_d
    small = jnp.concatenate(
        [
            wide_rows.reshape(6 * lines, own_d),
            lay(kg[:, HW:], shared_lines),
            lay(heads_all, 1),
            pre_part.reshape(pre_lines, own_d),
        ],
        axis=0,
    )
    n_rest = shared + heads
    small = jnp.pad(small, ((0, -(n_rest + small.shape[0]) % 128), (0, 0)))
    copies = jnp.concatenate([small] * 2, axis=1)
    rest = [jnp.concatenate([p, copies], axis=0) for p in rest]
    rest_far = [p.astype(bf16) for p in rest[1:]]
    held = stages.settle([x_own, x_flat, dt_flat, rest_far, rest[0]], leave=[at_gates])
    x_own, x_flat, dt_flat, rest_far, rest_own = held
    at_rest = stages.add(g.gradient_task, rest_far, lambda: rest_own, 1, None)
    spill = at_spill["got"][0]
    spill, gate_grad, x_flat, dt_flat = stages.launch([spill, gate_grad, x_flat, dt_flat])

    NW = 512
    (n_grad,) = call(
        input_grad_body,
        (2, width // NW),
        [
            (gate_grad, (TE, HW), lambda s, n: (s, 0)),
            (x_flat, (TE, CW), lambda s, n: (s, 0)),
            (dt_flat, (TE, 128), lambda s, n: (s, 0)),
            (w_gate, (HW, NW), lambda s, n: (0, n)),
            (w_packed, (CW, NW), lambda s, n: (0, n)),
            (w_packed, (128, NW), lambda s, n: (CW // 128, n)),
            (spill, (1, HALO, NW), lambda s, n: (s, 0, n)),
        ],
        [
            ((2, T, width), bf16, (1, T, NW), lambda s, n: (s, 0, n)),
        ],
        flops=2 * 2 * TE * width * (2 * HW + 128),
        name="input_grad",
    )

    in_shape = (2 * inner + shared + heads, own_d)

    def moves_of(a, first, axis):
        n = a["done"][0].shape[axis] // 4
        moves = []
        for i, (d, e) in enumerate(a["from"]):
            source, target, sizes = [0, 0], [0, 0], [own_d, own_d]
            source[axis], sizes[axis] = i % 4 * n, n
            target[axis] = first + HW * ((g.w ^ d) * 2 + (g.c ^ e))
            moves.append((i // 4, tuple(source), tuple(sizes), tuple(target)))
        return moves

    (n_grad,) = stages.settle([n_grad], leave=[at_x])
    at_ngrad = stages.add(g.scatter_task, n_grad.reshape(2, g.W, own_len, width), (2, 1))
    if g.Z == 2:
        stages.launch([])
        stages.settle([], leave=[at_x, at_outs])
        stages.launch([], hold=[at_gates, at_ngrad])
        stages.settle([], leave=[at_x, at_outs])
        stages.launch([], hold=[at_ngrad])
    else:
        stages.launch([])
    stages.settle([])
    while "done" not in at_outs:
        stages.launch([])
        stages.settle([])
    stages.launch([])
    out_weight_gradient = place(at_outs["done"], moves_of(at_outs, 0, 1), (own_d, inner), None)
    block_output = (series + g.own_first_back(at_branch["sum"])).astype(bf16)[None]
    out_weight_gradient, block_output = stages.settle([out_weight_gradient, block_output])
    while "done" not in at_gates:
        stages.launch([])
        stages.settle([])
    stages.launch([])
    in_buf = place(at_gates["done"], moves_of(at_gates, 0, 0), in_shape, None)
    (in_buf,) = stages.settle([in_buf])
    while "sum" not in at_ngrad:
        stages.launch([])
        stages.settle([])
    stages.launch([])
    n_own = g.own_first_back(at_ngrad["sum"])
    lifted_n = n_own * pre_gain[None, :]
    token_gradient = (
        cotangent[0].astype(f32)
        + scale * lifted_n
        - series * scale**3 * jnp.mean(series * lifted_n, axis=-1, keepdims=True)
    )[None]
    token_gradient, in_buf = stages.settle([token_gradient, in_buf])
    while "done" not in at_x:
        stages.launch([])
        (in_buf,) = stages.settle([in_buf])
    if stages.tasks:
        stages.launch([])
    in_buf = place(at_x["done"], moves_of(at_x, inner, 0), in_shape, in_buf)
    while stages.tasks:
        (in_buf,) = stages.settle([in_buf])
        if stages.tasks:
            stages.launch([])
    rest_done = at_rest["done"]
    in_buf = place(
        [rest_done], [(0, (0, 0), (shared + heads, own_d), (2 * inner, 0))], in_shape, in_buf
    )
    in_weight_gradient = in_buf.T

    small = rest_done[n_rest:].astype(f32)
    gain_total = small[:lines].reshape(-1)
    kb = small[lines : 6 * lines].reshape(5, inner)
    at = 6 * lines
    shared_kb = small[at : at + shared_lines].reshape(-1)[: 5 * shared].reshape(5, shared)
    kb = jnp.concatenate([kb, shared_kb], axis=1)
    kernel_total, bias_total = kb[:taps], kb[taps]
    at += shared_lines
    step_total, decay_total, skip_total = small[at, : 3 * heads].reshape(3, heads)
    pre_total = small[at + 1 : at + 1 + pre_lines].reshape(-1)
    return (
        block_output,
        token_gradient,
        in_weight_gradient,
        out_weight_gradient,
        pre_total,
        kernel_total,
        bias_total,
        step_total,
        decay_total,
        skip_total,
        gain_total,
    )


def solution(mesh):
    placed = (
        P("shard", "seq", None),
        P("shard", None),
        P("shard", None),
        P(),
        P(),
        P(),
        P(),
        P(),
        P(),
        P(),
        P("shard", None),
        P("shard", "seq", None),
    )
    results = (P("shard", "seq", None),) * 2 + (P("shard", None),) * 2 + (P(),) * 7
    return jax.shard_map(
        partial(body, Slice(mesh)),
        mesh=mesh,
        in_specs=placed,
        out_specs=results,
        check_vma=False,
    )
```

```python
from functools import partial

import jax
import jax.numpy as jnp
import numpy as np
from jax import lax
from jax.experimental import pallas as pl
from jax.experimental.pallas import tpu as pltpu
from jax.sharding import PartitionSpec as P

BLOCK = 256
HALO = 16
epsilon = 1e-05
highest = lax.Precision.HIGHEST
f32 = jnp.float32
bf16 = jnp.bfloat16
AXES = ("seq", "shard")


class Slice:
    def __init__(self, mesh):
        self.seq = mesh.shape["seq"]
        self.shard = mesh.shape["shard"]
        self.Y = self.shard // 2
        self.W = 4
        self.Z = self.seq // self.W
        self.TP = 2 * self.W

    def place(self):
        s, k = lax.axis_index("seq"), lax.axis_index("shard")
        self.z, self.w = s // self.W, s % self.W
        self.y, self.c = k // 2, k % 2
        self.j = self.w * 2 + self.c

    def move(self, a, target):
        pairs = []
        for z in range(self.Z):
            for w in range(self.W):
                for y in range(self.Y):
                    for c in range(2):
                        to = target(z, w, y, c)
                        if to is None or not 0 <= to[0] < self.Z:
                            continue
                        tz, tw, ty, tc = to
                        src = (z * self.W + w) * self.shard + y * 2 + c
                        dst = (tz * self.W + tw) * self.shard + (ty % self.Y) * 2 + tc
                        pairs.append((src, dst))
        return lax.ppermute(a, AXES, pairs)

    def flip(self, a, d, e=0):
        return self.move(a, lambda z, w, y, c: (z, w ^ d, y, c ^ e))

    def bit(self, d, e):
        return self.c if e else (self.w // d) % 2

    def flip_core(self, a):
        return self.flip(a, 0, 1)

    def shift_y(self, a, d):
        return self.move(a, lambda z, w, y, c: (z, w, y + d, c))

    def shift_z(self, a, d):
        return self.move(a, lambda z, w, y, c: (z + d, w, y, c))

    def by_core(self, own, other):
        first = self.c == 0
        return jnp.where(first, own, other), jnp.where(first, other, own)

    def own_first(self, a):
        width = a.shape[-1] // self.Y
        parts = [
            lax.dynamic_slice_in_dim(a, ((self.y - i) % self.Y) * width, width, a.ndim - 1)
            for i in range(self.Y)
        ]
        return jnp.concatenate(parts, axis=-1)

    def own_first_back(self, a):
        width = a.shape[-1] // self.Y
        parts = [
            lax.dynamic_slice_in_dim(a, ((self.y - t) % self.Y) * width, width, a.ndim - 1)
            for t in range(self.Y)
        ]
        return jnp.concatenate(parts, axis=-1)

    def cut(self, a, axis, i, n):
        size = a.shape[axis] // n
        return lax.slice_in_dim(a, i * size, (i + 1) * size, axis=axis)


    def direct_task(self, half, shares, axis, out):
        n, m = half.shape
        edges = [n * sum(shares[:i]) // sum(shares) // 16 * 16 for i in range(len(shares) + 1)]
        pieces = [(half, None, (n, m), (0, 0))]
        for a, b in zip(edges[:-1], edges[1:]):
            sent = yield [half[a:b] if len(shares) > 1 else half]
            got = yield [self.shift_y(sent[0], d) for d in range(1, self.Y)]
            for d, r in enumerate(got):
                at = (a, (d + 1) * m) if axis else ((d + 1) * n + a, 0)
                pieces.append((r, None, (b - a, m), at))
        out["w"] = assemble(pieces, (n, m * self.Y) if axis else (n * self.Y, m))

    def gather_task(self, a, last, out):
        rows, F = a.shape
        half = rows // 2
        sent = yield [a] + ([] if last is None else [last])
        got = yield [self.flip(sent[0], 1), self.flip(sent[0], 2)] + [
            self.move(s, lambda z, w, y, c: (z + 1, t, y, c) if w == self.W - 1 else None)
            for s in sent[1:]
            for t in range(2)
        ]
        r1, r2 = got[:2]
        n = 0
        up, across = r1[:half], r2[half:]
        if last is not None:
            n = last.shape[0]
            edge = got[2] + got[3]
            up = jnp.concatenate([up, edge], axis=0)
        sent = yield [up, across, jnp.stack([a, r1, r2])]
        up, across, others = yield [
            self.flip(sent[0], 2),
            self.flip(sent[1], 1),
            self.flip_core(sent[2]),
        ]
        far = jnp.concatenate([up[:half], across], axis=0)
        if last is not None:
            edge = jnp.where(self.w < 2, edge, up[half:])
            far = jnp.concatenate([far, edge], axis=0)
        (far,) = yield [far]
        (far_other,) = yield [self.flip_core(far)]
        pieces = []
        for i, (d, mine) in enumerate(((0, a), (1, r1), (2, r2))):
            at = (self.w ^ d) * rows
            pieces.append((mine[None], None, (1, rows, F), (self.c, at, 0)))
            pieces.append((others, (i, 0, 0), (1, rows, F), (1 - self.c, at, 0)))
        length = self.W * rows
        for c, part in ((self.c, far[None]), (1 - self.c, far_other[None])):
            pieces.append((part, (0, 0, 0), (1, rows, F), (c, (self.w ^ 3) * rows, 0)))
            if n:
                pieces.append((part, (0, rows, 0), (1, n, F), (c, length, 0)))
        out["all"] = assemble(pieces, (2, length + n, F))

    def scatter_task(self, a, order, out):
        keep, send = self.by_core(a[0], a[1])
        sent = yield [send]
        got = yield [self.flip(sent[0], 0, 1)]
        total = (keep.astype(f32) + got[0].astype(f32)).astype(bf16)

        def part(d):
            return lax.dynamic_index_in_dim(total, self.w ^ d, 0, False)

        d1, d2 = order
        sent = yield [jnp.stack([part(d1), part(3)])]
        got = yield [self.flip(sent[0], d1)]
        mine = part(0).astype(f32) + got[0][0].astype(f32)
        pass_on = (part(d2).astype(f32) + got[0][1].astype(f32)).astype(bf16)
        sent = yield [pass_on]
        got = yield [self.flip(sent[0], d2)]
        out["sum"] = mine + got[0].astype(f32)

    def gradient_task(self, send, own_part, axis, order, out):
        half = self.Z // 2
        over_group = order is None
        halvings = [(0, 1), (2, 0), (1, 0)]
        sent = yield send
        got = yield [self.shift_y(p, -i - 1) for i, p in enumerate(sent)]
        acc = own_part()
        for r in got:
            acc = acc + r.astype(f32)
        q = acc.astype(bf16)
        if over_group:
            for d, e in halvings:
                n = q.shape[0] // 2
                b = self.bit(d, e)
                keep = lax.dynamic_slice_in_dim(q, b * n, n, 0)
                (send,) = yield [lax.dynamic_slice_in_dim(q, (1 - b) * n, n, 0)]
                (got,) = yield [self.flip(send, d, e)]
                q = (keep.astype(f32) + got.astype(f32)).astype(bf16)
        for step in range(half - 1):
            (q,) = yield [q]
            got = yield [
                self.move(
                    q,
                    lambda z, w, y, c: (z + 1, w, y, c)
                    if z == step
                    else ((z - 1, w, y, c) if z == self.Z - 1 - step else None),
                )
            ]
            q = (q.astype(f32) + got[0].astype(f32)).astype(bf16)
        (q,) = yield [q]
        got = yield [
            self.move(
                q,
                lambda z, w, y, c: (z + 1, w, y, c)
                if z == half - 1
                else ((z - 1, w, y, c) if z == half else None),
            )
        ]
        q = (q.astype(f32) + got[0].astype(f32)).astype(bf16)
        for step in range(half - 1):
            a, b = half - 1 - step, half + step
            (q,) = yield [q]
            got = yield [
                self.move(
                    q,
                    lambda z, w, y, c: (z - 1, w, y, c)
                    if z == a
                    else ((z + 1, w, y, c) if z == b else None),
                )
            ]
            q = jnp.where((self.z == a - 1) | (self.z == b + 1), got[0], q)
        if over_group:
            for d, e in reversed(halvings):
                (q,) = yield [q]
                if e:
                    keep, send = self.by_core(self.cut(q, 1, 0, 2), self.cut(q, 1, 1, 2))
                    (got,) = yield [self.flip(send, d, e)]
                    q = keep
                else:
                    (got,) = yield [self.flip(q, d, e)]
                low = self.bit(d, e) == 0
                q = jnp.concatenate([jnp.where(low, q, got), jnp.where(low, got, q)], axis=0)
            out["done"] = q
            return
        keep, send = self.by_core(self.cut(q, axis, 0, 2), self.cut(q, axis, 1, 2))
        (send,) = yield [send]
        got = yield [self.flip(send, 0, 1)]
        pair = jnp.concatenate([keep, got[0]], axis=1 - axis)
        (pair,) = yield [pair]
        got = yield [self.flip(pair, order[0])]
        quad = jnp.concatenate([pair, got[0]], axis=1 - axis)
        (quad,) = yield [quad]
        got = yield [self.flip(quad, order[1])]
        out["done"] = [quad, got[0]]
        a, b = order
        out["from"] = [(0, 0), (0, 1), (a, 0), (a, 1), (b, 0), (b, 1), (a ^ b, 0), (a ^ b, 1)]

    def state_task(self, cur, cc, spread, direction, out):
        d = 1
        while d < self.Z // 2:
            send = [cur.astype(bf16)] + ([cc] if 2 * d < self.Z // 2 else [])
            sent = yield send
            got = yield [self.shift_z(a, direction * d) for a in sent]
            cur = cur + spread(cc)[:, None, :] * got[0].astype(f32)
            if len(got) > 1:
                cc = cc * got[1]
            d *= 2
        sent = yield [cur.astype(bf16)]
        got = yield [self.shift_z(sent[0], direction)]
        out["state"] = got[0].astype(f32)

    def sum_tp_task(self, a, out):
        sent = yield [a]
        got = yield [self.flip_core(sent[0])]
        (a,) = yield [a + got[0]]
        got = yield [self.flip(a, d) for d in range(1, self.W)]
        for r in got:
            a = a + r
        out["sum"] = a

    def one_task(self, arrays, send, out):
        sent = yield arrays
        out["got"] = yield [send(a) for a in sent]


def fence(arrays):
    flat, tree = jax.tree.flatten(arrays)
    return jax.tree.unflatten(tree, lax.optimization_barrier(tuple(flat)))


class Stages:
    def __init__(self):
        self.tasks = []

    def add(self, task, *args):
        out = {}
        gen = task(*args, out)
        self.tasks.append([gen, next(gen), None, out])
        return out

    def settle(self, live, leave=()):
        flying = [t for t in self.tasks if t[2] is not None and not any(t[3] is o for o in leave)]
        got, live = fence(([t[2] for t in flying], live))
        for t, r in zip(flying, got):
            t[2] = None
            try:
                t[1] = t[0].send(r)
            except StopIteration:
                self.tasks.remove(t)
        return live

    def launch(self, live, hold=()):
        waiting = [t for t in self.tasks if t[2] is None and not any(t[3] is o for o in hold)]
        ready, live = fence(([t[1] for t in waiting], live))
        for t, a in zip(waiting, ready):
            t[2] = t[0].send(a)
        return live


def low_dot(a, b, dims):
    return lax.dot_general(a.astype(bf16), b.astype(bf16), dims, preferred_element_type=f32)


NT = (((1,), (1,)), ((), ()))
TN = (((0,), (0,)), ((), ()))
NN = (((1,), (0,)), ((), ()))
GH = 4
LANES = 256
FAR = -1e30
VMEM_LIMIT = 40 * 1024 * 1024


def bdot(a, b, dims):
    return lax.dot_general(a.astype(bf16), b.astype(bf16), dims, preferred_element_type=f32)


def fdot(a, b, dims):
    return lax.dot_general(a, b, dims, precision=highest, preferred_element_type=f32)


def wide(fac):
    low = lax.broadcasted_iota(jnp.int32, (fac.shape[0], 128), 1) < 64
    pairs = [jnp.where(low, fac[:, i : i + 1], fac[:, i + 1 : i + 2]) for i in (0, 2)]
    return jnp.concatenate(pairs, axis=1)


def head_sum(v):
    lane = lax.broadcasted_iota(jnp.int32, (LANES, 128), 0) // 64
    head = lax.broadcasted_iota(jnp.int32, (LANES, 128), 1)
    return bdot(v, (lane == head).astype(bf16), NN)[:, :GH]


def triangle(strict_lower=False, upper=False):
    r = lax.broadcasted_iota(jnp.int32, (BLOCK, BLOCK), 0)
    t = lax.broadcasted_iota(jnp.int32, (BLOCK, BLOCK), 1)
    keep = t >= r if upper else (t < r if strict_lower else t <= r)
    return keep.astype(f32)


def sigmoid(v):
    return 0.5 * jnp.tanh(0.5 * v) + 0.5


def turned(rows):
    pad = jnp.zeros((120, 128), f32)
    parts = []
    for i in range(rows.shape[1] // 128):
        square = jnp.concatenate([rows[:, i * 128 : (i + 1) * 128], pad], axis=0)
        parts.append(square.T[:, :8])
    return jnp.concatenate(parts, axis=0)


def turn_body(rows, out):
    out[0] = turned(rows[0])


def softplus(v):
    u = jnp.exp(-jnp.abs(v))
    w = 1.0 + u
    log1p = jnp.where(w == 1.0, u, jnp.log(w) * u / jnp.where(w == 1.0, 1.0, w - 1.0))
    return jnp.maximum(v, 0.0) + log1p


def call(kernel, grid, ins, outs, scratch=(), flops=0, name=None):
    arrays = [a for a, _, _ in ins]
    total = sum(a.size * a.dtype.itemsize for a in arrays)
    total += sum(int(np.prod(s)) * jnp.dtype(d).itemsize for s, d, _, _ in outs)
    return pl.pallas_call(
        kernel,
        grid=grid,
        in_specs=[
            pl.BlockSpec(memory_space=pltpu.SMEM) if b is None else pl.BlockSpec(b, m)
            for _, b, m in ins
        ],
        out_specs=[pl.BlockSpec(b, m) for _, _, b, m in outs],
        out_shape=[jax.ShapeDtypeStruct(s, d) for s, d, _, _ in outs],
        scratch_shapes=list(scratch),
        compiler_params=pltpu.CompilerParams(vmem_limit_bytes=VMEM_LIMIT),
        cost_estimate=pl.CostEstimate(flops=0, bytes_accessed=1024, transcendentals=0),
        name=name,
    )(*arrays)


def conv_kernel_body(
    nb, pk, dt, sel, hp, marks, kern, bias, x_out, bc_out, s_out, step_out, cum_out, row_out, v_scr, keys_scr
):
    T = nb * BLOCK
    v_scr[:HALO, :] = pk[0, T:, :].astype(f32)
    v_scr[HALO:, :] = pk[0, :T, :].astype(f32)
    pre = bias[...] + kern[0:1, :] * v_scr[HALO : HALO + T, :]
    for k in range(1, 4):
        pre = pre + kern[k : k + 1, :] * (v_scr[HALO - k : HALO - k + T, :] * marks[0, :, k - 1 : k])
    act = pre * sigmoid(pre)
    chunk = pl.program_id(1)

    @pl.when(chunk == 0)
    def _():
        bc_out[...] = act.astype(bf16)
        keys_scr[...] = act[:, : keys_scr.shape[1]].astype(bf16)

    @pl.when(chunk > 0)
    def _():
        x_out[...] = act.astype(bf16)
        raw = bdot(dt[0, :T, :], sel[0], NN)[:, :GH] + hp[0, 0:1, :]
        step = softplus(raw)
        step_out[0, 0] = step
        tri = triangle()
        for b in range(nb):
            rows = slice(b * BLOCK, (b + 1) * BLOCK)
            st = step[rows]
            cum = fdot(tri, -hp[0, 1:2, :] * st, NN)
            cum_out[0, 0, rows, :] = cum
            padded = jnp.concatenate([cum, jnp.zeros((BLOCK, 128 - GH), f32)], axis=1)
            row_out[0, 0, b] = padded.T[:GH]
            tail = jnp.exp(cum[BLOCK - 1 :, :] - cum) * marks[0, rows, 3:4]
            xst = act[rows] * wide(st * tail)
            s_out[0, b] = bdot(keys_scr[rows, :], xst, TN)


def gaps_mask(seg_col, seg_row, transposed):
    r = lax.broadcasted_iota(jnp.int32, (BLOCK, BLOCK), 0)
    t = lax.broadcasted_iota(jnp.int32, (BLOCK, BLOCK), 1)
    order = t >= r if transposed else r >= t
    return jnp.where(order & (seg_col == seg_row), 0.0, FAR)


HALF = BLOCK // 2


def intra_forward_body(x, bc, cum, row, step, marks, flags, hp, y_out, gram, mask):
    @pl.when(pl.program_id(1) == 0)
    def _():
        n = bc.shape[1] // 2
        gram[...] = bdot(bc[:, n:], bc[:, :n], NT)
        mask[...] = gaps_mask(marks[0, :, 6:7], flags[0, 6:7, :], False)

    xf = x[...].astype(f32)
    xs = (xf * wide(step[0, 0])).astype(bf16)
    low = lax.broadcasted_iota(jnp.int32, (HALF, 128), 1) < 64
    c = cum[0, 0]
    for half in range(2):
        rows = slice(half * HALF, (half + 1) * HALF)
        reachable = (half + 1) * HALF
        g = gram[rows, :reachable]
        m = mask[rows, :reachable]
        parts = []
        for i in range(GH):
            d = c[rows, i : i + 1] - row[0, 0, 0, i : i + 1, :reachable] + m
            p = (jnp.exp(d) * g).astype(bf16)
            pair = i // 2 * 128
            parts.append(bdot(p, xs[:reachable, pair : pair + 128], NN))
        y = jnp.concatenate(
            [jnp.where(low, parts[0], parts[1]), jnp.where(low, parts[2], parts[3])], axis=1
        )
        y_out[rows, :] = (y + wide(hp[0, 2:3, :]) * xf[rows]).astype(bf16)


def reach_of(cum, marks):
    return jnp.exp(jnp.minimum(cum, 0.0)) * marks[:, 4:5]


def join_body(nb, y, bc, enter, cum, marks, gate, og, gain, mixed_out, sums_out):
    n = bc.shape[1] // 2
    ones = jnp.ones((16, LANES), bf16)
    first = lax.broadcasted_iota(jnp.int32, (8, BLOCK), 0) == 0
    for b in range(nb):
        rows = slice(b * BLOCK, (b + 1) * BLOCK)
        reach = wide(reach_of(cum[0, 0, rows, :], marks[0, rows, :]))
        state = bdot(bc[rows, n:], enter[0, b], NN) * reach
        mixed = (y[rows, :].astype(f32) + state).astype(bf16)
        mixed_out[rows, :] = mixed
        gv = gate[0, rows, :].astype(f32)
        gated = mixed.astype(f32) * (gv * sigmoid(gv))
        lifted = og[rows, :].astype(f32) * gain[...]
        ss = bdot(ones, gated * gated, NT)[:8]
        sg = bdot(ones, gated * lifted, NT)[:8]
        both = jnp.where(first, ss, sg)

        @pl.when(pl.program_id(1) == 0)
        def _(both=both, rows=rows):
            sums_out[0, :, rows] = both

        @pl.when(pl.program_id(1) > 0)
        def _(both=both, rows=rows):
            sums_out[0, :, rows] += both


def gates_body(
    nb, inner, mixed, gate, og, sums, gain, bc, cum, marks, no_out, gg_out, do_out, gain_out, de_out
):
    n = bc.shape[1] // 2
    T = nb * BLOCK
    total = turned(sums[0]) / inner
    part = None
    for b in range(nb):
        rows = slice(b * BLOCK, (b + 1) * BLOCK)
        gv = gate[0, rows, :].astype(f32)
        sg = sigmoid(gv)
        act = gv * sg
        mx = mixed[rows, :].astype(f32)
        ogv = og[rows, :].astype(f32)
        r = lax.rsqrt(total[rows, 0:1] + epsilon)
        gr = mx * act * r
        no_out[rows, :] = (gr * gain[...]).astype(bf16)
        p = jnp.sum(ogv * gr, axis=0, keepdims=True)
        part = p if part is None else part + p
        grad = r * (ogv * gain[...]) - gr * (r * r * total[rows, 1:2])
        d_out = (grad * act).astype(bf16)
        do_out[rows, :] = d_out
        gg_out[0, rows, :] = (grad * mx * (sg * (1.0 + gv * (1.0 - sg)))).astype(bf16)
        dr = d_out.astype(f32) * wide(reach_of(cum[0, 0, rows, :], marks[0, rows, :]))
        de_out[0, b] = bdot(bc[rows, n:], dr, TN)
    gg_out[0, T:, :] = jnp.zeros((HALO, LANES), bf16)

    @pl.when(pl.program_id(1) == 0)
    def _():
        gain_out[...] = part

    @pl.when(pl.program_id(1) > 0)
    def _():
        gain_out[...] += part


def small_body(Y, HW, HL, heads, place_ref, *refs):
    pairs, (gain, kg, sm, pre_gain), out = refs[: 5 * Y], refs[5 * Y : -1], refs[-1]
    j, y = place_ref[0], place_ref[1]
    own_d = out.shape[1]
    per = HW // own_d
    lines = per * (heads // HL)
    shared = kg.shape[2] - HW
    out[...] = jnp.zeros_like(out)
    both = kg[0] + kg[1]
    for q in range(per):
        lanes = slice(q * own_d, (q + 1) * own_d)
        out[pl.ds(per * j + q, 1), :] = gain[:, lanes]
        for k in range(5):
            out[pl.ds((k + 1) * lines + per * j + q, 1), :] = both[k : k + 1, lanes]
    at = 6 * lines
    out[at : at + 5, :shared] = both[:5, HW:]
    lane = lax.broadcasted_iota(jnp.int32, (1, own_d), 1)
    row = jnp.zeros((1, own_d), f32)
    for k in range(3):
        for h in range(HL):
            value = sm[0, h // GH, k : k + 1, h % GH : h % GH + 1]
            value = value + sm[1, h // GH, k : k + 1, h % GH : h % GH + 1]
            row = jnp.where(lane == k * heads + HL * j + h, value, row)
    out[at + 5 : at + 6, :] = row
    for i in range(Y):
        wg, pg, wp, px, pr = pairs[5 * i : 5 * i + 5]
        n = pr.shape[0]
        total = jnp.sum(wg[...].astype(f32) * pg[...].astype(f32), axis=0, keepdims=True)
        total += jnp.sum(wp[:HW, :].astype(f32) * px[...].astype(f32), axis=0, keepdims=True)
        total += jnp.sum(wp[HW : HW + n, :].astype(f32) * pr[...].astype(f32), axis=0, keepdims=True)
        rows = total.shape[1] // own_d
        first = lax.rem(y - i + Y, Y) * rows
        for q in range(rows):
            part = total[:, q * own_d : (q + 1) * own_d]
            out[pl.ds(at + 6 + first + q, 1), :] = part / pre_gain[pl.ds(first + q, 1), :]


def input_grad_body(gg, xb, tb, wg, wx, wt, spill, out):
    total = bdot(gg[...], wg[...], NN) + bdot(xb[...], wx[...], NN) + bdot(tb[...], wt[...], NN)
    T = out.shape[1]
    out[0, : T - HALO, :] = total[: T - HALO].astype(bf16)
    out[0, T - HALO :, :] = (total[T - HALO : T] + spill[0].astype(f32)).astype(bf16)


def intra_backward_body(
    x, bc, do, cum, row, step, enter, marks, flags, dxs_out, dec_out, dbc_out, gram, mask, zt, dq
):
    n = bc.shape[1] // 2
    keys, queries = bc[:, :n], bc[:, n:]
    g_id = pl.program_id(1)

    @pl.when(g_id == 0)
    def _():
        gram[...] = bdot(keys, queries, NT)
        mask[...] = gaps_mask(marks[0, :, 6:7], flags[0, 6:7, :], True)
        zt[...] = jnp.zeros_like(zt)
        dq[...] = jnp.zeros_like(dq)

    low = lax.broadcasted_iota(jnp.int32, (BLOCK, 128), 1) < 64
    c = cum[0, 0]
    st = step[0, 0]
    row_sums = [None] * GH
    col_sums = []
    dxs = [[], []]
    for i in range(GH):
        pair = i // 2 * 128
        mine = low if i % 2 == 0 else ~low
        dop = do[:, pair : pair + 128]
        xm = jnp.where(mine, x[:, pair : pair + 128].astype(f32), 0.0).astype(bf16)
        cols = []
        for half in range(2):
            rows = slice(half * HALF, (half + 1) * HALF)
            after = slice(half * HALF, BLOCK)
            e = bdot(xm[rows], dop[after], NT)
            d = row[0, 0, 0, i : i + 1, after] - c[rows, i : i + 1] + mask[rows, after]
            decay = jnp.exp(d)
            le = decay * e * st[rows, i : i + 1]
            zt[rows, after] += le
            gr = gram[rows, after]
            m = le * gr
            total = jnp.sum(m, axis=0, keepdims=True)
            if half == 0:
                row_sums[i] = total
            else:
                row_sums[i] = row_sums[i] + jnp.concatenate([jnp.zeros((1, HALF), f32), total], axis=1)
            cols.append(jnp.sum(m, axis=1, keepdims=True))
            dxs[half].append(bdot((decay * gr).astype(bf16), dop[after], NN))
        col_sums.append(jnp.concatenate(cols, axis=0))
    for half in range(2):
        p = dxs[half]
        lo = low[:HALF]
        dxs_out[half * HALF : (half + 1) * HALF, :] = jnp.concatenate(
            [jnp.where(lo, p[0], p[1]), jnp.where(lo, p[2], p[3])], axis=1
        ).astype(bf16)
    dof = do[...].astype(f32)
    rw = wide(reach_of(c, marks[0]))
    from_state = bdot(queries, enter[0], NN) * rw
    came = head_sum(dof * from_state)
    upper = triangle(upper=True)
    rows4 = jnp.concatenate(row_sums + [jnp.zeros((16 - GH, BLOCK), f32)], axis=0)
    cols4 = jnp.concatenate(col_sums, axis=1)
    dec_out[0, 0] = fdot(upper, rows4, NT)[:, :GH] + fdot(upper, came - cols4, NN)
    dq[...] += bdot(dof * rw, enter[0], NT)

    @pl.when(g_id == pl.num_programs(1) - 1)
    def _():
        z = zt[...].astype(bf16)
        dbc_out[:, :n] = bdot(z, queries, NN)
        dbc_out[:, n:] = dq[...] + bdot(z, keys, TN)


def finish_body(
    nb, pk, x, do, dxl, bc, dbc, leave, enter, cum, step, dec, dt, sel, hp, marks, kern, bias,
    back_out, dt_out, kg_out, sm_out, v_scr, m_scr, grad, dk,
):
    T = nb * BLOCK
    n = bc.shape[1] // 2
    g_id = pl.program_id(1)
    last = pl.num_programs(1) - 1

    @pl.when(g_id == 0)
    def _():
        dk[...] = jnp.zeros_like(dk)
        dt_out[0] = jnp.zeros((T + HALO, 128), bf16)

    @pl.when(g_id < last)
    def _():
        rate = hp[0, 1:2, :]
        skip = wide(hp[0, 2:3, :])
        strict = triangle(strict_lower=True)
        sums = [0.0, 0.0, 0.0]
        for b in range(nb):
            rows = slice(b * BLOCK, (b + 1) * BLOCK)
            c = cum[0, 0, rows, :]
            st = step[0, 0, rows, :]
            end = c[BLOCK - 1 :, :]
            tail = wide(jnp.exp(end - c) * marks[0, rows, 3:4])
            stw = wide(st)
            lv = leave[0, b]
            kl = bdot(bc[rows, :n], lv, NN) * tail
            dxs = dxl[rows, :].astype(f32) + kl
            dof = do[rows, :].astype(f32)
            xf = x[rows, :].astype(f32)
            xs = xf * stw
            grad[rows, :] = skip * dof + stw * dxs
            out4 = head_sum(xs * kl)
            direct = head_sum(xf * dxs)
            sums[2] = sums[2] + jnp.sum(head_sum(dof * xf), axis=0, keepdims=True)
            dk[rows, :] += bdot(xs * tail, lv, NT)
            both = jnp.sum(enter[0, b].astype(f32) * lv.astype(f32), axis=0, keepdims=True)
            both = jnp.concatenate([both, jnp.zeros((15, LANES), f32)], axis=0)
            through = head_sum(both)[:1] * jnp.exp(end) * marks[0, b * BLOCK : b * BLOCK + 1, 5:6]
            decay = dec[0, 0, rows, :] + fdot(strict, out4, NN) + through
            sums[1] = sums[1] - rate * jnp.sum(st * decay, axis=0, keepdims=True)
            raw = bdot(dt[0, rows, :], sel[0], NN)[:, :GH] + hp[0, 0:1, :]
            rg = (direct - rate * decay) * sigmoid(raw)
            sums[0] = sums[0] + jnp.sum(rg, axis=0, keepdims=True)
            padded = jnp.concatenate([rg, jnp.zeros((BLOCK, 128 - GH), f32)], axis=1)
            spot = bdot(padded, sel[0], NT)
            dt_out[0, rows, :] = (dt_out[0, rows, :].astype(f32) + spot).astype(bf16)
        sm_out[0, 0] = jnp.concatenate(sums + [jnp.zeros((5, GH), f32)], axis=0)

    @pl.when(g_id == last)
    def _():
        grad[...] = jnp.concatenate([dbc[:, :n] + dk[...], dbc[:, n:]], axis=1)

    v_scr[:HALO, :] = pk[0, T:, :].astype(f32)
    v_scr[HALO:, :] = pk[0, :T, :].astype(f32)
    pre = bias[...] + kern[0:1, :] * v_scr[HALO : HALO + T, :]
    for k in range(1, 4):
        pre = pre + kern[k : k + 1, :] * (v_scr[HALO - k : HALO - k + T, :] * marks[0, :, k - 1 : k])
    sg = sigmoid(pre)
    cg = grad[...] * (sg * (1.0 + pre * (1.0 - sg)))
    m_scr[:HALO, :] = jnp.zeros((HALO, LANES), f32)
    m_scr[HALO + T :, :] = jnp.zeros((HALO, LANES), f32)
    kgs = []
    back = None
    for k in range(4):
        m = cg if k == 0 else cg * marks[0, :, k - 1 : k]
        kgs.append(jnp.sum(m * v_scr[HALO - k : HALO - k + T, :], axis=0, keepdims=True))
        m_scr[HALO : HALO + T, :] = m
        part = kern[k : k + 1, :] * m_scr[k : k + T + HALO, :]
        back = part if back is None else back + part
    kgs.append(jnp.sum(cg, axis=0, keepdims=True))
    kg_out[0] = jnp.concatenate(kgs + [jnp.zeros((3, LANES), f32)], axis=0)
    back = back.astype(bf16)
    back_out[0, :T, :] = back[HALO:]
    back_out[0, T:, :] = back[:HALO]

def offsets(index, starts, sizes, steps):
    window = []
    for s, n, step in zip(starts, sizes, steps):
        if not isinstance(s, int):
            s = pl.multiple_of(index[s[0]], step)
        window.append(pl.ds(s, n))
    return tuple(window)


def tabled(moves):
    table = []

    def entry(v):
        if isinstance(v, (int, np.integer)):
            return int(v)
        table.append(jnp.asarray(v, jnp.int32))
        return (len(table) - 1,)

    moves = [tuple(tuple(entry(v) for v in part) for part in m) for m in moves]
    table = table or [jnp.zeros((), jnp.int32)]
    return moves, jnp.stack(table)


def assemble(pieces, shape):
    arrays = [p[0] for p in pieces]
    zero = (0,) * len(shape)
    moves, table = tabled([(zero if s is None else s, at) for _, s, _, at in pieces])
    steps = (1,) * (len(shape) - 2) + (16, 128)

    n = len(arrays)

    def kernel(index, *refs):
        out, held, sems = refs[n], refs[n + 1 : -1], refs[-1]
        loads, stores = [], []
        for i, (source, _) in enumerate(moves):
            window = offsets(index, source, pieces[i][2], steps)
            loads.append(pltpu.make_async_copy(refs[i].at[window], held[i], sems.at[0, i]))
            loads[-1].start()
        for i, (_, target) in enumerate(moves):
            loads[i].wait()
            window = offsets(index, target, pieces[i][2], steps)
            stores.append(pltpu.make_async_copy(held[i], out.at[window], sems.at[1, i]))
            stores[-1].start()
        for c in stores:
            c.wait()

    size = 4 * int(np.prod(shape))
    return pl.pallas_call(
        kernel,
        in_specs=[pl.BlockSpec(memory_space=pltpu.SMEM)]
        + [pl.BlockSpec(memory_space=pltpu.HBM)] * len(arrays),
        out_specs=pl.BlockSpec(memory_space=pl.ANY),
        out_shape=jax.ShapeDtypeStruct(shape, arrays[0].dtype),
        scratch_shapes=[pltpu.VMEM(p[2], p[0].dtype) for p in pieces]
        + [pltpu.SemaphoreType.DMA((2, n))],
        compiler_params=pltpu.CompilerParams(vmem_limit_bytes=VMEM_LIMIT),
        cost_estimate=pl.CostEstimate(flops=0, bytes_accessed=size, transcendentals=0),
        name="assemble",
    )(table, *arrays)


def place(pieces, moves, shape, buf):
    spots, table = tabled([(s, at) for _, s, _, at in moves])
    n = len(pieces)

    def kernel(index, *refs):
        out, wide_refs, sems = refs[-n - 2], refs[-n - 1 : -1], refs[-1]
        copies = []
        for i in range(n):
            wide_refs[i][...] = refs[i][...].astype(f32)
            for k, (source, target) in enumerate(spots):
                if moves[k][0] != i:
                    continue
                sizes = moves[k][2]
                copies.append(
                    pltpu.make_async_copy(
                        wide_refs[i].at[offsets(index, source, sizes, (8, 128))],
                        out.at[offsets(index, target, sizes, (8, 128))],
                        sems.at[k],
                    )
                )
                copies[-1].start()
        for c in copies:
            c.wait()

    size = sum(6 * p.size for p in pieces)
    extra = [] if buf is None else [buf]
    return pl.pallas_call(
        kernel,
        in_specs=[pl.BlockSpec(memory_space=pltpu.SMEM)]
        + [pl.BlockSpec(memory_space=pltpu.VMEM)] * n
        + [pl.BlockSpec(memory_space=pl.ANY)] * len(extra),
        out_specs=pl.BlockSpec(memory_space=pl.ANY),
        out_shape=jax.ShapeDtypeStruct(shape, f32),
        scratch_shapes=[pltpu.VMEM(p.shape, f32) for p in pieces]
        + [pltpu.SemaphoreType.DMA((len(moves),))],
        input_output_aliases={} if buf is None else {1 + n: 0},
        compiler_params=pltpu.CompilerParams(vmem_limit_bytes=VMEM_LIMIT),
        cost_estimate=pl.CostEstimate(flops=0, bytes_accessed=size, transcendentals=0),
        name="place",
    )(table, *pieces, *extra)


def body(
    g,
    tokens,
    in_weight,
    out_weight,
    pre_gain,
    conv_kernel,
    conv_bias,
    step_bias,
    decay_log,
    skip_gain,
    gate_gain,
    segments,
    cotangent,
):
    g.place()
    heads = step_bias.shape[0]
    inner = gate_gain.shape[0]
    channels = conv_bias.shape[0]
    shared = channels - inner
    state = shared // 2
    taps = conv_kernel.shape[0]
    hd = inner // heads
    HL = heads // g.TP
    HW = HL * hd
    CW = HW + shared
    own_len = tokens.shape[1]
    width = tokens.shape[2]
    own_d = in_weight.shape[0]
    T = own_len * g.W
    TE = T + HALO
    nb = T // BLOCK
    NB = 2 * nb
    G = HW // LANES
    KW = HW + shared + 128
    j = g.j
    other_j = g.w * 2 + 1 - g.c

    w_t = in_weight.T
    n_rest = KW - HW
    rest = jnp.pad(w_t[2 * inner :], ((0, KW - CW - heads), (0, 0)))

    def with_rest(jj):
        return jnp.concatenate([lax.dynamic_slice_in_dim(w_t, inner + HW * jj, HW, 0), rest], axis=0)

    far = g.flip_core(with_rest(other_j))
    half_packed = assemble(
        [
            (w_t, (inner + HW * j, 0), (HW, own_d), (0, g.c * own_d)),
            (rest, None, (n_rest, own_d), (HW, g.c * own_d)),
            (far, None, (KW, own_d), (0, (1 - g.c) * own_d)),
        ],
        (KW, 2 * own_d),
    )

    series = tokens[0].astype(f32)
    scale = lax.rsqrt(jnp.mean(series * series, axis=-1, keepdims=True) + epsilon)
    normed = g.own_first((series * scale * pre_gain[None, :]).astype(bf16))

    stages = Stages()
    at_n = stages.add(g.gather_task, normed, normed[own_len - HALO :])
    at_packed = stages.add(g.direct_task, half_packed, [9, 5], 1)
    in_weight, out_weight, cotangent = stages.launch([in_weight, out_weight, cotangent])
    w_t = in_weight.T
    cot_own = g.own_first(cotangent[0])
    near_gate = lax.dynamic_slice_in_dim(w_t, HW * j, HW, 0)
    far_gate = lax.dynamic_slice_in_dim(w_t, HW * other_j, HW, 0)
    near_out = lax.dynamic_slice_in_dim(out_weight, HW * j, HW, 1)
    far_out = lax.dynamic_slice_in_dim(out_weight, HW * other_j, HW, 1)
    at_seg = stages.add(g.one_task, [segments], g.flip_core)
    at_far = stages.add(g.one_task, [far_gate, far_out], g.flip_core)
    stages.settle([])
    stages.launch([])
    stages.settle([], leave=[at_n, at_packed])
    far_gate, far_out = at_far["got"]
    half_gate = assemble(
        [
            (near_gate, None, (HW, own_d), (0, g.c * own_d)),
            (far_gate, None, (HW, own_d), (0, (1 - g.c) * own_d)),
        ],
        (HW, 2 * own_d),
    )
    half_out = assemble(
        [
            (near_out, None, (own_d, HW), (g.c * own_d, 0)),
            (far_out, None, (own_d, HW), ((1 - g.c) * own_d, 0)),
        ],
        (2 * own_d, HW),
    )

    s_lo, s_hi = g.by_core(segments, at_seg["got"][0])
    seg_all = jnp.concatenate([s_lo, s_hi], axis=0)
    seg_pad = jnp.concatenate([jnp.full((2, HALO), -1, jnp.int32), seg_all], axis=1)
    seg_ext = lax.dynamic_slice_in_dim(seg_pad, g.z * T, T + HALO, 1)
    seg = seg_ext[:, HALO:]
    ends = [seg[:, (b + 1) * BLOCK - 1 : (b + 1) * BLOCK] for b in range(nb)]
    begins = [seg_ext[:, HALO - 1 + b * BLOCK : HALO + b * BLOCK] for b in range(nb)]
    block_end = jnp.concatenate(ends, axis=1)
    prior_end = jnp.concatenate(begins, axis=1)
    carry_flag = (prior_end == block_end).astype(f32)

    def across(cols):
        return jnp.concatenate([jnp.broadcast_to(v, (2, BLOCK)) for v in cols], axis=1)

    end_row, prior_row = across(ends), across(begins)
    flags = [(seg_ext[:, HALO - k : HALO - k + T] == seg) for k in range(1, taps)]
    flags += [seg == end_row, seg == prior_row, end_row == prior_row, seg, jnp.zeros_like(seg)]
    flags = jnp.stack([v.astype(f32) for v in flags], axis=1)

    def own_channels(a):
        x_part = lax.dynamic_slice_in_dim(a, HW * j, HW, a.ndim - 1)
        return jnp.concatenate([x_part, a[..., inner:]], axis=-1)

    def own_heads(a):
        return lax.dynamic_slice_in_dim(a, HL * j, HL, a.ndim - 1)

    kernel_own = own_channels(conv_kernel)
    bias_own = own_channels(conv_bias)[None, :]
    rate = jnp.exp(own_heads(decay_log))
    hp = jnp.stack([own_heads(step_bias), rate, own_heads(skip_gain)]).reshape(3, G, GH)
    hp = jnp.pad(hp.transpose(1, 0, 2), ((0, 0), (0, 5), (0, 0)))
    ids = HL * j + GH * lax.broadcasted_iota(jnp.int32, (G, 128, 128), 0)
    lane = lax.broadcasted_iota(jnp.int32, (G, 128, 128), 2)
    sel = (lax.broadcasted_iota(jnp.int32, (G, 128, 128), 1) == ids + lane) & (lane < GH)
    sel = sel.astype(bf16)
    gain_own = lax.dynamic_slice_in_dim(gate_gain, HW * j, HW, 0)[None, :]
    (marks,) = call(
        turn_body,
        (2,),
        [(flags, (1, 8, T), lambda s: (s, 0, 0))],
        [((2, T, 8), f32, (1, T, 8), lambda s: (s, 0, 0))],
        name="turn",
    )
    held = [half_gate, half_out, cot_own, marks, flags, kernel_own, bias_own, hp, sel, gain_own]
    held = stages.settle(held)
    half_gate, half_out, cot_own, marks, flags, kernel_own, bias_own, hp, sel, gain_own = held
    at_gate = stages.add(g.direct_task, half_gate, [1], 1)
    at_cot = stages.add(g.gather_task, cot_own, None)
    stages.launch([])
    stages.settle([], leave=[at_gate, at_cot])
    n_ext = at_n["all"].reshape(2 * TE, width)
    w_packed = at_packed["w"]
    packed = low_dot(n_ext, w_packed, NT).astype(bf16)
    (packed,) = stages.settle([packed], leave=[at_gate])
    (packed,) = stages.launch([packed])
    packed = packed.reshape(2, TE, KW)
    marks_b = marks.reshape(NB, BLOCK, 8)

    def seq_block(b):
        return lax.div(b, nb), lax.rem(b, nb)

    def late(c):
        return jnp.maximum(c - 1, 0)

    def shared_first(c):
        return jnp.where(c == 0, G, c - 1)

    dt_block = CW // 128
    x, bc, s_block, step, cum, row = call(
        partial(conv_kernel_body, nb),
        (2, G + 1),
        [
            (packed, (1, TE, LANES), lambda s, c: (s, 0, shared_first(c))),
            (packed, (1, TE, 128), lambda s, c: (s, 0, dt_block)),
            (sel, (1, 128, 128), lambda s, c: (late(c), 0, 0)),
            (hp, (1, 8, GH), lambda s, c: (late(c), 0, 0)),
            (marks, (1, T, 8), lambda s, c: (s, 0, 0)),
            (kernel_own, (taps, LANES), lambda s, c: (0, shared_first(c))),
            (bias_own, (1, LANES), lambda s, c: (0, shared_first(c))),
        ],
        [
            ((2 * T, HW), bf16, (T, LANES), lambda s, c: (s, late(c))),
            ((2 * T, shared), bf16, (T, shared), lambda s, c: (s, 0)),
            ((2, nb, state, HW), f32, (1, nb, state, LANES), lambda s, c: (s, 0, 0, late(c))),
            ((2, G, T, GH), f32, (1, 1, T, GH), lambda s, c: (s, late(c), 0, 0)),
            ((2, G, T, GH), f32, (1, 1, T, GH), lambda s, c: (s, late(c), 0, 0)),
            ((2, G, nb, GH, BLOCK), f32, (1, 1, nb, GH, BLOCK), lambda s, c: (s, late(c), 0, 0, 0)),
        ],
        [pltpu.VMEM((TE, LANES), f32), pltpu.VMEM((T, state), bf16)],
        flops=2 * T * HW * state * 20,
        name="convolve",
    )

    end = jnp.exp(row[..., BLOCK - 1]).transpose(0, 2, 1, 3).reshape(2, nb, HL)
    carry_b = end * carry_flag[:, :, None]

    def spread(a):
        return jnp.repeat(a, hd, axis=-1)

    carry_wide = spread(carry_b)[:, :, None, :]
    carry_range = jnp.prod(carry_b, axis=1)
    s_range = s_block[:, 0]
    for b in range(1, nb):
        s_range = s_block[:, b] + carry_wide[:, b] * s_range
    s_range, x, bc, cum, row, step = stages.settle(
        [s_range, x, bc, cum, row, step], leave=[at_cot]
    )
    at_out = stages.add(g.direct_task, half_out, [1], 0)
    at_enter = stages.add(g.state_task, s_range, carry_range, spread, 1)
    x, bc, cum, row, step = stages.launch([x, bc, cum, row, step])

    def tile(a):
        return (a, (BLOCK, LANES), lambda b, k: (b, k))

    def whole(a):
        return (a, (BLOCK, a.shape[1]), lambda b, k: (b, 0))

    def small_tile(a):
        def at(b, k):
            s, m = seq_block(b)
            return s, k, m, 0

        return (a, (1, 1, BLOCK, GH), at)

    def row_tile(b, k):
        s, m = seq_block(b)
        return s, k, m, 0, 0

    def flag_tile(b, k):
        s, m = seq_block(b)
        return s, 0, m

    pair_flops = 2 * 2 * T * BLOCK * HW
    (y_local,) = call(
        intra_forward_body,
        (NB, G),
        [
            tile(x),
            whole(bc),
            small_tile(cum),
            (row, (1, 1, 1, GH, BLOCK), row_tile),
            small_tile(step),
            (marks_b, (1, BLOCK, 8), lambda b, k: (b, 0, 0)),
            (flags, (1, 8, BLOCK), flag_tile),
            (hp, (1, 8, GH), lambda b, k: (k, 0, 0)),
        ],
        [((2 * T, HW), bf16, (BLOCK, LANES), lambda b, k: (b, k))],
        [pltpu.VMEM((BLOCK, BLOCK), f32)] * 2,
        flops=pair_flops * 8,
        name="intra_forward",
    )
    w_gate = at_gate["w"]
    gate = low_dot(n_ext, w_gate, NT).astype(bf16)
    y_local, gate = stages.settle([y_local, gate])
    while "state" not in at_enter or "w" not in at_out or "all" not in at_cot:
        stages.launch([])
        stages.settle([])
    enter = [at_enter["state"]]
    for b in range(nb - 1):
        enter.append(s_block[:, b] + carry_wide[:, b] * enter[b])
    enter = jnp.stack(enter, axis=1).astype(bf16)
    w_out = at_out["w"]
    cot_all = at_cot["all"].reshape(2 * T, width)
    out_grad = low_dot(cot_all, w_out, NN).astype(bf16)
    gate = gate.reshape(2, TE, HW)

    def seq_tile(a):
        return (a, (T, LANES), lambda s, k: (s, k))

    def seq_small(a):
        return (a, (1, 1, T, GH), lambda s, k: (s, k, 0, 0))

    def seq_state(a):
        return (a, (1, nb, state, LANES), lambda s, k: (s, 0, 0, k))

    def seq_whole(a):
        return (a, (1,) + a.shape[1:], lambda s, k: (s, 0, 0))

    def lane_tile(a):
        return (a, (a.shape[0], LANES), lambda s, k: (0, k))

    bc_seq = (bc, (T, shared), lambda s, k: (s, 0))
    main_tile = (gate, (1, T, LANES), lambda s, k: (s, 0, k))
    mixed, sums = call(
        partial(join_body, nb),
        (2, G),
        [
            seq_tile(y_local),
            bc_seq,
            seq_state(enter),
            seq_small(cum),
            seq_whole(marks),
            main_tile,
            seq_tile(out_grad),
            lane_tile(gain_own),
        ],
        [
            ((2 * T, HW), bf16, (T, LANES), lambda s, k: (s, k)),
            ((2, 8, T), f32, (1, 8, T), lambda s, k: (s, 0, 0)),
        ],
        flops=pair_flops,
        name="join",
    )
    at_sums = stages.add(g.sum_tp_task, sums)
    while "sum" not in at_sums:
        stages.launch([])
        stages.settle([])

    def turn(spec):
        a, block, at = spec
        return (a, block, lambda k, s: at(s, k))

    normed_out, gate_grad, d_out, gain_grad, de_block = call(
        partial(gates_body, nb, inner),
        (G, 2),
        [
            turn(v)
            for v in [
                seq_tile(mixed),
                main_tile,
                seq_tile(out_grad),
                seq_whole(at_sums["sum"]),
                lane_tile(gain_own),
                bc_seq,
                seq_small(cum),
                seq_whole(marks),
            ]
        ],
        [
            ((2 * T, HW), bf16, (T, LANES), lambda k, s: (s, k)),
            ((2, TE, HW), bf16, (1, TE, LANES), lambda k, s: (s, 0, k)),
            ((2 * T, HW), bf16, (T, LANES), lambda k, s: (s, k)),
            ((1, HW), f32, (1, LANES), lambda k, s: (0, k)),
            ((2, nb, state, HW), f32, (1, nb, state, LANES), lambda k, s: (s, 0, 0, k)),
        ],
        flops=pair_flops,
        name="gates",
    )
    gate_grad = gate_grad.reshape(2 * TE, HW)

    def far_rows(f, n):
        return [f(i).astype(bf16) for i in range(1, n)]

    def out_part(i):
        return low_dot(g.cut(cot_all, 1, i, g.Y), normed_out, TN)

    def in_part(a, i):
        return low_dot(a, g.cut(n_ext, 1, i, g.Y), TN)

    d_range = de_block[:, nb - 1]
    for b in range(nb - 2, -1, -1):
        d_range = de_block[:, b] + carry_wide[:, b] * d_range
    at_leave = stages.add(g.state_task, d_range, carry_range, spread, -1)
    at_outs = stages.add(
        g.gradient_task, far_rows(out_part, g.Y), lambda: out_part(0), 0, (2, 1)
    )
    x, d_out, normed_out, gate_grad = stages.launch([x, d_out, normed_out, gate_grad])
    branch = low_dot(normed_out, w_out, NT).astype(bf16)
    at_branch = stages.add(g.scatter_task, branch.reshape(2, g.W, own_len, width), (1, 2))
    x, d_out = stages.launch([x, d_out])
    dxs, dec, dbc = call(
        intra_backward_body,
        (NB, G),
        [
            tile(x),
            whole(bc),
            tile(d_out),
            small_tile(cum),
            (row, (1, 1, 1, GH, BLOCK), row_tile),
            small_tile(step),
            (
                enter.reshape(NB, state, HW),
                (1, state, LANES),
                lambda b, k: (b, 0, k),
            ),
            (marks_b, (1, BLOCK, 8), lambda b, k: (b, 0, 0)),
            (flags, (1, 8, BLOCK), flag_tile),
        ],
        [
            ((2 * T, HW), bf16, (BLOCK, LANES), lambda b, k: (b, k)),
            ((2, G, T, GH), f32) + small_tile(cum)[1:],
            ((2 * T, shared), f32, (BLOCK, shared), lambda b, k: (b, 0)),
        ],
        [pltpu.VMEM((BLOCK, BLOCK), f32)] * 3 + [pltpu.VMEM((BLOCK, state), f32)],
        flops=pair_flops * 16,
        name="intra_backward",
    )
    gate_far = far_rows(lambda i: in_part(gate_grad, i), g.Y)
    dxs, gate_far = stages.settle([dxs, gate_far])
    kept = {}

    def gate_first():
        kept["gate"] = in_part(gate_grad, 0)
        return kept["gate"]

    at_gates = stages.add(g.gradient_task, gate_far, gate_first, 1, (2, 1))

    while "state" not in at_leave:
        stages.launch([])
        stages.settle([])
    leave = [at_leave["state"]]
    for b in range(nb - 1, 0, -1):
        leave.insert(0, de_block[:, b] + carry_wide[:, b] * leave[0])
    leave = jnp.stack(leave, axis=1).astype(bf16)
    leave, dxs = stages.launch([leave, dxs])

    def held(s, k):
        return s, jnp.minimum(k, G - 1)

    def late_tile(a):
        return (a, (T, LANES), lambda s, k: held(s, k))

    def late_small(a):
        return (a, (1, 1, T, GH), lambda s, k: (*held(s, k), 0, 0))

    def late_state(a):
        return (a, (1, nb, state, LANES), lambda s, k: (s, 0, 0, jnp.minimum(k, G - 1)))

    x_back, dt_back, kg, sm = call(
        partial(finish_body, nb),
        (2, G + 1),
        [
            (packed, (1, TE, LANES), lambda s, k: (s, 0, k)),
            late_tile(x),
            late_tile(d_out),
            late_tile(dxs),
            bc_seq,
            (dbc, (T, shared), lambda s, k: (s, 0)),
            late_state(leave),
            late_state(enter),
            late_small(cum),
            late_small(step),
            late_small(dec),
            (packed, (1, TE, 128), lambda s, k: (s, 0, dt_block)),
            (sel, (1, 128, 128), lambda s, k: (jnp.minimum(k, G - 1), 0, 0)),
            (hp, (1, 8, GH), lambda s, k: (jnp.minimum(k, G - 1), 0, 0)),
            seq_whole(marks),
            lane_tile(kernel_own),
            lane_tile(bias_own),
        ],
        [
            ((2, TE, CW), bf16, (1, TE, LANES), lambda s, k: (s, 0, k)),
            ((2, TE, 128), bf16, (1, TE, 128), lambda s, k: (s, 0, 0)),
            ((2, 8, CW), f32, (1, 8, LANES), lambda s, k: (s, 0, k)),
            ((2, G, 8, GH), f32, (1, 1, 8, GH), lambda s, k: (*held(s, k), 0, 0)),
        ],
        [
            pltpu.VMEM((TE, LANES), f32),
            pltpu.VMEM((HALO + TE, LANES), f32),
            pltpu.VMEM((T, LANES), f32),
            pltpu.VMEM((T, state), f32),
        ],
        flops=pair_flops * 16,
        name="finish",
    )
    edge = jnp.concatenate([x_back[:, T:], dt_back[:, T:]], axis=-1).reshape(2 * HALO, KW)
    spill = low_dot(edge, w_packed, NN).astype(bf16).reshape(2, HALO, width)
    x_flat = x_back.reshape(2 * TE, CW)
    dt_flat = dt_back.reshape(2 * TE, 128)

    def x_part(i):
        return in_part(x_flat[:, :HW], i)

    x_far = far_rows(x_part, g.Y)
    x_far, spill, x_flat, dt_flat, kg, sm = stages.settle([x_far, spill, x_flat, dt_flat, kg, sm])
    at_x = stages.add(g.gradient_task, x_far, lambda: x_own, 1, (2, 1))
    at_spill = stages.add(g.one_task, [spill], lambda a: g.shift_z(a, -1))
    x_flat, dt_flat, kg, sm = stages.launch([x_flat, dt_flat, kg, sm])
    x_own = x_part(0)
    rest_back = jnp.concatenate([x_flat[:, HW:], dt_flat[:, :heads]], axis=1)
    rest = [in_part(rest_back, i) for i in range(g.Y)]
    gate_own = kept["gate"]

    n_rest = shared + heads
    lines = inner // own_d
    pre_lines = width // own_d
    lanes = width // g.Y
    n_small = 6 * lines + 6 + pre_lines
    n_small += -(n_rest + n_small) % 128
    ins = [(jnp.stack([j, g.y]).astype(jnp.int32), None, None)]
    for i in range(g.Y):
        for a, rows, col in (
            (w_gate, HW, i),
            (([gate_own] + gate_far)[i], HW, 0),
            (w_packed, KW, i),
            (([x_own] + x_far)[i], HW, 0),
            (rest[i], n_rest, 0),
        ):
            ins.append((a, (rows, lanes), lambda n, col=col: (0, col)))
    for a in (gain_grad, kg, sm, pre_gain.reshape(pre_lines, own_d)):
        ins.append((a, a.shape, lambda n, d=a.ndim: (0,) * d))
    (small,) = call(
        partial(small_body, g.Y, HW, HL, heads),
        (1,),
        ins,
        [((n_small, own_d), f32, (n_small, own_d), lambda n: (0, 0))],
        name="small",
    )
    copies = jnp.concatenate([small] * 2, axis=1)
    rest = [jnp.concatenate([p, copies], axis=0) for p in rest]
    rest_far = [p.astype(bf16) for p in rest[1:]]
    held = stages.settle([x_own, x_flat, dt_flat, rest_far, rest[0]], leave=[at_gates])
    x_own, x_flat, dt_flat, rest_far, rest_own = held
    at_rest = stages.add(g.gradient_task, rest_far, lambda: rest_own, 1, None)
    spill = at_spill["got"][0]
    spill, gate_grad, x_flat, dt_flat = stages.launch([spill, gate_grad, x_flat, dt_flat])

    NW = 512
    (n_grad,) = call(
        input_grad_body,
        (2, width // NW),
        [
            (gate_grad, (TE, HW), lambda s, n: (s, 0)),
            (x_flat, (TE, CW), lambda s, n: (s, 0)),
            (dt_flat, (TE, 128), lambda s, n: (s, 0)),
            (w_gate, (HW, NW), lambda s, n: (0, n)),
            (w_packed, (CW, NW), lambda s, n: (0, n)),
            (w_packed, (128, NW), lambda s, n: (CW // 128, n)),
            (spill, (1, HALO, NW), lambda s, n: (s, 0, n)),
        ],
        [
            ((2, T, width), bf16, (1, T, NW), lambda s, n: (s, 0, n)),
        ],
        flops=2 * 2 * TE * width * (2 * HW + 128),
        name="input_grad",
    )

    in_shape = (2 * inner + shared + heads, own_d)

    def moves_of(a, first, axis):
        n = a["done"][0].shape[axis] // 4
        moves = []
        for i, (d, e) in enumerate(a["from"]):
            source, target, sizes = [0, 0], [0, 0], [own_d, own_d]
            source[axis], sizes[axis] = i % 4 * n, n
            target[axis] = first + HW * ((g.w ^ d) * 2 + (g.c ^ e))
            moves.append((i // 4, tuple(source), tuple(sizes), tuple(target)))
        return moves

    (n_grad,) = stages.settle([n_grad], leave=[at_x])
    at_ngrad = stages.add(g.scatter_task, n_grad.reshape(2, g.W, own_len, width), (2, 1))
    if g.Z == 2:
        stages.launch([])
        stages.settle([], leave=[at_x, at_outs])
        stages.launch([], hold=[at_gates, at_ngrad])
        stages.settle([], leave=[at_x, at_outs])
        stages.launch([], hold=[at_ngrad])
    else:
        stages.launch([])
    stages.settle([])
    while "done" not in at_outs:
        stages.launch([])
        stages.settle([])
    stages.launch([])
    out_weight_gradient = place(at_outs["done"], moves_of(at_outs, 0, 1), (own_d, inner), None)
    block_output = (series + g.own_first_back(at_branch["sum"])).astype(bf16)[None]
    out_weight_gradient, block_output = stages.settle([out_weight_gradient, block_output])
    while "done" not in at_gates:
        stages.launch([])
        stages.settle([])
    stages.launch([])
    in_buf = place(at_gates["done"], moves_of(at_gates, 0, 0), in_shape, None)
    (in_buf,) = stages.settle([in_buf])
    while "sum" not in at_ngrad:
        stages.launch([])
        stages.settle([])
    stages.launch([])
    n_own = g.own_first_back(at_ngrad["sum"])
    lifted_n = n_own * pre_gain[None, :]
    token_gradient = (
        cotangent[0].astype(f32)
        + scale * lifted_n
        - series * scale**3 * jnp.mean(series * lifted_n, axis=-1, keepdims=True)
    )[None]
    token_gradient, in_buf = stages.settle([token_gradient, in_buf])
    while "done" not in at_x:
        stages.launch([])
        (in_buf,) = stages.settle([in_buf])
    if stages.tasks:
        stages.launch([])
    in_buf = place(at_x["done"], moves_of(at_x, inner, 0), in_shape, in_buf)
    while stages.tasks:
        (in_buf,) = stages.settle([in_buf])
        if stages.tasks:
            stages.launch([])
    rest_done = at_rest["done"]
    in_buf = place(
        [rest_done], [(0, (0, 0), (shared + heads, own_d), (2 * inner, 0))], in_shape, in_buf
    )
    in_weight_gradient = in_buf.T

    small = rest_done[n_rest:].astype(f32)
    gain_total = small[:lines].reshape(-1)
    kb = small[lines : 6 * lines].reshape(5, inner)
    at = 6 * lines
    kb = jnp.concatenate([kb, small[at : at + 5, :shared]], axis=1)
    kernel_total, bias_total = kb[:taps], kb[taps]
    step_total, decay_total, skip_total = small[at + 5, : 3 * heads].reshape(3, heads)
    pre_total = small[at + 6 : at + 6 + pre_lines].reshape(-1)
    return (
        block_output,
        token_gradient,
        in_weight_gradient,
        out_weight_gradient,
        pre_total,
        kernel_total,
        bias_total,
        step_total,
        decay_total,
        skip_total,
        gain_total,
    )


def solution(mesh):
    placed = (
        P("shard", "seq", None),
        P("shard", None),
        P("shard", None),
        P(),
        P(),
        P(),
        P(),
        P(),
        P(),
        P(),
        P("shard", None),
        P("shard", "seq", None),
    )
    results = (P("shard", "seq", None),) * 2 + (P("shard", None),) * 2 + (P(),) * 7
    return jax.shard_map(
        partial(body, Slice(mesh)),
        mesh=mesh,
        in_specs=placed,
        out_specs=results,
        check_vma=False,
    )
```

```python
from functools import partial

import jax
import jax.numpy as jnp
import numpy as np
from jax import lax
from jax.experimental import pallas as pl
from jax.experimental.pallas import tpu as pltpu
from jax.sharding import PartitionSpec as P

BLOCK = 256
HALO = 16
epsilon = 1e-05
highest = lax.Precision.HIGHEST
f32 = jnp.float32
bf16 = jnp.bfloat16
AXES = ("seq", "shard")


class Slice:
    def __init__(self, mesh):
        self.seq = mesh.shape["seq"]
        self.shard = mesh.shape["shard"]
        self.Y = self.shard // 2
        self.W = 4
        self.Z = self.seq // self.W
        self.TP = 2 * self.W

    def place(self):
        s, k = lax.axis_index("seq"), lax.axis_index("shard")
        self.z, self.w = s // self.W, s % self.W
        self.y, self.c = k // 2, k % 2
        self.j = self.w * 2 + self.c

    def move(self, a, target):
        pairs = []
        for z in range(self.Z):
            for w in range(self.W):
                for y in range(self.Y):
                    for c in range(2):
                        to = target(z, w, y, c)
                        if to is None or not 0 <= to[0] < self.Z:
                            continue
                        tz, tw, ty, tc = to
                        src = (z * self.W + w) * self.shard + y * 2 + c
                        dst = (tz * self.W + tw) * self.shard + (ty % self.Y) * 2 + tc
                        pairs.append((src, dst))
        return lax.ppermute(a, AXES, pairs)

    def flip(self, a, d, e=0):
        return self.move(a, lambda z, w, y, c: (z, w ^ d, y, c ^ e))

    def bit(self, d, e):
        return self.c if e else (self.w // d) % 2

    def flip_core(self, a):
        return self.flip(a, 0, 1)

    def shift_y(self, a, d):
        return self.move(a, lambda z, w, y, c: (z, w, y + d, c))

    def shift_z(self, a, d):
        return self.move(a, lambda z, w, y, c: (z + d, w, y, c))

    def by_core(self, own, other):
        first = self.c == 0
        return jnp.where(first, own, other), jnp.where(first, other, own)

    def own_first(self, a):
        width = a.shape[-1] // self.Y
        parts = [
            lax.dynamic_slice_in_dim(a, ((self.y - i) % self.Y) * width, width, a.ndim - 1)
            for i in range(self.Y)
        ]
        return jnp.concatenate(parts, axis=-1)

    def own_first_back(self, a):
        width = a.shape[-1] // self.Y
        parts = [
            lax.dynamic_slice_in_dim(a, ((self.y - t) % self.Y) * width, width, a.ndim - 1)
            for t in range(self.Y)
        ]
        return jnp.concatenate(parts, axis=-1)

    def cut(self, a, axis, i, n):
        size = a.shape[axis] // n
        return lax.slice_in_dim(a, i * size, (i + 1) * size, axis=axis)


    def direct_task(self, half, shares, axis, out):
        n, m = half.shape
        edges = [n * sum(shares[:i]) // sum(shares) // 16 * 16 for i in range(len(shares) + 1)]
        pieces = [(half, None, (n, m), (0, 0))]
        for a, b in zip(edges[:-1], edges[1:]):
            sent = yield [half[a:b] if len(shares) > 1 else half]
            got = yield [self.shift_y(sent[0], d) for d in range(1, self.Y)]
            for d, r in enumerate(got):
                at = (a, (d + 1) * m) if axis else ((d + 1) * n + a, 0)
                pieces.append((r, None, (b - a, m), at))
        out["w"] = assemble(pieces, (n, m * self.Y) if axis else (n * self.Y, m))

    def gather_task(self, a, last, out):
        rows, F = a.shape
        half = rows // 2
        sent = yield [a] + ([] if last is None else [last])
        got = yield [self.flip(sent[0], 1), self.flip(sent[0], 2)] + [
            self.move(s, lambda z, w, y, c: (z + 1, t, y, c) if w == self.W - 1 else None)
            for s in sent[1:]
            for t in range(2)
        ]
        r1, r2 = got[:2]
        n = 0
        up, across = r1[:half], r2[half:]
        if last is not None:
            n = last.shape[0]
            edge = got[2] + got[3]
            up = jnp.concatenate([up, edge], axis=0)
        sent = yield [up, across, jnp.stack([a, r1, r2])]
        up, across, others = yield [
            self.flip(sent[0], 2),
            self.flip(sent[1], 1),
            self.flip_core(sent[2]),
        ]
        far = jnp.concatenate([up[:half], across], axis=0)
        if last is not None:
            edge = jnp.where(self.w < 2, edge, up[half:])
            far = jnp.concatenate([far, edge], axis=0)
        (far,) = yield [far]
        (far_other,) = yield [self.flip_core(far)]
        pieces = []
        for i, (d, mine) in enumerate(((0, a), (1, r1), (2, r2))):
            at = (self.w ^ d) * rows
            pieces.append((mine[None], None, (1, rows, F), (self.c, at, 0)))
            pieces.append((others, (i, 0, 0), (1, rows, F), (1 - self.c, at, 0)))
        length = self.W * rows
        for c, part in ((self.c, far[None]), (1 - self.c, far_other[None])):
            pieces.append((part, (0, 0, 0), (1, rows, F), (c, (self.w ^ 3) * rows, 0)))
            if n:
                pieces.append((part, (0, rows, 0), (1, n, F), (c, length, 0)))
        out["all"] = assemble(pieces, (2, length + n, F))

    def scatter_task(self, a, order, out):
        keep, send = self.by_core(a[0], a[1])
        sent = yield [send]
        got = yield [self.flip(sent[0], 0, 1)]
        total = (keep.astype(f32) + got[0].astype(f32)).astype(bf16)

        def part(d):
            return lax.dynamic_index_in_dim(total, self.w ^ d, 0, False)

        d1, d2 = order
        sent = yield [jnp.stack([part(d1), part(3)])]
        got = yield [self.flip(sent[0], d1)]
        mine = part(0).astype(f32) + got[0][0].astype(f32)
        pass_on = (part(d2).astype(f32) + got[0][1].astype(f32)).astype(bf16)
        sent = yield [pass_on]
        got = yield [self.flip(sent[0], d2)]
        out["sum"] = mine + got[0].astype(f32)

    def gradient_task(self, send, own_part, axis, order, out):
        half = self.Z // 2
        over_group = order is None
        halvings = [(0, 1), (2, 0), (1, 0)]
        sent = yield send
        got = yield [self.shift_y(p, -i - 1) for i, p in enumerate(sent)]
        acc = own_part()
        for r in got:
            acc = acc + r.astype(f32)
        q = acc.astype(bf16)
        if over_group:
            for d, e in halvings:
                n = q.shape[0] // 2
                b = self.bit(d, e)
                keep = lax.dynamic_slice_in_dim(q, b * n, n, 0)
                (send,) = yield [lax.dynamic_slice_in_dim(q, (1 - b) * n, n, 0)]
                (got,) = yield [self.flip(send, d, e)]
                q = (keep.astype(f32) + got.astype(f32)).astype(bf16)
        for step in range(half - 1):
            (q,) = yield [q]
            got = yield [
                self.move(
                    q,
                    lambda z, w, y, c: (z + 1, w, y, c)
                    if z == step
                    else ((z - 1, w, y, c) if z == self.Z - 1 - step else None),
                )
            ]
            q = (q.astype(f32) + got[0].astype(f32)).astype(bf16)
        (q,) = yield [q]
        got = yield [
            self.move(
                q,
                lambda z, w, y, c: (z + 1, w, y, c)
                if z == half - 1
                else ((z - 1, w, y, c) if z == half else None),
            )
        ]
        q = (q.astype(f32) + got[0].astype(f32)).astype(bf16)
        for step in range(half - 1):
            a, b = half - 1 - step, half + step
            (q,) = yield [q]
            got = yield [
                self.move(
                    q,
                    lambda z, w, y, c: (z - 1, w, y, c)
                    if z == a
                    else ((z + 1, w, y, c) if z == b else None),
                )
            ]
            q = jnp.where((self.z == a - 1) | (self.z == b + 1), got[0], q)
        if over_group:
            for d, e in reversed(halvings):
                (q,) = yield [q]
                if e:
                    keep, send = self.by_core(self.cut(q, 1, 0, 2), self.cut(q, 1, 1, 2))
                    (got,) = yield [self.flip(send, d, e)]
                    q = keep
                else:
                    (got,) = yield [self.flip(q, d, e)]
                low = self.bit(d, e) == 0
                q = jnp.concatenate([jnp.where(low, q, got), jnp.where(low, got, q)], axis=0)
            out["done"] = q
            return
        keep, send = self.by_core(self.cut(q, axis, 0, 2), self.cut(q, axis, 1, 2))
        (send,) = yield [send]
        got = yield [self.flip(send, 0, 1)]
        pair = jnp.concatenate([keep, got[0]], axis=1 - axis)
        (pair,) = yield [pair]
        got = yield [self.flip(pair, order[0])]
        quad = jnp.concatenate([pair, got[0]], axis=1 - axis)
        (quad,) = yield [quad]
        got = yield [self.flip(quad, order[1])]
        out["done"] = [quad, got[0]]
        a, b = order
        out["from"] = [(0, 0), (0, 1), (a, 0), (a, 1), (b, 0), (b, 1), (a ^ b, 0), (a ^ b, 1)]

    def state_task(self, cur, cc, spread, direction, out):
        d = 1
        while d < self.Z // 2:
            send = [cur.astype(bf16)] + ([cc] if 2 * d < self.Z // 2 else [])
            sent = yield send
            got = yield [self.shift_z(a, direction * d) for a in sent]
            cur = cur + spread(cc)[:, None, :] * got[0].astype(f32)
            if len(got) > 1:
                cc = cc * got[1]
            d *= 2
        sent = yield [cur.astype(bf16)]
        got = yield [self.shift_z(sent[0], direction)]
        out["state"] = got[0].astype(f32)

    def sum_tp_task(self, a, out):
        sent = yield [a]
        got = yield [self.flip_core(sent[0])]
        (a,) = yield [a + got[0]]
        got = yield [self.flip(a, d) for d in range(1, self.W)]
        for r in got:
            a = a + r
        out["sum"] = a

    def one_task(self, arrays, send, out):
        sent = yield arrays
        out["got"] = yield [send(a) for a in sent]


def fence(arrays):
    flat, tree = jax.tree.flatten(arrays)
    return jax.tree.unflatten(tree, lax.optimization_barrier(tuple(flat)))


class Stages:
    def __init__(self):
        self.tasks = []

    def add(self, task, *args):
        out = {}
        gen = task(*args, out)
        self.tasks.append([gen, next(gen), None, out])
        return out

    def settle(self, live, leave=()):
        flying = [t for t in self.tasks if t[2] is not None and not any(t[3] is o for o in leave)]
        got, live = fence(([t[2] for t in flying], live))
        for t, r in zip(flying, got):
            t[2] = None
            try:
                t[1] = t[0].send(r)
            except StopIteration:
                self.tasks.remove(t)
        return live

    def launch(self, live, hold=()):
        waiting = [t for t in self.tasks if t[2] is None and not any(t[3] is o for o in hold)]
        ready, live = fence(([t[1] for t in waiting], live))
        for t, a in zip(waiting, ready):
            t[2] = t[0].send(a)
        return live


def low_dot(a, b, dims):
    return lax.dot_general(a.astype(bf16), b.astype(bf16), dims, preferred_element_type=f32)


NT = (((1,), (1,)), ((), ()))
TN = (((0,), (0,)), ((), ()))
NN = (((1,), (0,)), ((), ()))
GH = 4
LANES = 256
FAR = -1e30
VMEM_LIMIT = 40 * 1024 * 1024


def bdot(a, b, dims):
    return lax.dot_general(a.astype(bf16), b.astype(bf16), dims, preferred_element_type=f32)


def fdot(a, b, dims):
    return lax.dot_general(a, b, dims, precision=highest, preferred_element_type=f32)


def wide(fac):
    low = lax.broadcasted_iota(jnp.int32, (fac.shape[0], 128), 1) < 64
    pairs = [jnp.where(low, fac[:, i : i + 1], fac[:, i + 1 : i + 2]) for i in (0, 2)]
    return jnp.concatenate(pairs, axis=1)


def head_sum(v):
    lane = lax.broadcasted_iota(jnp.int32, (LANES, 128), 0) // 64
    head = lax.broadcasted_iota(jnp.int32, (LANES, 128), 1)
    return bdot(v, (lane == head).astype(bf16), NN)[:, :GH]


def triangle(strict_lower=False, upper=False):
    r = lax.broadcasted_iota(jnp.int32, (BLOCK, BLOCK), 0)
    t = lax.broadcasted_iota(jnp.int32, (BLOCK, BLOCK), 1)
    keep = t >= r if upper else (t < r if strict_lower else t <= r)
    return keep.astype(f32)


def sigmoid(v):
    return 0.5 * jnp.tanh(0.5 * v) + 0.5


def turned(rows):
    pad = jnp.zeros((120, 128), f32)
    parts = []
    for i in range(rows.shape[1] // 128):
        square = jnp.concatenate([rows[:, i * 128 : (i + 1) * 128], pad], axis=0)
        parts.append(square.T[:, :8])
    return jnp.concatenate(parts, axis=0)


def turn_body(rows, out):
    out[0] = turned(rows[0])


def softplus(v):
    u = jnp.exp(-jnp.abs(v))
    w = 1.0 + u
    log1p = jnp.where(w == 1.0, u, jnp.log(w) * u / jnp.where(w == 1.0, 1.0, w - 1.0))
    return jnp.maximum(v, 0.0) + log1p


def call(kernel, grid, ins, outs, scratch=(), flops=0, name=None):
    arrays = [a for a, _, _ in ins]
    total = sum(a.size * a.dtype.itemsize for a in arrays)
    total += sum(int(np.prod(s)) * jnp.dtype(d).itemsize for s, d, _, _ in outs)
    return pl.pallas_call(
        kernel,
        grid=grid,
        in_specs=[
            pl.BlockSpec(memory_space=pltpu.SMEM) if b is None else pl.BlockSpec(b, m)
            for _, b, m in ins
        ],
        out_specs=[pl.BlockSpec(b, m) for _, _, b, m in outs],
        out_shape=[jax.ShapeDtypeStruct(s, d) for s, d, _, _ in outs],
        scratch_shapes=list(scratch),
        compiler_params=pltpu.CompilerParams(vmem_limit_bytes=VMEM_LIMIT),
        cost_estimate=pl.CostEstimate(flops=0, bytes_accessed=1024, transcendentals=0),
        name=name,
    )(*arrays)


def conv_kernel_body(
    nb, pk, dt, sel, hp, marks, kern, bias, x_out, bc_out, s_out, step_out, cum_out, row_out, v_scr, keys_scr
):
    T = nb * BLOCK
    v_scr[:HALO, :] = pk[0, T:, :].astype(f32)
    v_scr[HALO:, :] = pk[0, :T, :].astype(f32)
    pre = bias[...] + kern[0:1, :] * v_scr[HALO : HALO + T, :]
    for k in range(1, 4):
        pre = pre + kern[k : k + 1, :] * (v_scr[HALO - k : HALO - k + T, :] * marks[0, :, k - 1 : k])
    act = pre * sigmoid(pre)
    chunk = pl.program_id(1)

    @pl.when(chunk == 0)
    def _():
        bc_out[...] = act.astype(bf16)
        keys_scr[...] = act[:, : keys_scr.shape[1]].astype(bf16)

    @pl.when(chunk > 0)
    def _():
        x_out[...] = act.astype(bf16)
        raw = bdot(dt[0, :T, :], sel[0], NN)[:, :GH] + hp[0, 0:1, :]
        step = softplus(raw)
        step_out[0, 0] = step
        tri = triangle()
        for b in range(nb):
            rows = slice(b * BLOCK, (b + 1) * BLOCK)
            st = step[rows]
            cum = fdot(tri, -hp[0, 1:2, :] * st, NN)
            cum_out[0, 0, rows, :] = cum
            padded = jnp.concatenate([cum, jnp.zeros((BLOCK, 128 - GH), f32)], axis=1)
            row_out[0, 0, b] = padded.T[:GH]
            tail = jnp.exp(cum[BLOCK - 1 :, :] - cum) * marks[0, rows, 3:4]
            xst = act[rows] * wide(st * tail)
            s_out[0, b] = bdot(keys_scr[rows, :], xst, TN)


def gaps_mask(seg_col, seg_row, transposed):
    r = lax.broadcasted_iota(jnp.int32, (BLOCK, BLOCK), 0)
    t = lax.broadcasted_iota(jnp.int32, (BLOCK, BLOCK), 1)
    order = t >= r if transposed else r >= t
    return jnp.where(order & (seg_col == seg_row), 0.0, FAR)


HALF = BLOCK // 2


def intra_forward_body(x, bc, cum, row, step, marks, flags, hp, y_out, gram, mask):
    @pl.when(pl.program_id(1) == 0)
    def _():
        n = bc.shape[1] // 2
        gram[...] = bdot(bc[:, n:], bc[:, :n], NT)
        mask[...] = gaps_mask(marks[0, :, 6:7], flags[0, 6:7, :], False)

    xf = x[...].astype(f32)
    xs = (xf * wide(step[0, 0])).astype(bf16)
    low = lax.broadcasted_iota(jnp.int32, (HALF, 128), 1) < 64
    c = cum[0, 0]
    for half in range(2):
        rows = slice(half * HALF, (half + 1) * HALF)
        reachable = (half + 1) * HALF
        g = gram[rows, :reachable]
        m = mask[rows, :reachable]
        parts = []
        for i in range(GH):
            d = c[rows, i : i + 1] - row[0, 0, 0, i : i + 1, :reachable] + m
            p = (jnp.exp(d) * g).astype(bf16)
            pair = i // 2 * 128
            parts.append(bdot(p, xs[:reachable, pair : pair + 128], NN))
        y = jnp.concatenate(
            [jnp.where(low, parts[0], parts[1]), jnp.where(low, parts[2], parts[3])], axis=1
        )
        y_out[rows, :] = (y + wide(hp[0, 2:3, :]) * xf[rows]).astype(bf16)


def reach_of(cum, marks):
    return jnp.exp(jnp.minimum(cum, 0.0)) * marks[:, 4:5]


def join_body(nb, y, bc, enter, cum, marks, gate, og, gain, mixed_out, sums_out):
    n = bc.shape[1] // 2
    ones = jnp.ones((16, LANES), bf16)
    first = lax.broadcasted_iota(jnp.int32, (8, BLOCK), 0) == 0
    for b in range(nb):
        rows = slice(b * BLOCK, (b + 1) * BLOCK)
        reach = wide(reach_of(cum[0, 0, rows, :], marks[0, rows, :]))
        state = bdot(bc[rows, n:], enter[0, b], NN) * reach
        mixed = (y[rows, :].astype(f32) + state).astype(bf16)
        mixed_out[rows, :] = mixed
        gv = gate[0, rows, :].astype(f32)
        gated = mixed.astype(f32) * (gv * sigmoid(gv))
        lifted = og[rows, :].astype(f32) * gain[...]
        ss = bdot(ones, gated * gated, NT)[:8]
        sg = bdot(ones, gated * lifted, NT)[:8]
        both = jnp.where(first, ss, sg)

        @pl.when(pl.program_id(1) == 0)
        def _(both=both, rows=rows):
            sums_out[0, :, rows] = both

        @pl.when(pl.program_id(1) > 0)
        def _(both=both, rows=rows):
            sums_out[0, :, rows] += both


def gates_body(
    nb, inner, mixed, gate, og, sums, gain, bc, cum, marks, no_out, gg_out, do_out, gain_out, de_out
):
    n = bc.shape[1] // 2
    T = nb * BLOCK
    total = turned(sums[0]) / inner
    part = None
    for b in range(nb):
        rows = slice(b * BLOCK, (b + 1) * BLOCK)
        gv = gate[0, rows, :].astype(f32)
        sg = sigmoid(gv)
        act = gv * sg
        mx = mixed[rows, :].astype(f32)
        ogv = og[rows, :].astype(f32)
        r = lax.rsqrt(total[rows, 0:1] + epsilon)
        gr = mx * act * r
        no_out[rows, :] = (gr * gain[...]).astype(bf16)
        p = jnp.sum(ogv * gr, axis=0, keepdims=True)
        part = p if part is None else part + p
        grad = r * (ogv * gain[...]) - gr * (r * r * total[rows, 1:2])
        d_out = (grad * act).astype(bf16)
        do_out[rows, :] = d_out
        gg_out[0, rows, :] = (grad * mx * (sg * (1.0 + gv * (1.0 - sg)))).astype(bf16)
        dr = d_out.astype(f32) * wide(reach_of(cum[0, 0, rows, :], marks[0, rows, :]))
        de_out[0, b] = bdot(bc[rows, n:], dr, TN)
    gg_out[0, T:, :] = jnp.zeros((HALO, LANES), bf16)

    @pl.when(pl.program_id(1) == 0)
    def _():
        gain_out[...] = part

    @pl.when(pl.program_id(1) > 0)
    def _():
        gain_out[...] += part


def small_body(Y, HW, HL, heads, place_ref, *refs):
    pairs, (gain, kg, sm, pre_gain), out = refs[: 5 * Y], refs[5 * Y : -1], refs[-1]
    j, y = place_ref[0], place_ref[1]
    own_d = out.shape[1]
    per = HW // own_d
    lines = per * (heads // HL)
    shared = kg.shape[2] - HW
    out[...] = jnp.zeros_like(out)
    both = kg[0] + kg[1]
    for q in range(per):
        lanes = slice(q * own_d, (q + 1) * own_d)
        out[pl.ds(per * j + q, 1), :] = gain[:, lanes]
        for k in range(5):
            out[pl.ds((k + 1) * lines + per * j + q, 1), :] = both[k : k + 1, lanes]
    at = 6 * lines
    out[at : at + 5, :shared] = both[:5, HW:]
    lane = lax.broadcasted_iota(jnp.int32, (1, own_d), 1)
    row = jnp.zeros((1, own_d), f32)
    for k in range(3):
        for h in range(HL):
            value = sm[0, h // GH, k : k + 1, h % GH : h % GH + 1]
            value = value + sm[1, h // GH, k : k + 1, h % GH : h % GH + 1]
            row = jnp.where(lane == k * heads + HL * j + h, value, row)
    out[at + 5 : at + 6, :] = row
    for i in range(Y):
        wg, pg, wp, px, pr = pairs[5 * i : 5 * i + 5]
        n = pr.shape[0]
        total = jnp.sum(wg[...].astype(f32) * pg[...].astype(f32), axis=0, keepdims=True)
        total += jnp.sum(wp[:HW, :].astype(f32) * px[...].astype(f32), axis=0, keepdims=True)
        total += jnp.sum(wp[HW : HW + n, :].astype(f32) * pr[...].astype(f32), axis=0, keepdims=True)
        rows = total.shape[1] // own_d
        first = lax.rem(y - i + Y, Y) * rows
        for q in range(rows):
            part = total[:, q * own_d : (q + 1) * own_d]
            out[pl.ds(at + 6 + first + q, 1), :] = part / pre_gain[pl.ds(first + q, 1), :]


def input_grad_body(gg, xb, tb, wg, wx, wt, spill, out):
    total = bdot(gg[...], wg[...], NN) + bdot(xb[...], wx[...], NN) + bdot(tb[...], wt[...], NN)
    T = out.shape[1]
    out[0, : T - HALO, :] = total[: T - HALO].astype(bf16)
    out[0, T - HALO :, :] = (total[T - HALO : T] + spill[0].astype(f32)).astype(bf16)


def intra_backward_body(
    x, bc, do, cum, row, step, enter, marks, flags, dxs_out, dec_out, dbc_out, gram, mask, zt, dq
):
    n = bc.shape[1] // 2
    keys, queries = bc[:, :n], bc[:, n:]
    g_id = pl.program_id(1)

    @pl.when(g_id == 0)
    def _():
        gram[...] = bdot(keys, queries, NT)
        mask[...] = gaps_mask(marks[0, :, 6:7], flags[0, 6:7, :], True)
        zt[...] = jnp.zeros_like(zt)
        dq[...] = jnp.zeros_like(dq)

    low = lax.broadcasted_iota(jnp.int32, (BLOCK, 128), 1) < 64
    c = cum[0, 0]
    st = step[0, 0]
    row_sums = [None] * GH
    col_sums = []
    dxs = [[], []]
    for i in range(GH):
        pair = i // 2 * 128
        mine = low if i % 2 == 0 else ~low
        dop = do[:, pair : pair + 128]
        xm = jnp.where(mine, x[:, pair : pair + 128].astype(f32), 0.0).astype(bf16)
        cols = []
        for half in range(2):
            rows = slice(half * HALF, (half + 1) * HALF)
            after = slice(half * HALF, BLOCK)
            e = bdot(xm[rows], dop[after], NT)
            d = row[0, 0, 0, i : i + 1, after] - c[rows, i : i + 1] + mask[rows, after]
            decay = jnp.exp(d)
            le = decay * e * st[rows, i : i + 1]
            zt[rows, after] += le
            gr = gram[rows, after]
            m = le * gr
            total = jnp.sum(m, axis=0, keepdims=True)
            if half == 0:
                row_sums[i] = total
            else:
                row_sums[i] = row_sums[i] + jnp.concatenate([jnp.zeros((1, HALF), f32), total], axis=1)
            cols.append(jnp.sum(m, axis=1, keepdims=True))
            dxs[half].append(bdot((decay * gr).astype(bf16), dop[after], NN))
        col_sums.append(jnp.concatenate(cols, axis=0))
    for half in range(2):
        p = dxs[half]
        lo = low[:HALF]
        dxs_out[half * HALF : (half + 1) * HALF, :] = jnp.concatenate(
            [jnp.where(lo, p[0], p[1]), jnp.where(lo, p[2], p[3])], axis=1
        ).astype(bf16)
    dof = do[...].astype(f32)
    rw = wide(reach_of(c, marks[0]))
    from_state = bdot(queries, enter[0], NN) * rw
    came = head_sum(dof * from_state)
    upper = triangle(upper=True)
    rows4 = jnp.concatenate(row_sums + [jnp.zeros((16 - GH, BLOCK), f32)], axis=0)
    cols4 = jnp.concatenate(col_sums, axis=1)
    dec_out[0, 0] = fdot(upper, rows4, NT)[:, :GH] + fdot(upper, came - cols4, NN)
    dq[...] += bdot(dof * rw, enter[0], NT)

    @pl.when(g_id == pl.num_programs(1) - 1)
    def _():
        z = zt[...].astype(bf16)
        dbc_out[:, :n] = bdot(z, queries, NN)
        dbc_out[:, n:] = dq[...] + bdot(z, keys, TN)


def finish_body(
    nb, pk, x, do, dxl, bc, dbc, leave, enter, cum, step, dec, dt, sel, hp, marks, kern, bias,
    back_out, dt_out, kg_out, sm_out, v_scr, m_scr, grad, dk,
):
    T = nb * BLOCK
    n = bc.shape[1] // 2
    g_id = pl.program_id(1)
    last = pl.num_programs(1) - 1

    @pl.when(g_id == 0)
    def _():
        dk[...] = jnp.zeros_like(dk)
        dt_out[0] = jnp.zeros((T + HALO, 128), bf16)

    @pl.when(g_id < last)
    def _():
        rate = hp[0, 1:2, :]
        skip = wide(hp[0, 2:3, :])
        strict = triangle(strict_lower=True)
        sums = [0.0, 0.0, 0.0]
        for b in range(nb):
            rows = slice(b * BLOCK, (b + 1) * BLOCK)
            c = cum[0, 0, rows, :]
            st = step[0, 0, rows, :]
            end = c[BLOCK - 1 :, :]
            tail = wide(jnp.exp(end - c) * marks[0, rows, 3:4])
            stw = wide(st)
            lv = leave[0, b]
            kl = bdot(bc[rows, :n], lv, NN) * tail
            dxs = dxl[rows, :].astype(f32) + kl
            dof = do[rows, :].astype(f32)
            xf = x[rows, :].astype(f32)
            xs = xf * stw
            grad[rows, :] = skip * dof + stw * dxs
            out4 = head_sum(xs * kl)
            direct = head_sum(xf * dxs)
            sums[2] = sums[2] + jnp.sum(head_sum(dof * xf), axis=0, keepdims=True)
            dk[rows, :] += bdot(xs * tail, lv, NT)
            both = jnp.sum(enter[0, b].astype(f32) * lv.astype(f32), axis=0, keepdims=True)
            both = jnp.concatenate([both, jnp.zeros((15, LANES), f32)], axis=0)
            through = head_sum(both)[:1] * jnp.exp(end) * marks[0, b * BLOCK : b * BLOCK + 1, 5:6]
            decay = dec[0, 0, rows, :] + fdot(strict, out4, NN) + through
            sums[1] = sums[1] - rate * jnp.sum(st * decay, axis=0, keepdims=True)
            raw = bdot(dt[0, rows, :], sel[0], NN)[:, :GH] + hp[0, 0:1, :]
            rg = (direct - rate * decay) * sigmoid(raw)
            sums[0] = sums[0] + jnp.sum(rg, axis=0, keepdims=True)
            padded = jnp.concatenate([rg, jnp.zeros((BLOCK, 128 - GH), f32)], axis=1)
            spot = bdot(padded, sel[0], NT)
            dt_out[0, rows, :] = (dt_out[0, rows, :].astype(f32) + spot).astype(bf16)
        sm_out[0, 0] = jnp.concatenate(sums + [jnp.zeros((5, GH), f32)], axis=0)

    @pl.when(g_id == last)
    def _():
        grad[...] = jnp.concatenate([dbc[:, :n] + dk[...], dbc[:, n:]], axis=1)

    v_scr[:HALO, :] = pk[0, T:, :].astype(f32)
    v_scr[HALO:, :] = pk[0, :T, :].astype(f32)
    pre = bias[...] + kern[0:1, :] * v_scr[HALO : HALO + T, :]
    for k in range(1, 4):
        pre = pre + kern[k : k + 1, :] * (v_scr[HALO - k : HALO - k + T, :] * marks[0, :, k - 1 : k])
    sg = sigmoid(pre)
    cg = grad[...] * (sg * (1.0 + pre * (1.0 - sg)))
    m_scr[:HALO, :] = jnp.zeros((HALO, LANES), f32)
    m_scr[HALO + T :, :] = jnp.zeros((HALO, LANES), f32)
    kgs = []
    back = None
    for k in range(4):
        m = cg if k == 0 else cg * marks[0, :, k - 1 : k]
        kgs.append(jnp.sum(m * v_scr[HALO - k : HALO - k + T, :], axis=0, keepdims=True))
        m_scr[HALO : HALO + T, :] = m
        part = kern[k : k + 1, :] * m_scr[k : k + T + HALO, :]
        back = part if back is None else back + part
    kgs.append(jnp.sum(cg, axis=0, keepdims=True))
    kg_out[0] = jnp.concatenate(kgs + [jnp.zeros((3, LANES), f32)], axis=0)
    back = back.astype(bf16)
    back_out[0, :T, :] = back[HALO:]
    back_out[0, T:, :] = back[:HALO]

def offsets(index, starts, sizes, steps):
    window = []
    for s, n, step in zip(starts, sizes, steps):
        if not isinstance(s, int):
            s = pl.multiple_of(index[s[0]], step)
        window.append(pl.ds(s, n))
    return tuple(window)


def tabled(moves):
    table = []

    def entry(v):
        if isinstance(v, (int, np.integer)):
            return int(v)
        table.append(jnp.asarray(v, jnp.int32))
        return (len(table) - 1,)

    moves = [tuple(tuple(entry(v) for v in part) for part in m) for m in moves]
    table = table or [jnp.zeros((), jnp.int32)]
    return moves, jnp.stack(table)


def assemble(pieces, shape):
    arrays = [p[0] for p in pieces]
    zero = (0,) * len(shape)
    moves, table = tabled([(zero if s is None else s, at) for _, s, _, at in pieces])
    steps = (1,) * (len(shape) - 2) + (16, 128)

    n = len(arrays)

    def kernel(index, *refs):
        out, held, sems = refs[n], refs[n + 1 : -1], refs[-1]
        loads, stores = [], []
        for i, (source, _) in enumerate(moves):
            window = offsets(index, source, pieces[i][2], steps)
            loads.append(pltpu.make_async_copy(refs[i].at[window], held[i], sems.at[0, i]))
            loads[-1].start()
        for i, (_, target) in enumerate(moves):
            loads[i].wait()
            window = offsets(index, target, pieces[i][2], steps)
            stores.append(pltpu.make_async_copy(held[i], out.at[window], sems.at[1, i]))
            stores[-1].start()
        for c in stores:
            c.wait()

    size = 4 * int(np.prod(shape))
    return pl.pallas_call(
        kernel,
        in_specs=[pl.BlockSpec(memory_space=pltpu.SMEM)]
        + [pl.BlockSpec(memory_space=pltpu.HBM)] * len(arrays),
        out_specs=pl.BlockSpec(memory_space=pl.ANY),
        out_shape=jax.ShapeDtypeStruct(shape, arrays[0].dtype),
        scratch_shapes=[pltpu.VMEM(p[2], p[0].dtype) for p in pieces]
        + [pltpu.SemaphoreType.DMA((2, n))],
        compiler_params=pltpu.CompilerParams(vmem_limit_bytes=VMEM_LIMIT),
        cost_estimate=pl.CostEstimate(flops=0, bytes_accessed=size, transcendentals=0),
        name="assemble",
    )(table, *arrays)


def place(pieces, moves, shape, buf):
    spots, table = tabled([(s, at) for _, s, _, at in moves])
    n = len(pieces)

    def kernel(index, *refs):
        out, wide_refs, sems = refs[-n - 2], refs[-n - 1 : -1], refs[-1]
        copies = []
        for i in range(n):
            wide_refs[i][...] = refs[i][...].astype(f32)
            for k, (source, target) in enumerate(spots):
                if moves[k][0] != i:
                    continue
                sizes = moves[k][2]
                copies.append(
                    pltpu.make_async_copy(
                        wide_refs[i].at[offsets(index, source, sizes, (8, 128))],
                        out.at[offsets(index, target, sizes, (8, 128))],
                        sems.at[k],
                    )
                )
                copies[-1].start()
        for c in copies:
            c.wait()

    size = sum(6 * p.size for p in pieces)
    extra = [] if buf is None else [buf]
    return pl.pallas_call(
        kernel,
        in_specs=[pl.BlockSpec(memory_space=pltpu.SMEM)]
        + [pl.BlockSpec(memory_space=pltpu.VMEM)] * n
        + [pl.BlockSpec(memory_space=pl.ANY)] * len(extra),
        out_specs=pl.BlockSpec(memory_space=pl.ANY),
        out_shape=jax.ShapeDtypeStruct(shape, f32),
        scratch_shapes=[pltpu.VMEM(p.shape, f32) for p in pieces]
        + [pltpu.SemaphoreType.DMA((len(moves),))],
        input_output_aliases={} if buf is None else {1 + n: 0},
        compiler_params=pltpu.CompilerParams(vmem_limit_bytes=VMEM_LIMIT),
        cost_estimate=pl.CostEstimate(flops=0, bytes_accessed=size, transcendentals=0),
        name="place",
    )(table, *pieces, *extra)


def body(
    g,
    tokens,
    in_weight,
    out_weight,
    pre_gain,
    conv_kernel,
    conv_bias,
    step_bias,
    decay_log,
    skip_gain,
    gate_gain,
    segments,
    cotangent,
):
    g.place()
    heads = step_bias.shape[0]
    inner = gate_gain.shape[0]
    channels = conv_bias.shape[0]
    shared = channels - inner
    state = shared // 2
    taps = conv_kernel.shape[0]
    hd = inner // heads
    HL = heads // g.TP
    HW = HL * hd
    CW = HW + shared
    own_len = tokens.shape[1]
    width = tokens.shape[2]
    own_d = in_weight.shape[0]
    T = own_len * g.W
    TE = T + HALO
    nb = T // BLOCK
    NB = 2 * nb
    G = HW // LANES
    KW = HW + shared + 128
    j = g.j
    other_j = g.w * 2 + 1 - g.c

    w_t = in_weight.T
    n_rest = KW - HW
    rest = jnp.pad(w_t[2 * inner :], ((0, KW - CW - heads), (0, 0)))

    def with_rest(jj):
        return jnp.concatenate([lax.dynamic_slice_in_dim(w_t, inner + HW * jj, HW, 0), rest], axis=0)

    far = g.flip_core(with_rest(other_j))
    near = lax.dynamic_slice_in_dim(w_t, inner + HW * j, HW, 0)
    half_packed = assemble(
        [
            (near, None, (HW, own_d), (0, g.c * own_d)),
            (rest, None, (n_rest, own_d), (HW, g.c * own_d)),
            (far, None, (KW, own_d), (0, (1 - g.c) * own_d)),
        ],
        (KW, 2 * own_d),
    )

    series = tokens[0].astype(f32)
    scale = lax.rsqrt(jnp.mean(series * series, axis=-1, keepdims=True) + epsilon)
    normed = g.own_first((series * scale * pre_gain[None, :]).astype(bf16))

    stages = Stages()
    at_n = stages.add(g.gather_task, normed, normed[own_len - HALO :])
    at_packed = stages.add(g.direct_task, half_packed, [9, 5], 1)
    in_weight, out_weight, cotangent = stages.launch([in_weight, out_weight, cotangent])
    w_t = in_weight.T
    cot_own = g.own_first(cotangent[0])
    near_gate = lax.dynamic_slice_in_dim(w_t, HW * j, HW, 0)
    far_gate = lax.dynamic_slice_in_dim(w_t, HW * other_j, HW, 0)
    near_out = lax.dynamic_slice_in_dim(out_weight, HW * j, HW, 1)
    far_out = lax.dynamic_slice_in_dim(out_weight, HW * other_j, HW, 1)
    at_seg = stages.add(g.one_task, [segments], g.flip_core)
    at_far = stages.add(g.one_task, [far_gate, far_out], g.flip_core)
    stages.settle([])
    stages.launch([])
    stages.settle([], leave=[at_n, at_packed])
    far_gate, far_out = at_far["got"]
    half_gate = assemble(
        [
            (near_gate, None, (HW, own_d), (0, g.c * own_d)),
            (far_gate, None, (HW, own_d), (0, (1 - g.c) * own_d)),
        ],
        (HW, 2 * own_d),
    )
    half_out = assemble(
        [
            (near_out, None, (own_d, HW), (g.c * own_d, 0)),
            (far_out, None, (own_d, HW), ((1 - g.c) * own_d, 0)),
        ],
        (2 * own_d, HW),
    )

    s_lo, s_hi = g.by_core(segments, at_seg["got"][0])
    seg_all = jnp.concatenate([s_lo, s_hi], axis=0)
    seg_pad = jnp.concatenate([jnp.full((2, HALO), -1, jnp.int32), seg_all], axis=1)
    seg_ext = lax.dynamic_slice_in_dim(seg_pad, g.z * T, T + HALO, 1)
    seg = seg_ext[:, HALO:]
    ends = [seg[:, (b + 1) * BLOCK - 1 : (b + 1) * BLOCK] for b in range(nb)]
    begins = [seg_ext[:, HALO - 1 + b * BLOCK : HALO + b * BLOCK] for b in range(nb)]
    block_end = jnp.concatenate(ends, axis=1)
    prior_end = jnp.concatenate(begins, axis=1)
    carry_flag = (prior_end == block_end).astype(f32)

    def across(cols):
        return jnp.concatenate([jnp.broadcast_to(v, (2, BLOCK)) for v in cols], axis=1)

    end_row, prior_row = across(ends), across(begins)
    flags = [(seg_ext[:, HALO - k : HALO - k + T] == seg) for k in range(1, taps)]
    flags += [seg == end_row, seg == prior_row, end_row == prior_row, seg, jnp.zeros_like(seg)]
    flags = jnp.stack([v.astype(f32) for v in flags], axis=1)

    def own_channels(a):
        x_part = lax.dynamic_slice_in_dim(a, HW * j, HW, a.ndim - 1)
        return jnp.concatenate([x_part, a[..., inner:]], axis=-1)

    def own_heads(a):
        return lax.dynamic_slice_in_dim(a, HL * j, HL, a.ndim - 1)

    kernel_own = own_channels(conv_kernel)
    bias_own = own_channels(conv_bias)[None, :]
    rate = jnp.exp(own_heads(decay_log))
    hp = jnp.stack([own_heads(step_bias), rate, own_heads(skip_gain)]).reshape(3, G, GH)
    hp = jnp.pad(hp.transpose(1, 0, 2), ((0, 0), (0, 5), (0, 0)))
    ids = HL * j + GH * lax.broadcasted_iota(jnp.int32, (G, 128, 128), 0)
    lane = lax.broadcasted_iota(jnp.int32, (G, 128, 128), 2)
    sel = (lax.broadcasted_iota(jnp.int32, (G, 128, 128), 1) == ids + lane) & (lane < GH)
    sel = sel.astype(bf16)
    gain_own = lax.dynamic_slice_in_dim(gate_gain, HW * j, HW, 0)[None, :]
    (marks,) = call(
        turn_body,
        (2,),
        [(flags, (1, 8, T), lambda s: (s, 0, 0))],
        [((2, T, 8), f32, (1, T, 8), lambda s: (s, 0, 0))],
        name="turn",
    )
    held = [half_gate, half_out, cot_own, marks, flags, kernel_own, bias_own, hp, sel, gain_own]
    held = stages.settle(held)
    half_gate, half_out, cot_own, marks, flags, kernel_own, bias_own, hp, sel, gain_own = held
    at_gate = stages.add(g.direct_task, half_gate, [1], 1)
    at_cot = stages.add(g.gather_task, cot_own, None)
    stages.launch([])
    stages.settle([], leave=[at_gate, at_cot])
    n_ext = at_n["all"].reshape(2 * TE, width)
    w_packed = at_packed["w"]
    packed = low_dot(n_ext, w_packed, NT).astype(bf16)
    (packed,) = stages.settle([packed], leave=[at_gate])
    (packed,) = stages.launch([packed])
    packed = packed.reshape(2, TE, KW)
    marks_b = marks.reshape(NB, BLOCK, 8)

    def seq_block(b):
        return lax.div(b, nb), lax.rem(b, nb)

    def late(c):
        return jnp.maximum(c - 1, 0)

    def shared_first(c):
        return jnp.where(c == 0, G, c - 1)

    dt_block = CW // 128
    x, bc, s_block, step, cum, row = call(
        partial(conv_kernel_body, nb),
        (2, G + 1),
        [
            (packed, (1, TE, LANES), lambda s, c: (s, 0, shared_first(c))),
            (packed, (1, TE, 128), lambda s, c: (s, 0, dt_block)),
            (sel, (1, 128, 128), lambda s, c: (late(c), 0, 0)),
            (hp, (1, 8, GH), lambda s, c: (late(c), 0, 0)),
            (marks, (1, T, 8), lambda s, c: (s, 0, 0)),
            (kernel_own, (taps, LANES), lambda s, c: (0, shared_first(c))),
            (bias_own, (1, LANES), lambda s, c: (0, shared_first(c))),
        ],
        [
            ((2 * T, HW), bf16, (T, LANES), lambda s, c: (s, late(c))),
            ((2 * T, shared), bf16, (T, shared), lambda s, c: (s, 0)),
            ((2, nb, state, HW), f32, (1, nb, state, LANES), lambda s, c: (s, 0, 0, late(c))),
            ((2, G, T, GH), f32, (1, 1, T, GH), lambda s, c: (s, late(c), 0, 0)),
            ((2, G, T, GH), f32, (1, 1, T, GH), lambda s, c: (s, late(c), 0, 0)),
            ((2, G, nb, GH, BLOCK), f32, (1, 1, nb, GH, BLOCK), lambda s, c: (s, late(c), 0, 0, 0)),
        ],
        [pltpu.VMEM((TE, LANES), f32), pltpu.VMEM((T, state), bf16)],
        flops=2 * T * HW * state * 20,
        name="convolve",
    )

    end = jnp.exp(row[..., BLOCK - 1]).transpose(0, 2, 1, 3).reshape(2, nb, HL)
    carry_b = end * carry_flag[:, :, None]

    def spread(a):
        return jnp.repeat(a, hd, axis=-1)

    carry_wide = spread(carry_b)[:, :, None, :]
    carry_range = jnp.prod(carry_b, axis=1)
    s_range = s_block[:, 0]
    for b in range(1, nb):
        s_range = s_block[:, b] + carry_wide[:, b] * s_range
    s_range, x, bc, cum, row, step = stages.settle(
        [s_range, x, bc, cum, row, step], leave=[at_cot]
    )
    at_out = stages.add(g.direct_task, half_out, [1], 0)
    at_enter = stages.add(g.state_task, s_range, carry_range, spread, 1)
    x, bc, cum, row, step = stages.launch([x, bc, cum, row, step])

    def tile(a):
        return (a, (BLOCK, LANES), lambda b, k: (b, k))

    def whole(a):
        return (a, (BLOCK, a.shape[1]), lambda b, k: (b, 0))

    def small_tile(a):
        def at(b, k):
            s, m = seq_block(b)
            return s, k, m, 0

        return (a, (1, 1, BLOCK, GH), at)

    def row_tile(b, k):
        s, m = seq_block(b)
        return s, k, m, 0, 0

    def flag_tile(b, k):
        s, m = seq_block(b)
        return s, 0, m

    pair_flops = 2 * 2 * T * BLOCK * HW
    (y_local,) = call(
        intra_forward_body,
        (NB, G),
        [
            tile(x),
            whole(bc),
            small_tile(cum),
            (row, (1, 1, 1, GH, BLOCK), row_tile),
            small_tile(step),
            (marks_b, (1, BLOCK, 8), lambda b, k: (b, 0, 0)),
            (flags, (1, 8, BLOCK), flag_tile),
            (hp, (1, 8, GH), lambda b, k: (k, 0, 0)),
        ],
        [((2 * T, HW), bf16, (BLOCK, LANES), lambda b, k: (b, k))],
        [pltpu.VMEM((BLOCK, BLOCK), f32)] * 2,
        flops=pair_flops * 8,
        name="intra_forward",
    )
    w_gate = at_gate["w"]
    gate = low_dot(n_ext, w_gate, NT).astype(bf16)
    y_local, gate = stages.settle([y_local, gate])
    while "state" not in at_enter or "w" not in at_out or "all" not in at_cot:
        stages.launch([])
        stages.settle([])
    enter = [at_enter["state"]]
    for b in range(nb - 1):
        enter.append(s_block[:, b] + carry_wide[:, b] * enter[b])
    enter = jnp.stack(enter, axis=1).astype(bf16)
    w_out = at_out["w"]
    cot_all = at_cot["all"].reshape(2 * T, width)
    out_grad = low_dot(cot_all, w_out, NN).astype(bf16)
    gate = gate.reshape(2, TE, HW)

    def seq_tile(a):
        return (a, (T, LANES), lambda s, k: (s, k))

    def seq_small(a):
        return (a, (1, 1, T, GH), lambda s, k: (s, k, 0, 0))

    def seq_state(a):
        return (a, (1, nb, state, LANES), lambda s, k: (s, 0, 0, k))

    def seq_whole(a):
        return (a, (1,) + a.shape[1:], lambda s, k: (s, 0, 0))

    def lane_tile(a):
        return (a, (a.shape[0], LANES), lambda s, k: (0, k))

    bc_seq = (bc, (T, shared), lambda s, k: (s, 0))
    main_tile = (gate, (1, T, LANES), lambda s, k: (s, 0, k))
    mixed, sums = call(
        partial(join_body, nb),
        (2, G),
        [
            seq_tile(y_local),
            bc_seq,
            seq_state(enter),
            seq_small(cum),
            seq_whole(marks),
            main_tile,
            seq_tile(out_grad),
            lane_tile(gain_own),
        ],
        [
            ((2 * T, HW), bf16, (T, LANES), lambda s, k: (s, k)),
            ((2, 8, T), f32, (1, 8, T), lambda s, k: (s, 0, 0)),
        ],
        flops=pair_flops,
        name="join",
    )
    at_sums = stages.add(g.sum_tp_task, sums)
    while "sum" not in at_sums:
        stages.launch([])
        stages.settle([])

    def turn(spec):
        a, block, at = spec
        return (a, block, lambda k, s: at(s, k))

    normed_out, gate_grad, d_out, gain_grad, de_block = call(
        partial(gates_body, nb, inner),
        (G, 2),
        [
            turn(v)
            for v in [
                seq_tile(mixed),
                main_tile,
                seq_tile(out_grad),
                seq_whole(at_sums["sum"]),
                lane_tile(gain_own),
                bc_seq,
                seq_small(cum),
                seq_whole(marks),
            ]
        ],
        [
            ((2 * T, HW), bf16, (T, LANES), lambda k, s: (s, k)),
            ((2, TE, HW), bf16, (1, TE, LANES), lambda k, s: (s, 0, k)),
            ((2 * T, HW), bf16, (T, LANES), lambda k, s: (s, k)),
            ((1, HW), f32, (1, LANES), lambda k, s: (0, k)),
            ((2, nb, state, HW), f32, (1, nb, state, LANES), lambda k, s: (s, 0, 0, k)),
        ],
        flops=pair_flops,
        name="gates",
    )
    gate_grad = gate_grad.reshape(2 * TE, HW)

    def far_rows(f, n):
        return [f(i).astype(bf16) for i in range(1, n)]

    def out_part(i):
        return low_dot(g.cut(cot_all, 1, i, g.Y), normed_out, TN)

    def in_part(a, i):
        return low_dot(a, g.cut(n_ext, 1, i, g.Y), TN)

    d_range = de_block[:, nb - 1]
    for b in range(nb - 2, -1, -1):
        d_range = de_block[:, b] + carry_wide[:, b] * d_range
    at_leave = stages.add(g.state_task, d_range, carry_range, spread, -1)
    at_outs = stages.add(
        g.gradient_task, far_rows(out_part, g.Y), lambda: out_part(0), 0, (2, 1)
    )
    x, d_out, normed_out, gate_grad = stages.launch([x, d_out, normed_out, gate_grad])
    branch = low_dot(normed_out, w_out, NT).astype(bf16)
    at_branch = stages.add(g.scatter_task, branch.reshape(2, g.W, own_len, width), (1, 2))
    x, d_out = stages.launch([x, d_out])
    dxs, dec, dbc = call(
        intra_backward_body,
        (NB, G),
        [
            tile(x),
            whole(bc),
            tile(d_out),
            small_tile(cum),
            (row, (1, 1, 1, GH, BLOCK), row_tile),
            small_tile(step),
            (
                enter.reshape(NB, state, HW),
                (1, state, LANES),
                lambda b, k: (b, 0, k),
            ),
            (marks_b, (1, BLOCK, 8), lambda b, k: (b, 0, 0)),
            (flags, (1, 8, BLOCK), flag_tile),
        ],
        [
            ((2 * T, HW), bf16, (BLOCK, LANES), lambda b, k: (b, k)),
            ((2, G, T, GH), f32) + small_tile(cum)[1:],
            ((2 * T, shared), f32, (BLOCK, shared), lambda b, k: (b, 0)),
        ],
        [pltpu.VMEM((BLOCK, BLOCK), f32)] * 3 + [pltpu.VMEM((BLOCK, state), f32)],
        flops=pair_flops * 16,
        name="intra_backward",
    )
    gate_far = far_rows(lambda i: in_part(gate_grad, i), g.Y)
    dxs, gate_far = stages.settle([dxs, gate_far])
    kept = {}

    def gate_first():
        kept["gate"] = in_part(gate_grad, 0)
        return kept["gate"]

    at_gates = stages.add(g.gradient_task, gate_far, gate_first, 1, (2, 1))

    while "state" not in at_leave:
        stages.launch([])
        stages.settle([])
    leave = [at_leave["state"]]
    for b in range(nb - 1, 0, -1):
        leave.insert(0, de_block[:, b] + carry_wide[:, b] * leave[0])
    leave = jnp.stack(leave, axis=1).astype(bf16)
    leave, dxs = stages.launch([leave, dxs])

    def held(s, k):
        return s, jnp.minimum(k, G - 1)

    def late_tile(a):
        return (a, (T, LANES), lambda s, k: held(s, k))

    def late_small(a):
        return (a, (1, 1, T, GH), lambda s, k: (*held(s, k), 0, 0))

    def late_state(a):
        return (a, (1, nb, state, LANES), lambda s, k: (s, 0, 0, jnp.minimum(k, G - 1)))

    x_back, dt_back, kg, sm = call(
        partial(finish_body, nb),
        (2, G + 1),
        [
            (packed, (1, TE, LANES), lambda s, k: (s, 0, k)),
            late_tile(x),
            late_tile(d_out),
            late_tile(dxs),
            bc_seq,
            (dbc, (T, shared), lambda s, k: (s, 0)),
            late_state(leave),
            late_state(enter),
            late_small(cum),
            late_small(step),
            late_small(dec),
            (packed, (1, TE, 128), lambda s, k: (s, 0, dt_block)),
            (sel, (1, 128, 128), lambda s, k: (jnp.minimum(k, G - 1), 0, 0)),
            (hp, (1, 8, GH), lambda s, k: (jnp.minimum(k, G - 1), 0, 0)),
            seq_whole(marks),
            lane_tile(kernel_own),
            lane_tile(bias_own),
        ],
        [
            ((2, TE, CW), bf16, (1, TE, LANES), lambda s, k: (s, 0, k)),
            ((2, TE, 128), bf16, (1, TE, 128), lambda s, k: (s, 0, 0)),
            ((2, 8, CW), f32, (1, 8, LANES), lambda s, k: (s, 0, k)),
            ((2, G, 8, GH), f32, (1, 1, 8, GH), lambda s, k: (*held(s, k), 0, 0)),
        ],
        [
            pltpu.VMEM((TE, LANES), f32),
            pltpu.VMEM((HALO + TE, LANES), f32),
            pltpu.VMEM((T, LANES), f32),
            pltpu.VMEM((T, state), f32),
        ],
        flops=pair_flops * 16,
        name="finish",
    )
    edge = jnp.concatenate([x_back[:, T:], dt_back[:, T:]], axis=-1).reshape(2 * HALO, KW)
    spill = low_dot(edge, w_packed, NN).astype(bf16).reshape(2, HALO, width)
    x_flat = x_back.reshape(2 * TE, CW)
    dt_flat = dt_back.reshape(2 * TE, 128)

    def x_part(i):
        return in_part(x_flat[:, :HW], i)

    x_far = far_rows(x_part, g.Y)
    x_far, spill, x_flat, dt_flat, kg, sm = stages.settle([x_far, spill, x_flat, dt_flat, kg, sm])
    at_x = stages.add(g.gradient_task, x_far, lambda: x_own, 1, (2, 1))
    at_spill = stages.add(g.one_task, [spill], lambda a: g.shift_z(a, -1))
    x_flat, dt_flat, kg, sm = stages.launch([x_flat, dt_flat, kg, sm])
    x_own = x_part(0)
    rest_back = jnp.concatenate([x_flat[:, HW:], dt_flat[:, :heads]], axis=1)
    rest = [in_part(rest_back, i) for i in range(g.Y)]
    gate_own = kept["gate"]

    n_rest = shared + heads
    lines = inner // own_d
    pre_lines = width // own_d
    lanes = width // g.Y
    n_small = 6 * lines + 6 + pre_lines
    n_small += -(n_rest + n_small) % 128
    ins = [(jnp.stack([j, g.y]).astype(jnp.int32), None, None)]
    for i in range(g.Y):
        for a, rows, col in (
            (w_gate, HW, i),
            (([gate_own] + gate_far)[i], HW, 0),
            (w_packed, KW, i),
            (([x_own] + x_far)[i], HW, 0),
            (rest[i], n_rest, 0),
        ):
            ins.append((a, (rows, lanes), lambda n, col=col: (0, col)))
    for a in (gain_grad, kg, sm, pre_gain.reshape(pre_lines, own_d)):
        ins.append((a, a.shape, lambda n, d=a.ndim: (0,) * d))
    (small,) = call(
        partial(small_body, g.Y, HW, HL, heads),
        (1,),
        ins,
        [((n_small, own_d), f32, (n_small, own_d), lambda n: (0, 0))],
        name="small",
    )
    copies = jnp.concatenate([small] * 2, axis=1)
    rest = [jnp.concatenate([p, copies], axis=0) for p in rest]
    rest_far = [p.astype(bf16) for p in rest[1:]]
    held = stages.settle([x_own, x_flat, dt_flat, rest_far, rest[0]], leave=[at_gates])
    x_own, x_flat, dt_flat, rest_far, rest_own = held
    at_rest = stages.add(g.gradient_task, rest_far, lambda: rest_own, 1, None)
    spill = at_spill["got"][0]
    spill, gate_grad, x_flat, dt_flat = stages.launch([spill, gate_grad, x_flat, dt_flat])

    NW = 512
    (n_grad,) = call(
        input_grad_body,
        (2, width // NW),
        [
            (gate_grad, (TE, HW), lambda s, n: (s, 0)),
            (x_flat, (TE, CW), lambda s, n: (s, 0)),
            (dt_flat, (TE, 128), lambda s, n: (s, 0)),
            (w_gate, (HW, NW), lambda s, n: (0, n)),
            (w_packed, (CW, NW), lambda s, n: (0, n)),
            (w_packed, (128, NW), lambda s, n: (CW // 128, n)),
            (spill, (1, HALO, NW), lambda s, n: (s, 0, n)),
        ],
        [
            ((2, T, width), bf16, (1, T, NW), lambda s, n: (s, 0, n)),
        ],
        flops=2 * 2 * TE * width * (2 * HW + 128),
        name="input_grad",
    )

    in_shape = (2 * inner + shared + heads, own_d)

    def moves_of(a, first, axis):
        n = a["done"][0].shape[axis] // 4
        moves = []
        for i, (d, e) in enumerate(a["from"]):
            source, target, sizes = [0, 0], [0, 0], [own_d, own_d]
            source[axis], sizes[axis] = i % 4 * n, n
            target[axis] = first + HW * ((g.w ^ d) * 2 + (g.c ^ e))
            moves.append((i // 4, tuple(source), tuple(sizes), tuple(target)))
        return moves

    (n_grad,) = stages.settle([n_grad], leave=[at_x])
    at_ngrad = stages.add(g.scatter_task, n_grad.reshape(2, g.W, own_len, width), (2, 1))
    if g.Z == 2:
        stages.launch([])
        stages.settle([], leave=[at_x, at_outs])
        stages.launch([], hold=[at_gates, at_ngrad])
        stages.settle([], leave=[at_x, at_outs])
        stages.launch([], hold=[at_ngrad])
    else:
        stages.launch([])
    stages.settle([])
    while "done" not in at_outs:
        stages.launch([])
        stages.settle([])
    stages.launch([])
    out_weight_gradient = place(at_outs["done"], moves_of(at_outs, 0, 1), (own_d, inner), None)
    block_output = (series + g.own_first_back(at_branch["sum"])).astype(bf16)[None]
    out_weight_gradient, block_output = stages.settle([out_weight_gradient, block_output])
    while "done" not in at_gates:
        stages.launch([])
        stages.settle([])
    stages.launch([])
    in_buf = place(at_gates["done"], moves_of(at_gates, 0, 0), in_shape, None)
    (in_buf,) = stages.settle([in_buf])
    while "sum" not in at_ngrad:
        stages.launch([])
        stages.settle([])
    stages.launch([])
    n_own = g.own_first_back(at_ngrad["sum"])
    lifted_n = n_own * pre_gain[None, :]
    token_gradient = (
        cotangent[0].astype(f32)
        + scale * lifted_n
        - series * scale**3 * jnp.mean(series * lifted_n, axis=-1, keepdims=True)
    )[None]
    token_gradient, in_buf = stages.settle([token_gradient, in_buf])
    while "done" not in at_x:
        stages.launch([])
        (in_buf,) = stages.settle([in_buf])
    if stages.tasks:
        stages.launch([])
    in_buf = place(at_x["done"], moves_of(at_x, inner, 0), in_shape, in_buf)
    while stages.tasks:
        (in_buf,) = stages.settle([in_buf])
        if stages.tasks:
            stages.launch([])
    rest_done = at_rest["done"]
    in_buf = place(
        [rest_done], [(0, (0, 0), (shared + heads, own_d), (2 * inner, 0))], in_shape, in_buf
    )
    in_weight_gradient = in_buf.T

    small = rest_done[n_rest:].astype(f32)
    gain_total = small[:lines].reshape(-1)
    kb = small[lines : 6 * lines].reshape(5, inner)
    at = 6 * lines
    kb = jnp.concatenate([kb, small[at : at + 5, :shared]], axis=1)
    kernel_total, bias_total = kb[:taps], kb[taps]
    step_total, decay_total, skip_total = small[at + 5, : 3 * heads].reshape(3, heads)
    pre_total = small[at + 6 : at + 6 + pre_lines].reshape(-1)
    return (
        block_output,
        token_gradient,
        in_weight_gradient,
        out_weight_gradient,
        pre_total,
        kernel_total,
        bias_total,
        step_total,
        decay_total,
        skip_total,
        gain_total,
    )


def solution(mesh):
    placed = (
        P("shard", "seq", None),
        P("shard", None),
        P("shard", None),
        P(),
        P(),
        P(),
        P(),
        P(),
        P(),
        P(),
        P("shard", None),
        P("shard", "seq", None),
    )
    results = (P("shard", "seq", None),) * 2 + (P("shard", None),) * 2 + (P(),) * 7
    return jax.shard_map(
        partial(body, Slice(mesh)),
        mesh=mesh,
        in_specs=placed,
        out_specs=results,
        check_vma=False,
    )
```
